128 devices in a mesh: elem: 32 (over z, y, core), grp: 4 (over x).
Axes of the slice: x: 4, y: 4, z: 4, core: 2. Of those that a mesh axis runs over, the one named last changes fastest.
Arguments:
- state: float32 [4, 72, 65536], P(None, None, ('elem', 'grp')), may hold values from -6 to 6
- surface: float32 [3, 32, 65536], P(None, None, ('elem', 'grp')), may hold values from -6 to 6
- mass: float32 [65536], P(('elem', 'grp')), may hold values from 1 to 10
- plan: int32 [2, 65536], P(None, ('elem', 'grp')), may hold values from 0 to 159, as said below
- active: int32 [65536], P(('elem', 'grp')), may hold values from 0 to 1, as said below
Outputs:
- new_state: float32 [4, 72, 65536], P(None, None, ('elem', 'grp'))
- crm_diag: float32 [3, 32, 65536], P(None, None, ('elem', 'grp'))
The draws below stay inside these ranges and needn't reach their ends.
Inputs may be any that keep to these rules, and one draw needn't show every extreme that they name: `plan`: row 0 holds owners from 0 to 127, row 1 slots from 0 to 159. An inactive column names its own device and slot 0. Each device with active columns sends every owner the same number of them, at most 2, and one device sends exactly 2 to every owner; the active columns of all devices fill each owner's 160 slots exactly, with no slot named twice. One device has 512 // 2 active columns; every count of active columns on a device is 128 times a whole number.
All inputs are finite; a program needn't handle non-finite values.
Results may differ from the reference program's by a relative error of at most 0.0001.
Values sent between devices are 32-bit elements; how exact they have to be, the bound alone decides.
A program may use at most 128 MiB of HBM per device.

```python
import math
import jax
import jax.numpy as jnp
from jax import lax

LEV = 72
CZ = 58
CX = 32
EDGE = 64
COL_DEV = 512
SPAN = 160
PACKED = 384
COLUMNS = 65536
N_ELEM = 32
N_GRP = 4


def span_plan(key):
    devices = N_ELEM * N_GRP
    pair_cap = COL_DEV // (2 * devices)
    splits = jax.random.split(key, 4)
    pattern = jax.random.permutation(splits[0], jnp.arange(devices, dtype=jnp.int32) % 4)
    shares = jnp.maximum(1, jnp.right_shift(jnp.int32(pair_cap), pattern)).astype(jnp.int32)
    live_count = devices * shares
    ranks = jax.vmap(lambda sub_key: jax.random.permutation(sub_key, COL_DEV))(jax.random.split(splits[1], devices)).astype(jnp.int32)
    is_live = ranks < live_count[:, None]
    relabel = jax.random.permutation(splits[2], devices).astype(jnp.int32)
    source = jnp.arange(devices, dtype=jnp.int32)[:, None]
    owners = relabel[(source + ranks) % devices]
    offsets = jnp.cumsum(shares) - shares
    within = ranks // devices
    orders = jax.vmap(lambda sub_key: jax.random.permutation(sub_key, SPAN))(jax.random.split(splits[3], devices)).astype(jnp.int32)
    spots = jnp.minimum(offsets[:, None] + within, SPAN - 1)
    slot_ids = orders[owners, spots]
    owners = jnp.where(is_live, owners, source)
    slot_ids = jnp.where(is_live, slot_ids, 0)
    return (is_live.astype(jnp.int32).reshape(-1), jnp.stack([owners, slot_ids]).reshape(2, -1).astype(jnp.int32))


def draw_plan(key, part):
    return span_plan(key)[1]


def draw_active(key, part):
    return span_plan(key)[0]


def block_scale(stream_key, extent, cuts, least, top_value):
    def one(dim, parts):
        steps = jax.random.uniform(jax.random.fold_in(jax.random.fold_in(stream_key, 6), dim), (parts,), jnp.float32, least / len(cuts), top_value / len(cuts))
        return jnp.repeat(jnp.exp(steps), extent[dim] // parts).reshape((-1,) + (1,) * (len(extent) - dim - 1))

    gain = one(*cuts[0])
    for cut in cuts[1:]:
        gain = gain * one(*cut)
    return gain


def bell_draw(rng, dims, spread, bound, cuts=(), kind=jnp.bfloat16):
    result = spread * jax.random.normal(rng, dims, jnp.float32)
    if cuts:
        result = result * block_scale(rng, dims, cuts, -0.22, 0.18)
    return jnp.clip(result, -bound, bound).astype(kind)


def setup_inputs(seed: int = 0) -> dict:
    keys = jax.random.split(jax.random.key(seed), 6)
    state = bell_draw(keys[0], (4, LEV, COLUMNS), 1.0, 6.0, ((2, 128),), jnp.float32)
    surface = bell_draw(keys[1], (3, CX, COLUMNS), 1.0, 6.0, ((2, 128),), jnp.float32)
    mass = jnp.clip(jnp.exp(math.log(10.0) - 2.3025851 * jax.random.uniform(keys[2], (COLUMNS,), jnp.float32) ** block_scale(keys[2], (COLUMNS,), ((0, 128),), -0.2, 0.2)), 1.0, 10.0)
    plan = draw_plan(jax.random.fold_in(keys[5], 71), 0)
    active = draw_active(jax.random.fold_in(keys[5], 71), 0)
    return dict(state=state, surface=surface, mass=mass, plan=plan, active=active)


def interp_tables():
    crm_level = jnp.arange(CZ, dtype=jnp.float32)
    gcm_level = jnp.arange(LEV, dtype=jnp.float32)
    upward = jnp.maximum(0.0, 1.0 - jnp.abs(crm_level[:, None] * ((LEV - 1) / (CZ - 1)) - gcm_level[None, :]))
    downward = jnp.maximum(0.0, 1.0 - jnp.abs(gcm_level[:, None] * ((CZ - 1) / (LEV - 1)) - crm_level[None, :]))
    return upward, downward


def cloud_model(forcing):
    upward, downward = interp_tables()
    columns = forcing.shape[1]
    profiles = forcing[:4 * LEV].reshape(4, LEV, columns)
    surface_rows = forcing[4 * LEV:].reshape(3, CX, columns)
    baseline = jnp.einsum("zl,jls->jzs", upward, profiles, precision=lax.Precision.HIGHEST)
    surface_all = jnp.concatenate([surface_rows, jnp.zeros((1, CX, columns), jnp.float32)], 0)
    height = jnp.arange(CZ, dtype=jnp.float32)
    falloff = (1.0 - 0.5 * height / (CZ - 1))[None, :, None, None]
    fields = baseline[:, :, None, :] + falloff * surface_all[:, None, :, :]
    mixing = (0.1 + 0.2 * height / (CZ - 1))[None, :, None, None]
    rainfall = jnp.zeros((CX, columns), jnp.float32)
    for substep in range(2):
        eastward = jnp.roll(fields, -1, axis=2)
        westward = jnp.roll(fields, 1, axis=2)
        fields = fields + 0.2 * (eastward + westward - 2.0 * fields) - 0.1 * fields[2][None] * (eastward - westward)
        above = jnp.concatenate([fields[:, 1:], fields[:, CZ - 1:]], 1)
        beneath = jnp.concatenate([fields[:, :1], fields[:, :CZ - 1]], 1)
        fields = fields + mixing * (above + beneath - 2.0 * fields)
        excess = 0.5 * jax.nn.softplus(fields[1] - 0.3 * fields[0])
        fields = jnp.stack([fields[0] + 0.8 * excess, fields[1] - excess, fields[2], fields[3]])
        rainfall = rainfall + jnp.sum(excess, axis=0)
    change = jnp.mean(fields, axis=2) - baseline
    tendency = jnp.einsum("lz,jzs->jls", downward, change, precision=lax.Precision.HIGHEST).reshape(4 * LEV, columns)
    moisture = jnp.mean(fields[1], axis=0)
    heating = jnp.mean(fields[0], axis=0) - jnp.mean(baseline[0], axis=0)[None, :]
    return jnp.concatenate([tendency, rainfall, moisture, heating], 0)


def edge_sum(state, mass):
    levels = 4 * LEV
    blocks = state.reshape(levels, N_ELEM, N_GRP, COL_DEV)
    weights = mass.reshape(N_ELEM, N_GRP, COL_DEV)
    weighted = blocks * weights[None]
    own_first = weighted[..., :EDGE]
    own_last = weighted[..., COL_DEV - EDGE:]
    mass_first = weights[..., :EDGE]
    mass_last = weights[..., COL_DEV - EDGE:]
    new_first = (own_first + jnp.roll(own_last, 1, axis=1)) / (mass_first + jnp.roll(mass_last, 1, axis=0))
    new_last = (own_last + jnp.roll(own_first, -1, axis=1)) / (mass_last + jnp.roll(mass_first, -1, axis=0))
    middle = blocks[..., EDGE:COL_DEV - EDGE]
    return jnp.concatenate([new_first, middle, new_last], 3).reshape(levels, N_ELEM * N_GRP * COL_DEV)


def reference(state, surface, mass, plan, active):
    all_columns = state.shape[2]
    devices = N_ELEM * N_GRP
    levels = 4 * LEV
    shared = edge_sum(state, mass)
    forcing = jnp.concatenate([shared, surface.reshape(3 * CX, all_columns)], 0)
    is_live = active == 1
    target = jnp.where(is_live, plan[0] * SPAN + plan[1], devices * SPAN).astype(jnp.int32)
    gathered = jnp.zeros((devices * SPAN, PACKED), jnp.float32).at[target].set(forcing.T, mode="drop")
    computed = lax.map(lambda owner_rows: cloud_model(owner_rows.T).T, gathered.reshape(devices, SPAN, PACKED))
    picked = computed.reshape(devices * SPAN, PACKED)[jnp.clip(target, 0, devices * SPAN - 1)].T
    new_state = shared + jnp.where(is_live[None, :], picked[:levels], 0.0)
    crm_diag = jnp.where(is_live[None, :], picked[levels:], 0.0)
    return new_state.reshape(4, LEV, all_columns), crm_diag.reshape(3, CX, all_columns)
```

```python
import functools
import math

import jax
import jax.numpy as jnp
import ml_dtypes
import numpy as np
from jax import lax
from jax.experimental import pallas as pl
from jax.experimental.pallas import tpu as pltpu
from jax.sharding import PartitionSpec as P

LEV = 72
CZ = 58
CX = 32
EDGE = 64
LANES = 128
BLOCK = 128
ZP = 64
HALF = 2 * LEV
STATE_ROWS = 224
F32 = jnp.float32
BF16 = jnp.bfloat16
MESH = pl.DeviceIdType.MESH
UNROLL = 3


def split_np(matrix):
    high = matrix.astype(np.float32).astype(ml_dtypes.bfloat16)
    low = (matrix - high.astype(np.float64)).astype(np.float32).astype(ml_dtypes.bfloat16)
    return high, low


def tables():
    z = np.arange(CZ, dtype=np.float64)
    lev = np.arange(LEV, dtype=np.float64)
    up = np.maximum(0.0, 1.0 - np.abs(z[:, None] * ((LEV - 1) / (CZ - 1)) - lev[None, :]))
    down = np.maximum(0.0, 1.0 - np.abs(lev[:, None] * ((CZ - 1) / (LEV - 1)) - z[None, :]))
    fall = 1.0 - 0.5 * z / (CZ - 1)
    k = 0.1 + 0.2 * z / (CZ - 1)
    mix = np.zeros((CZ, CZ))
    for i in range(CZ):
        mix[i, i] += 1.0 - 2.0 * k[i]
        mix[i, min(i + 1, CZ - 1)] += k[i]
        mix[i, max(i - 1, 0)] += k[i]
    kap = mix.sum(0)
    c1 = mix @ fall
    c2 = -0.1 * (mix @ (fall * fall))
    kb = mix @ up
    qb = -0.1 * (mix @ (fall[:, None] * up))

    m = np.zeros((344, STATE_ROWS))
    p0, p1, p2 = slice(0, 72), slice(72, 144), slice(144, 216)
    m[0:CZ, p1] = kb / 0.62
    m[0:CZ, p0] = -0.3 * kb / 0.62
    m[64:64 + CZ, p2] = 0.5 * kb
    m[128:128 + CZ, p2] = qb
    dkk = down @ mix @ kb
    m[192:264, p0] = dkk / 1.24 - down @ up
    m[192:264, p1] = 0.8 * dkk / 1.24
    m[264:336, p0] = 0.3 * dkk / 1.24
    m[264:336, p1] = 0.3 * 0.8 * dkk / 1.24 - down @ up
    m[336, p2] = (kap * c1) @ (0.5 * kb)
    m[337, p2] = (kap * c2) @ (0.5 * kb)
    m[338, p2] = (kap * c1) @ qb
    m[339, p2] = (kap * c2) @ qb
    m[340, p2] = kap @ qb
    m[341, p0] = kap @ kb
    m[341, p1] = 0.8 * (kap @ kb)
    m[342, p0] = up.sum(0)
    hi, lo = split_np(m)
    maps = np.concatenate([hi, lo, hi], 1)
    maps = np.concatenate([maps, np.zeros((8, maps.shape[1]), maps.dtype)], 0)

    t = np.zeros((HALF, 2 * ZP))
    t[0:72, 0:CZ] = down @ mix / 1.24
    t[72:144, 0:CZ] = 0.3 * (down @ mix) / 1.24
    t[0:72, ZP:ZP + CZ] = -0.8 * down / 1.24
    t[72:144, ZP:ZP + CZ] = down / 1.24
    hi, lo = split_np(t)
    tail = np.concatenate([hi, lo, hi], 1)

    e = np.zeros((HALF, HALF))
    e[0:72, 0:72] = down @ (mix @ kb - up)
    e[72:144, 72:144] = e[0:72, 0:72]
    hi, lo = split_np(e)
    passive = np.concatenate([hi, lo, hi], 1)
    drift = np.repeat(((down @ (mix @ (mix @ fall))) / CX)[:, None], LANES, 1).astype(np.float32)

    levels = np.zeros((5, ZP))
    levels[0, :CZ] = c1
    levels[1, :CZ] = c2
    levels[2, :CZ] = 0.124 * (1.0 - 2.0 * k)
    levels[3, :CZ] = 0.124 * k
    levels[4, :CZ] = kap
    levels = np.repeat(levels.reshape(-1)[:, None], LANES, 1).astype(np.float32)
    sums = (float((kap * c1 * c1).sum()), float((kap * c1 * c2).sum()), float((kap * c2 * c2).sum()),
            float((kap * c1).sum()), float((kap * c2).sum()))
    return maps, tail, passive, drift, levels, sums


def halves(x):
    high = x.astype(BF16)
    return high, (x - high.astype(F32)).astype(BF16)


def dot(a, b):
    return lax.dot_general(a, b, (((1,), (0,)), ((), ())), preferred_element_type=F32)


def dot_t(a, b):
    return lax.dot_general(a, b, (((1,), (1,)), ((), ())), preferred_element_type=F32)


def east(f):
    return jnp.concatenate([f[1:], pltpu.roll(f[0], 7, 0)[None]], 0)


def west(f):
    return jnp.concatenate([pltpu.roll(f[3], 1, 0)[None], f[:3]], 0)


def xsum(f):
    return jnp.sum((f[0] + f[1]) + (f[2] + f[3]), axis=0, keepdims=True)


def cloud(sums, g_hi, g_lo, maps_ref, tail_ref, lev_ref, sur_ref, prof_ref, part_ref, diag_ref):
    s11, s12, s22, sc1, sc2 = sums
    prof_ref[...] = dot(maps_ref[...], jnp.concatenate([g_hi, g_hi, g_lo], 0))

    def rows(j):
        return jnp.stack([sur_ref[pl.ds(CX * j + v, 8, stride=4), :] for v in range(4)], 0)

    r0, r1, s2 = rows(0), rows(1), rows(2)
    sy = (r1 - 0.3 * r0) * (1.0 / 0.62)
    sw = r0 + 0.8 * r1

    def parts(s):
        e, w = east(s), west(s)
        return 0.6 * s + 0.2 * (e + w), e - w

    ay, dy = parts(sy)
    a2, d2 = parts(s2)
    af, df = 0.5 * a2, 0.5 * d2

    def level(ref, base, z):
        return ref[pl.ds(base + z, 1), :][None]

    def horizontal(z):
        c1 = level(lev_ref, 0, z)
        turn = level(prof_ref, 128, z) + level(lev_ref, ZP, z) * s2
        y = (level(prof_ref, 0, z) + c1 * ay) + turn * dy
        f2 = (level(prof_ref, 64, z) + c1 * af) + turn * df
        one = jnp.log(1.0 + jnp.exp2(y * (0.62 * math.log2(math.e))))
        y = y - one
        e, w = east(y), west(y)
        return (3.0 * y + (e + w)) - f2 * (e - w), one

    def vertical(z, h, above, below):
        v = level(lev_ref, 2 * ZP, z) * h + level(lev_ref, 3 * ZP, z) * (above + below)
        two = jnp.maximum(jnp.log(1.0 + jnp.exp(jnp.minimum(v, 80.0))), v)
        vs = (v[0] + v[1]) + (v[2] + v[3])
        ts = (two[0] + two[1]) + (two[2] + two[3])
        part_ref[pl.ds(pl.multiple_of(z * 8, 8), 8), :] = vs - 0.62 * ts
        return v, two

    h0, rain = horizontal(0)

    def step(i, carry):
        h, below, rain, total_v, total_2 = carry
        for u in range(UNROLL):
            z = 1 + i * UNROLL + u
            above, one = horizontal(z)
            v, two = vertical(z - 1, h, above, below)
            rain, total_v, total_2 = rain + one, total_v + v, total_2 + two
            h, below = above, h
        return h, below, rain, total_v, total_2

    zero = jnp.zeros_like(rain)
    carry = lax.fori_loop(0, (CZ - 1) // UNROLL, step, (h0, h0, rain, zero, zero))
    h, below, rain, total_v, total_2 = carry
    v, two = vertical(CZ - 1, h, h, below)
    total_v, total_2 = total_v + v, total_2 + two
    sum_y = total_v - 0.62 * total_2

    aw, dw = parts(sw)
    ew, ef = s2 * dw, s2 * df
    haw, hdw, hew = east(aw) - west(aw), east(dw) - west(dw), east(ew) - west(ew)
    g11 = xsum(af * haw)
    g12 = xsum(af * hdw + df * haw)
    g13 = xsum(af * hew + ef * haw)
    g22 = xsum(df * hdw)
    g23 = xsum(df * hew + ef * hdw)
    g33 = xsum(ef * hew)
    c1 = lev_ref[0:ZP, :]
    c2 = lev_ref[ZP:2 * ZP, :]
    kap = lev_ref[4 * ZP:5 * ZP, :]
    pf = prof_ref[64:128, :]
    q = prof_ref[128:192, :]
    gram = c1 * (c1 * g11 + q * g12 + c2 * g13) + q * (q * g22 + c2 * g23) + (c2 * c2) * g33
    mean_w = c1 * (xsum(sw) * (1.0 / CX)) + c2 * (xsum(ew) * (1.0 / CX)) - (0.2 / CX) * gram
    qk = q * kap
    sqp = jnp.sum(qk * pf, axis=0, keepdims=True)
    sqq = jnp.sum(qk * q, axis=0, keepdims=True)
    s1p, s2p, s1q, sq2, sq, spw, sb = [prof_ref[336 + i:337 + i, :] for i in range(7)]
    w1 = (spw + sc1 * aw) + (sq * dw + sc2 * ew)
    sum_w = (
        (0.6 * w1 + 0.2 * (east(w1) + west(w1)))
        - 0.2 * (
            haw * ((s1p + s11 * af) + (s1q * df + s12 * ef))
            + hdw * ((sqp + s1q * af) + (sqq * df + sq2 * ef))
            + hew * ((s2p + s12 * af) + (sq2 * df + s22 * ef))
        )
    )
    rain = 0.5 * (rain + total_2)
    moist = (sum_y + 0.3 * sum_w) * (1.0 / (1.24 * CZ))
    heat = (sum_w - 0.8 * sum_y) * (1.0 / (1.24 * CZ)) - sb * (1.0 / CZ)
    for i, rows_out in enumerate((rain, moist, heat)):
        for v in range(4):
            diag_ref[pl.ds(CX * i + v, 8, stride=4), :] = rows_out[v]

    mean_y = part_ref[pl.ds(0, ZP, stride=8), :]
    for s in range(1, 8):
        mean_y = mean_y + part_ref[pl.ds(s, ZP, stride=8), :]
    live = lax.broadcasted_iota(jnp.int32, (ZP, BLOCK), 0) < CZ
    mean_y = jnp.where(live, mean_y * (1.0 / CX), 0.0)
    hi, lo = halves(jnp.concatenate([mean_w, mean_y], 0))
    return prof_ref[192:336, :] + dot(tail_ref[...], jnp.concatenate([hi, hi, lo], 0))


def kernel(sums, n_elem, state_ref, surface_ref, mass_ref, active_ref, maps_ref, tail_ref, passive_ref,
           drift_ref, lev_ref, out_ref, diag_out_ref,
           xs, hi_ref, lo_ref, su, ones_ref, send, recv, sur, prof, part, diag, both_hi, both_lo,
           in_sem, send_sem, recv_sem):
    e, g = lax.axis_index("elem"), lax.axis_index("grp")
    after = lax.rem(e + 1, n_elem)
    before = lax.rem(e + n_elem - 1, n_elem)
    barrier = pltpu.get_barrier_semaphore()
    for other in (before, after):
        pl.semaphore_signal(barrier, inc=1, device_id=(other, g), device_id_type=MESH)

    loads = [
        pltpu.make_async_copy(state_ref.at[:, pl.ds(a, n)], xs.at[:, pl.ds(a, n)], in_sem.at[i])
        for i, (a, n) in enumerate(((0, LANES), (3 * LANES, LANES), (LANES, 2 * LANES)))
    ] + [pltpu.make_async_copy(surface_ref, su, in_sem.at[3])]
    for load in loads:
        load.start()

    lane = lax.broadcasted_iota(jnp.int32, (1, LANES), 1)
    low = lane < EDGE

    act = [active_ref[:, pl.ds(LANES * b, LANES)].astype(F32) for b in range(4)]
    nil = jnp.zeros((1, LANES), F32)
    inner = [jnp.where(low, 0.0, act[0]), act[1], act[2], jnp.where(low, act[3], 0.0)]
    outer = [jnp.where(low, act[0], 0.0), nil, nil, jnp.where(low, 0.0, act[3])]
    marks = jnp.concatenate(inner + outer, 0)
    r = lax.broadcasted_iota(jnp.int32, (LANES, LANES), 0)
    c = lax.broadcasted_iota(jnp.int32, (LANES, LANES), 1)
    tri = jnp.where(r <= c, 1.0, 0.0).astype(BF16)
    counts = dot(marks.astype(BF16), jnp.concatenate([tri, jnp.ones((LANES, LANES), BF16)], 1))
    run, tot = counts[:, :LANES], counts[:, LANES:]
    offset = nil
    place = []
    for b in range(4):
        inside = run[b:b + 1] + (offset - 1.0)
        outside = (2.0 * BLOCK) - (run[4 + b:5 + b] + (tot[4:5] if b == 3 else 0.0))
        spot = inside if b in (1, 2) else jnp.where(low if b == 3 else ~low, inside, outside)
        place.append(jnp.where(act[b] > 0.5, spot, -1.0))
        offset = offset + tot[b:b + 1]
    where = lax.broadcasted_iota(jnp.int32, (2 * BLOCK, LANES), 0).astype(F32)
    for b in range(4):
        ones_ref[:, LANES * b:LANES * (b + 1)] = jnp.where(where == place[b], 1.0, 0.0).astype(BF16)

    mass0 = mass_ref[:, 0:LANES]
    mass3 = mass_ref[:, 3 * LANES:4 * LANES]
    loads[0].wait()
    loads[1].wait()
    first, last = xs[:, 0:LANES], xs[:, 3 * LANES:4 * LANES]
    send[0, 0:HALF, :] = jnp.where(low, first[:HALF], pltpu.roll(first[HALF:], EDGE, 1))
    send[1, 0:HALF, :] = jnp.where(low, pltpu.roll(last[:HALF], EDGE, 1), last[HALF:])
    send[0, HALF:, :] = jnp.broadcast_to(pltpu.roll(mass0, EDGE, 1), (8, LANES))
    send[1, HALF:, :] = jnp.broadcast_to(pltpu.roll(mass3, EDGE, 1), (8, LANES))
    pl.semaphore_wait(barrier, 2)
    copies = [
        pltpu.make_async_remote_copy(
            src_ref=send.at[i], dst_ref=recv.at[i], send_sem=send_sem.at[i], recv_sem=recv_sem.at[i],
            device_id=(other, g), device_id_type=MESH)
        for i, other in enumerate((before, after))
    ]
    for copy in copies:
        copy.start()

    loads[2].wait()
    loads[3].wait()

    def split_state(lanes):
        hi, lo = halves(xs[:, lanes])
        hi_ref[0:288, lanes] = hi
        lo_ref[0:288, lanes] = lo

    split_state(slice(0, 4 * LANES))
    hi, lo = halves(su[...])
    hi_ref[288:384, :] = hi
    lo_ref[288:384, :] = lo

    def block(i):
        pick = ones_ref[BLOCK * i:BLOCK * (i + 1), :]
        g_hi = dot_t(hi_ref[0:STATE_ROWS, :], pick).astype(BF16)
        g_lo = dot_t(lo_ref[0:STATE_ROWS, :], pick).astype(BF16)
        sur[...] = dot_t(hi_ref[288:384, :], pick) + dot_t(lo_ref[288:384, :], pick)
        tend = cloud(sums, g_hi, g_lo, maps_ref, tail_ref, lev_ref, sur, prof, part, diag)
        hi, lo = halves(jnp.concatenate([tend, diag[...]], 0))
        both_hi[:, BLOCK * i:BLOCK * (i + 1)] = hi
        both_lo[:, BLOCK * i:BLOCK * (i + 1)] = lo

    block(0)

    for copy in copies:
        copy.wait()
    for lanes, own, own_mass, other, keep in (
        (slice(0, LANES), low, mass0, 1, True), (slice(3 * LANES, 4 * LANES), ~low, mass3, 0, False)):
        other_mass = recv[other, HALF:HALF + 1, :]
        share = jnp.where(own, own_mass / (own_mass + other_mass), 1.0)
        rest = jnp.where(own, other_mass / (own_mass + other_mass), 0.0)
        got = recv[other, 0:HALF, :]
        moved = pltpu.roll(got, EDGE, 1)
        top, bottom = (got, moved) if keep else (moved, got)
        xs[0:HALF, lanes] = xs[0:HALF, lanes] * share + top * rest
        xs[HALF:, lanes] = xs[HALF:, lanes] * share + bottom * rest
        split_state(lanes)

    block(1)

    full_hi, full_lo = hi_ref[HALF:2 * HALF, :], lo_ref[HALF:2 * HALF, :]
    slow = dot(passive_ref[...], jnp.concatenate([full_hi, full_hi, full_lo], 0))
    for b in range(4):
        lanes = slice(LANES * b, LANES * (b + 1))
        mean2 = jnp.sum(su[2 * CX:3 * CX, lanes], axis=0, keepdims=True)
        on = act[b] > 0.5
        out_ref[HALF:HALF + LEV, lanes] = xs[HALF:HALF + LEV, lanes] + jnp.where(
            on, slow[:LEV, lanes] + drift_ref[...] * mean2, 0.0)
        out_ref[HALF + LEV:, lanes] = xs[HALF + LEV:, lanes] + jnp.where(on, slow[LEV:, lanes], 0.0)

    back = dot(both_hi[...], ones_ref[...]) + dot(both_lo[...], ones_ref[...])
    out_ref[0:HALF, :] = xs[0:HALF, :] + back[0:HALF]
    diag_out_ref[...] = back[HALF:]


def body(n_elem, state, surface, mass, plan, active):
    cols = state.shape[2]
    maps, tail, passive, drift, levels, sums = tables()
    any_space = pl.BlockSpec(memory_space=pl.ANY)
    vmem = pl.BlockSpec(memory_space=pltpu.VMEM)
    new_state, diag = pl.pallas_call(
        functools.partial(kernel, sums, n_elem),
        out_shape=(jax.ShapeDtypeStruct((4 * LEV, cols), F32), jax.ShapeDtypeStruct((3 * CX, cols), F32)),
        in_specs=[any_space, any_space] + [vmem] * 7,
        out_specs=(vmem, vmem),
        scratch_shapes=[
            pltpu.VMEM((4 * LEV, cols), F32),
            pltpu.VMEM((384, cols), BF16),
            pltpu.VMEM((384, cols), BF16),
            pltpu.VMEM((3 * CX, cols), F32),
            pltpu.VMEM((2 * BLOCK, cols), BF16),
            pltpu.VMEM((2, HALF + 8, LANES), F32),
            pltpu.VMEM((2, HALF + 8, LANES), F32),
            pltpu.VMEM((3 * CX, BLOCK), F32),
            pltpu.VMEM((352, BLOCK), F32),
            pltpu.VMEM((ZP * 8, BLOCK), F32),
            pltpu.VMEM((3 * CX, BLOCK), F32),
            pltpu.VMEM((HALF + 3 * CX, 2 * BLOCK), BF16),
            pltpu.VMEM((HALF + 3 * CX, 2 * BLOCK), BF16),
            pltpu.SemaphoreType.DMA((4,)),
            pltpu.SemaphoreType.DMA((2,)),
            pltpu.SemaphoreType.DMA((2,)),
        ],
        compiler_params=pltpu.CompilerParams(
            collective_id=0, has_side_effects=True, vmem_limit_bytes=32 * 1024 * 1024),
    )(
        state.reshape(4 * LEV, cols), surface.reshape(3 * CX, cols), mass.reshape(1, cols),
        active.reshape(1, cols), maps, tail, passive, drift, levels,
    )
    return new_state.reshape(state.shape), diag.reshape(surface.shape)


def solution(mesh):
    both = ("elem", "grp")
    return jax.shard_map(
        functools.partial(body, mesh.shape["elem"]),
        mesh=mesh,
        in_specs=(P(None, None, both), P(None, None, both), P(both), P(None, both), P(both)),
        out_specs=(P(None, None, both), P(None, None, both)),
        check_vma=False,
    )
```

```python
import functools
import math

import jax
import jax.numpy as jnp
import ml_dtypes
import numpy as np
from jax import lax
from jax.experimental import pallas as pl
from jax.experimental.pallas import tpu as pltpu
from jax.sharding import PartitionSpec as P

LEV = 72
CZ = 58
CX = 32
EDGE = 64
LANES = 128
BLOCK = 128
ZP = 64
HALF = 2 * LEV
STATE_ROWS = 224
F32 = jnp.float32
BF16 = jnp.bfloat16
MESH = pl.DeviceIdType.MESH
UNROLL = 19


def split_np(matrix):
    high = matrix.astype(np.float32).astype(ml_dtypes.bfloat16)
    low = (matrix - high.astype(np.float64)).astype(np.float32).astype(ml_dtypes.bfloat16)
    return high, low


def tables():
    z = np.arange(CZ, dtype=np.float64)
    lev = np.arange(LEV, dtype=np.float64)
    up = np.maximum(0.0, 1.0 - np.abs(z[:, None] * ((LEV - 1) / (CZ - 1)) - lev[None, :]))
    down = np.maximum(0.0, 1.0 - np.abs(lev[:, None] * ((CZ - 1) / (LEV - 1)) - z[None, :]))
    fall = 1.0 - 0.5 * z / (CZ - 1)
    k = 0.1 + 0.2 * z / (CZ - 1)
    mix = np.zeros((CZ, CZ))
    for i in range(CZ):
        mix[i, i] += 1.0 - 2.0 * k[i]
        mix[i, min(i + 1, CZ - 1)] += k[i]
        mix[i, max(i - 1, 0)] += k[i]
    kap = mix.sum(0)
    c1 = mix @ fall
    c2 = -0.1 * (mix @ (fall * fall))
    kb = mix @ up
    qb = -0.1 * (mix @ (fall[:, None] * up))

    m = np.zeros((344, STATE_ROWS))
    p0, p1, p2 = slice(0, 72), slice(72, 144), slice(144, 216)
    m[0:CZ, p1] = kb / 0.62
    m[0:CZ, p0] = -0.3 * kb / 0.62
    m[64:64 + CZ, p2] = 0.5 * kb
    m[128:128 + CZ, p2] = qb
    dkk = down @ mix @ kb
    m[192:264, p0] = dkk / 1.24 - down @ up
    m[192:264, p1] = 0.8 * dkk / 1.24
    m[264:336, p0] = 0.3 * dkk / 1.24
    m[264:336, p1] = 0.3 * 0.8 * dkk / 1.24 - down @ up
    m[336, p2] = (kap * c1) @ (0.5 * kb)
    m[337, p2] = (kap * c2) @ (0.5 * kb)
    m[338, p2] = (kap * c1) @ qb
    m[339, p2] = (kap * c2) @ qb
    m[340, p2] = kap @ qb
    m[341, p0] = kap @ kb
    m[341, p1] = 0.8 * (kap @ kb)
    m[342, p0] = up.sum(0)
    hi, lo = split_np(m)
    maps = np.concatenate([hi, lo, hi], 1)
    maps = np.concatenate([maps, np.zeros((8, maps.shape[1]), maps.dtype)], 0)

    t = np.zeros((HALF, 2 * ZP))
    t[0:72, 0:CZ] = down @ mix / 1.24
    t[72:144, 0:CZ] = 0.3 * (down @ mix) / 1.24
    t[0:72, ZP:ZP + CZ] = -0.8 * down / 1.24
    t[72:144, ZP:ZP + CZ] = down / 1.24
    hi, lo = split_np(t)
    tail = np.concatenate([hi, lo, hi], 1)

    e = np.zeros((HALF, HALF))
    e[0:72, 0:72] = down @ (mix @ kb - up)
    e[72:144, 72:144] = e[0:72, 0:72]
    hi, lo = split_np(e)
    passive = np.concatenate([hi, lo, hi], 1)
    drift = np.repeat(((down @ (mix @ (mix @ fall))) / CX)[:, None], LANES, 1).astype(np.float32)

    levels = np.zeros((5, ZP))
    levels[0, :CZ] = c1
    levels[1, :CZ] = c2
    levels[2, :CZ] = 0.124 * (1.0 - 2.0 * k)
    levels[3, :CZ] = 0.124 * k
    levels[4, :CZ] = kap
    levels = np.repeat(levels.reshape(-1)[:, None], LANES, 1).astype(np.float32)
    sums = (float((kap * c1 * c1).sum()), float((kap * c1 * c2).sum()), float((kap * c2 * c2).sum()),
            float((kap * c1).sum()), float((kap * c2).sum()))
    return maps, tail, passive, drift, levels, sums


def halves(x):
    high = x.astype(BF16)
    return high, (x - high.astype(F32)).astype(BF16)


def dot(a, b):
    return lax.dot_general(a, b, (((1,), (0,)), ((), ())), preferred_element_type=F32)


def dot_t(a, b):
    return lax.dot_general(a, b, (((1,), (1,)), ((), ())), preferred_element_type=F32)


def east(f):
    return jnp.concatenate([f[1:], pltpu.roll(f[0], 7, 0)[None]], 0)


def west(f):
    return jnp.concatenate([pltpu.roll(f[3], 1, 0)[None], f[:3]], 0)


def xsum(f):
    return jnp.sum((f[0] + f[1]) + (f[2] + f[3]), axis=0, keepdims=True)


def cloud(sums, g_hi, g_lo, maps_ref, tail_ref, lev_ref, sur_ref, prof_ref, part_ref, diag_ref):
    s11, s12, s22, sc1, sc2 = sums
    prof_ref[...] = dot(maps_ref[...], jnp.concatenate([g_hi, g_hi, g_lo], 0))

    def rows(j):
        return jnp.stack([sur_ref[pl.ds(CX * j + v, 8, stride=4), :] for v in range(4)], 0)

    r0, r1, s2 = rows(0), rows(1), rows(2)
    sy = (r1 - 0.3 * r0) * (1.0 / 0.62)
    sw = r0 + 0.8 * r1

    def parts(s):
        e, w = east(s), west(s)
        return 0.6 * s + 0.2 * (e + w), e - w

    ay, dy = parts(sy)
    a2, d2 = parts(s2)
    af, df = 0.5 * a2, 0.5 * d2

    def level(ref, base, z):
        return ref[pl.ds(base + z, 1), :][None]

    def horizontal(z):
        c1 = level(lev_ref, 0, z)
        turn = level(prof_ref, 128, z) + level(lev_ref, ZP, z) * s2
        y = (level(prof_ref, 0, z) + c1 * ay) + turn * dy
        f2 = (level(prof_ref, 64, z) + c1 * af) + turn * df
        one = jnp.log(1.0 + jnp.exp2(y * (0.62 * math.log2(math.e))))
        y = y - one
        e, w = east(y), west(y)
        return (3.0 * y + (e + w)) - f2 * (e - w), one

    def vertical(z, h, above, below):
        v = level(lev_ref, 2 * ZP, z) * h + level(lev_ref, 3 * ZP, z) * (above + below)
        two = jnp.maximum(jnp.log(1.0 + jnp.exp(jnp.minimum(v, 80.0))), v)
        vs = (v[0] + v[1]) + (v[2] + v[3])
        ts = (two[0] + two[1]) + (two[2] + two[3])
        part_ref[pl.ds(pl.multiple_of(z * 8, 8), 8), :] = vs - 0.62 * ts
        return v, two

    h0, rain = horizontal(0)

    def step(i, carry):
        h, below, rain, total_v, total_2 = carry
        for u in range(UNROLL):
            z = 1 + i * UNROLL + u
            above, one = horizontal(z)
            v, two = vertical(z - 1, h, above, below)
            rain, total_v, total_2 = rain + one, total_v + v, total_2 + two
            h, below = above, h
        return h, below, rain, total_v, total_2

    zero = jnp.zeros_like(rain)
    carry = lax.fori_loop(0, (CZ - 1) // UNROLL, step, (h0, h0, rain, zero, zero))
    h, below, rain, total_v, total_2 = carry
    v, two = vertical(CZ - 1, h, h, below)
    total_v, total_2 = total_v + v, total_2 + two
    sum_y = total_v - 0.62 * total_2

    aw, dw = parts(sw)
    ew, ef = s2 * dw, s2 * df
    haw, hdw, hew = east(aw) - west(aw), east(dw) - west(dw), east(ew) - west(ew)
    g11 = xsum(af * haw)
    g12 = xsum(af * hdw + df * haw)
    g13 = xsum(af * hew + ef * haw)
    g22 = xsum(df * hdw)
    g23 = xsum(df * hew + ef * hdw)
    g33 = xsum(ef * hew)
    c1 = lev_ref[0:ZP, :]
    c2 = lev_ref[ZP:2 * ZP, :]
    kap = lev_ref[4 * ZP:5 * ZP, :]
    pf = prof_ref[64:128, :]
    q = prof_ref[128:192, :]
    gram = c1 * (c1 * g11 + q * g12 + c2 * g13) + q * (q * g22 + c2 * g23) + (c2 * c2) * g33
    mean_w = c1 * (xsum(sw) * (1.0 / CX)) + c2 * (xsum(ew) * (1.0 / CX)) - (0.2 / CX) * gram
    qk = q * kap
    sqp = jnp.sum(qk * pf, axis=0, keepdims=True)
    sqq = jnp.sum(qk * q, axis=0, keepdims=True)
    s1p, s2p, s1q, sq2, sq, spw, sb = [prof_ref[336 + i:337 + i, :] for i in range(7)]
    w1 = (spw + sc1 * aw) + (sq * dw + sc2 * ew)
    sum_w = (
        (0.6 * w1 + 0.2 * (east(w1) + west(w1)))
        - 0.2 * (
            haw * ((s1p + s11 * af) + (s1q * df + s12 * ef))
            + hdw * ((sqp + s1q * af) + (sqq * df + sq2 * ef))
            + hew * ((s2p + s12 * af) + (sq2 * df + s22 * ef))
        )
    )
    rain = 0.5 * (rain + total_2)
    moist = (sum_y + 0.3 * sum_w) * (1.0 / (1.24 * CZ))
    heat = (sum_w - 0.8 * sum_y) * (1.0 / (1.24 * CZ)) - sb * (1.0 / CZ)
    for i, rows_out in enumerate((rain, moist, heat)):
        for v in range(4):
            diag_ref[pl.ds(CX * i + v, 8, stride=4), :] = rows_out[v]

    mean_y = part_ref[pl.ds(0, ZP, stride=8), :]
    for s in range(1, 8):
        mean_y = mean_y + part_ref[pl.ds(s, ZP, stride=8), :]
    live = lax.broadcasted_iota(jnp.int32, (ZP, BLOCK), 0) < CZ
    mean_y = jnp.where(live, mean_y * (1.0 / CX), 0.0)
    hi, lo = halves(jnp.concatenate([mean_w, mean_y], 0))
    return prof_ref[192:336, :] + dot(tail_ref[...], jnp.concatenate([hi, hi, lo], 0))


def kernel(sums, n_elem, state_ref, surface_ref, mass_hbm, active_hbm, maps_hbm, tail_hbm, passive_hbm,
           drift_hbm, lev_hbm, out_ref, diag_out_ref,
           xs, hi_ref, lo_ref, su, ones_ref, send, recv, sur, prof, part, diag, both_hi, both_lo,
           mass_ref, active_ref, maps_ref, tail_ref, passive_ref, drift_ref, lev_ref,
           in_sem, send_sem, recv_sem):
    e, g = lax.axis_index("elem"), lax.axis_index("grp")
    after = lax.rem(e + 1, n_elem)
    before = lax.rem(e + n_elem - 1, n_elem)
    barrier = pltpu.get_barrier_semaphore()
    for other in (before, after):
        pl.semaphore_signal(barrier, inc=1, device_id=(other, g), device_id_type=MESH)

    loads = [
        pltpu.make_async_copy(state_ref.at[:, pl.ds(a, n)], xs.at[:, pl.ds(a, n)], in_sem.at[i])
        for i, (a, n) in enumerate(((0, LANES), (3 * LANES, LANES), (LANES, 2 * LANES)))
    ] + [pltpu.make_async_copy(surface_ref, su, in_sem.at[3])]
    small = [
        pltpu.make_async_copy(a, b, in_sem.at[4 + i])
        for i, (a, b) in enumerate((
            (mass_hbm, mass_ref), (active_hbm, active_ref), (maps_hbm, maps_ref), (lev_hbm, lev_ref),
            (tail_hbm, tail_ref), (passive_hbm, passive_ref), (drift_hbm, drift_ref)))
    ]
    for load in loads[:2] + small[:2] + loads[2:] + small[2:]:
        load.start()
    small[1].wait()

    lane = lax.broadcasted_iota(jnp.int32, (1, LANES), 1)
    low = lane < EDGE

    act = [active_ref[:, pl.ds(LANES * b, LANES)].astype(F32) for b in range(4)]
    nil = jnp.zeros((1, LANES), F32)
    inner = [jnp.where(low, 0.0, act[0]), act[1], act[2], jnp.where(low, act[3], 0.0)]
    outer = [jnp.where(low, act[0], 0.0), nil, nil, jnp.where(low, 0.0, act[3])]
    marks = jnp.concatenate(inner + outer, 0)
    r = lax.broadcasted_iota(jnp.int32, (LANES, LANES), 0)
    c = lax.broadcasted_iota(jnp.int32, (LANES, LANES), 1)
    tri = jnp.where(r <= c, 1.0, 0.0).astype(BF16)
    counts = dot(marks.astype(BF16), jnp.concatenate([tri, jnp.ones((LANES, LANES), BF16)], 1))
    run, tot = counts[:, :LANES], counts[:, LANES:]
    offset = nil
    place = []
    for b in range(4):
        inside = run[b:b + 1] + (offset - 1.0)
        outside = (2.0 * BLOCK) - (run[4 + b:5 + b] + (tot[4:5] if b == 3 else 0.0))
        spot = inside if b in (1, 2) else jnp.where(low if b == 3 else ~low, inside, outside)
        place.append(jnp.where(act[b] > 0.5, spot, -1.0))
        offset = offset + tot[b:b + 1]
    where = lax.broadcasted_iota(jnp.int32, (2 * BLOCK, LANES), 0).astype(F32)
    for b in range(4):
        ones_ref[:, LANES * b:LANES * (b + 1)] = jnp.where(where == place[b], 1.0, 0.0).astype(BF16)

    small[0].wait()
    mass0 = mass_ref[:, 0:LANES]
    mass3 = mass_ref[:, 3 * LANES:4 * LANES]
    loads[0].wait()
    loads[1].wait()
    first, last = xs[:, 0:LANES], xs[:, 3 * LANES:4 * LANES]
    send[0, 0:HALF, :] = jnp.where(low, first[:HALF], pltpu.roll(first[HALF:], EDGE, 1))
    send[1, 0:HALF, :] = jnp.where(low, pltpu.roll(last[:HALF], EDGE, 1), last[HALF:])
    send[0, HALF:, :] = jnp.broadcast_to(pltpu.roll(mass0, EDGE, 1), (8, LANES))
    send[1, HALF:, :] = jnp.broadcast_to(pltpu.roll(mass3, EDGE, 1), (8, LANES))
    pl.semaphore_wait(barrier, 2)
    copies = [
        pltpu.make_async_remote_copy(
            src_ref=send.at[i], dst_ref=recv.at[i], send_sem=send_sem.at[i], recv_sem=recv_sem.at[i],
            device_id=(other, g), device_id_type=MESH)
        for i, other in enumerate((before, after))
    ]
    for copy in copies:
        copy.start()

    loads[2].wait()
    loads[3].wait()

    def split_state(lanes):
        hi, lo = halves(xs[:, lanes])
        hi_ref[0:288, lanes] = hi
        lo_ref[0:288, lanes] = lo

    split_state(slice(0, 4 * LANES))
    hi, lo = halves(su[...])
    hi_ref[288:384, :] = hi
    lo_ref[288:384, :] = lo

    for load in small[2:]:
        load.wait()

    def block(i):
        pick = ones_ref[BLOCK * i:BLOCK * (i + 1), :]
        g_hi = dot_t(hi_ref[0:STATE_ROWS, :], pick).astype(BF16)
        g_lo = dot_t(lo_ref[0:STATE_ROWS, :], pick).astype(BF16)
        sur[...] = dot_t(hi_ref[288:384, :], pick) + dot_t(lo_ref[288:384, :], pick)
        tend = cloud(sums, g_hi, g_lo, maps_ref, tail_ref, lev_ref, sur, prof, part, diag)
        hi, lo = halves(jnp.concatenate([tend, diag[...]], 0))
        both_hi[:, BLOCK * i:BLOCK * (i + 1)] = hi
        both_lo[:, BLOCK * i:BLOCK * (i + 1)] = lo

    block(0)

    for copy in copies:
        copy.wait()
    for lanes, own, own_mass, other, keep in (
        (slice(0, LANES), low, mass0, 1, True), (slice(3 * LANES, 4 * LANES), ~low, mass3, 0, False)):
        other_mass = recv[other, HALF:HALF + 1, :]
        share = jnp.where(own, own_mass / (own_mass + other_mass), 1.0)
        rest = jnp.where(own, other_mass / (own_mass + other_mass), 0.0)
        got = recv[other, 0:HALF, :]
        moved = pltpu.roll(got, EDGE, 1)
        top, bottom = (got, moved) if keep else (moved, got)
        xs[0:HALF, lanes] = xs[0:HALF, lanes] * share + top * rest
        xs[HALF:, lanes] = xs[HALF:, lanes] * share + bottom * rest
        split_state(lanes)

    block(1)

    full_hi, full_lo = hi_ref[HALF:2 * HALF, :], lo_ref[HALF:2 * HALF, :]
    slow = dot(passive_ref[...], jnp.concatenate([full_hi, full_hi, full_lo], 0))
    for b in range(4):
        lanes = slice(LANES * b, LANES * (b + 1))
        mean2 = jnp.sum(su[2 * CX:3 * CX, lanes], axis=0, keepdims=True)
        on = act[b] > 0.5
        out_ref[HALF:HALF + LEV, lanes] = xs[HALF:HALF + LEV, lanes] + jnp.where(
            on, slow[:LEV, lanes] + drift_ref[...] * mean2, 0.0)
        out_ref[HALF + LEV:, lanes] = xs[HALF + LEV:, lanes] + jnp.where(on, slow[LEV:, lanes], 0.0)

    back = dot(both_hi[...], ones_ref[...]) + dot(both_lo[...], ones_ref[...])
    out_ref[0:HALF, :] = xs[0:HALF, :] + back[0:HALF]
    diag_out_ref[...] = back[HALF:]


def write(state_ref, diag_ref, state_out, diag_out, sem):
    copies = [pltpu.make_async_copy(state_ref, state_out, sem.at[0]),
              pltpu.make_async_copy(diag_ref, diag_out, sem.at[1])]
    for copy in copies:
        copy.start()
    for copy in copies:
        copy.wait()


def body(n_elem, state, surface, mass, plan, active):
    cols = state.shape[2]
    maps, tail, passive, drift, levels, sums = tables()
    hbm = pl.BlockSpec(memory_space=pltpu.HBM)
    vmem = pl.BlockSpec(memory_space=pltpu.VMEM)
    state, surface, mass, active, maps, tail, passive, drift, levels = [
        pltpu.with_memory_space_constraint(x, pltpu.HBM) for x in (
            state.reshape(4 * LEV, cols), surface.reshape(3 * CX, cols), mass.reshape(1, cols),
            active.reshape(1, cols), *map(jnp.asarray, (maps, tail, passive, drift, levels)))]
    new_state, diag = pl.pallas_call(
        functools.partial(kernel, sums, n_elem),
        out_shape=(pltpu.VMEM((4 * LEV, cols), F32), pltpu.VMEM((3 * CX, cols), F32)),
        in_specs=[hbm] * 9,
        out_specs=(vmem, vmem),
        scratch_shapes=[
            pltpu.VMEM((4 * LEV, cols), F32),
            pltpu.VMEM((384, cols), BF16),
            pltpu.VMEM((384, cols), BF16),
            pltpu.VMEM((3 * CX, cols), F32),
            pltpu.VMEM((2 * BLOCK, cols), BF16),
            pltpu.VMEM((2, HALF + 8, LANES), F32),
            pltpu.VMEM((2, HALF + 8, LANES), F32),
            pltpu.VMEM((3 * CX, BLOCK), F32),
            pltpu.VMEM((352, BLOCK), F32),
            pltpu.VMEM((ZP * 8, BLOCK), F32),
            pltpu.VMEM((3 * CX, BLOCK), F32),
            pltpu.VMEM((HALF + 3 * CX, 2 * BLOCK), BF16),
            pltpu.VMEM((HALF + 3 * CX, 2 * BLOCK), BF16),
            pltpu.VMEM((1, cols), F32),
            pltpu.VMEM((1, cols), jnp.int32),
            pltpu.VMEM(maps.shape, BF16),
            pltpu.VMEM(tail.shape, BF16),
            pltpu.VMEM(passive.shape, BF16),
            pltpu.VMEM(drift.shape, F32),
            pltpu.VMEM(levels.shape, F32),
            pltpu.SemaphoreType.DMA((11,)),
            pltpu.SemaphoreType.DMA((2,)),
            pltpu.SemaphoreType.DMA((2,)),
        ],
        compiler_params=pltpu.CompilerParams(
            collective_id=0, has_side_effects=True, vmem_limit_bytes=32 * 1024 * 1024),
    )(
        state, surface, mass, active, maps, tail, passive, drift, levels,
    )
    new_state, diag = pl.pallas_call(
        write,
        out_shape=(jax.ShapeDtypeStruct(new_state.shape, F32), jax.ShapeDtypeStruct(diag.shape, F32)),
        in_specs=[vmem, vmem],
        out_specs=(hbm, hbm),
        scratch_shapes=[pltpu.SemaphoreType.DMA((2,))],
    )(pltpu.with_memory_space_constraint(new_state, pltpu.VMEM), pltpu.with_memory_space_constraint(diag, pltpu.VMEM))
    return new_state.reshape(4, LEV, cols), diag.reshape(3, CX, cols)


def solution(mesh):
    both = ("elem", "grp")
    return jax.shard_map(
        functools.partial(body, mesh.shape["elem"]),
        mesh=mesh,
        in_specs=(P(None, None, both), P(None, None, both), P(both), P(None, both), P(both)),
        out_specs=(P(None, None, both), P(None, None, both)),
        check_vma=False,
    )
```

```python
import functools
import math

import jax
import jax.numpy as jnp
import ml_dtypes
import numpy as np
from jax import lax
from jax.experimental import pallas as pl
from jax.experimental.pallas import tpu as pltpu
from jax.sharding import PartitionSpec as P

LEV = 72
CZ = 58
CX = 32
EDGE = 64
LANES = 128
BLOCK = 128
ZP = 64
HALF = 2 * LEV
STATE_ROWS = 224
F32 = jnp.float32
BF16 = jnp.bfloat16
MESH = pl.DeviceIdType.MESH


def split_np(matrix):
    high = matrix.astype(np.float32).astype(ml_dtypes.bfloat16)
    low = (matrix - high.astype(np.float64)).astype(np.float32).astype(ml_dtypes.bfloat16)
    return high, low


def tables():
    z = np.arange(CZ, dtype=np.float64)
    lev = np.arange(LEV, dtype=np.float64)
    up = np.maximum(0.0, 1.0 - np.abs(z[:, None] * ((LEV - 1) / (CZ - 1)) - lev[None, :]))
    down = np.maximum(0.0, 1.0 - np.abs(lev[:, None] * ((CZ - 1) / (LEV - 1)) - z[None, :]))
    fall = 1.0 - 0.5 * z / (CZ - 1)
    k = 0.1 + 0.2 * z / (CZ - 1)
    mix = np.zeros((CZ, CZ))
    for i in range(CZ):
        mix[i, i] += 1.0 - 2.0 * k[i]
        mix[i, min(i + 1, CZ - 1)] += k[i]
        mix[i, max(i - 1, 0)] += k[i]
    kap = mix.sum(0)
    c1 = mix @ fall
    c2 = -0.1 * (mix @ (fall * fall))
    kb = mix @ up
    qb = -0.1 * (mix @ (fall[:, None] * up))

    m = np.zeros((344, STATE_ROWS))
    p0, p1, p2 = slice(0, 72), slice(72, 144), slice(144, 216)
    m[0:CZ, p1] = kb / 0.62
    m[0:CZ, p0] = -0.3 * kb / 0.62
    m[64:64 + CZ, p2] = -0.25 * kb
    m[128:128 + CZ, p2] = qb
    dkk = down @ mix @ kb
    m[192:264, p0] = dkk / 1.24 - down @ up
    m[192:264, p1] = 0.8 * dkk / 1.24
    m[264:336, p0] = 0.3 * dkk / 1.24
    m[264:336, p1] = 0.3 * 0.8 * dkk / 1.24 - down @ up
    m[336, p2] = (kap * c1) @ (-0.25 * kb)
    m[337, p2] = (kap * c2) @ (-0.25 * kb)
    m[338, p2] = (kap * c1) @ qb
    m[339, p2] = (kap * c2) @ qb
    m[340, p2] = kap @ qb
    m[341, p0] = kap @ kb
    m[341, p1] = 0.8 * (kap @ kb)
    m[342, p0] = up.sum(0)
    hi, lo = split_np(m)
    maps = np.concatenate([hi, lo, hi], 1)
    maps = np.concatenate([maps, np.zeros((8, maps.shape[1]), maps.dtype)], 0)

    t = np.zeros((HALF, 2 * ZP))
    t[0:72, 0:CZ] = down @ mix / 1.24
    t[72:144, 0:CZ] = 0.3 * (down @ mix) / 1.24
    t[0:72, ZP:ZP + CZ] = -0.8 * down / 1.24
    t[72:144, ZP:ZP + CZ] = down / 1.24
    hi, lo = split_np(t)
    tail = np.concatenate([hi, lo, hi], 1)

    e = np.zeros((HALF, HALF))
    e[0:72, 0:72] = down @ (mix @ kb - up)
    e[72:144, 72:144] = e[0:72, 0:72]
    hi, lo = split_np(e)
    passive = np.concatenate([hi, lo, hi], 1)
    drift = np.repeat(((down @ (mix @ (mix @ fall))) / CX)[:, None], LANES, 1).astype(np.float32)

    rows = np.zeros((3, ZP))
    rows[0, :CZ] = c1
    rows[1, :CZ] = c2
    rows[2, :CZ] = kap
    levels = np.repeat(rows.reshape(-1)[:, None], LANES, 1).astype(np.float32)
    consts = dict(
        c1=[float(a) for a in c1], c2=[float(a) for a in c2],
        stay=[float(a) for a in 0.248 * (1.0 - 2.0 * k)], move=[float(a) for a in 0.248 * k],
        s11=float((kap * c1 * c1).sum()), s12=float((kap * c1 * c2).sum()), s22=float((kap * c2 * c2).sum()),
        sc1=float((kap * c1).sum()), sc2=float((kap * c2).sum()))
    return maps, tail, passive, drift, levels, consts


def halves(x):
    high = x.astype(BF16)
    return high, (x - high.astype(F32)).astype(BF16)


def dot(a, b):
    return lax.dot_general(a, b, (((1,), (0,)), ((), ())), preferred_element_type=F32)


def dot_t(a, b):
    return lax.dot_general(a, b, (((1,), (1,)), ((), ())), preferred_element_type=F32)


class Whole:
    @staticmethod
    def rows(ref, j):
        return jnp.stack([ref[pl.ds(CX * j + v, 8, stride=4), :] for v in range(4)], 0)

    @staticmethod
    def east(f):
        return jnp.concatenate([f[1:], pltpu.roll(f[0], 7, 0)[None]], 0)

    @staticmethod
    def west(f):
        return jnp.concatenate([pltpu.roll(f[3], 1, 0)[None], f[:3]], 0)

    @staticmethod
    def fold(f):
        return (f[0] + f[1]) + (f[2] + f[3])

    @staticmethod
    def join(f):
        return f

    @staticmethod
    def store(ref, i, f):
        for v in range(4):
            ref[pl.ds(CX * i + v, 8, stride=4), :] = f[v]


class Half:
    @staticmethod
    def rows(ref, j):
        low = lax.broadcasted_iota(jnp.int32, (1, LANES), 1) < EDGE
        return jnp.stack([
            jnp.where(low, ref[pl.ds(CX * j + v, 8, stride=2), :], ref[pl.ds(CX * j + 16 + v, 8, stride=2), :])
            for v in range(2)], 0)

    @staticmethod
    def east(f):
        near = pltpu.roll(f[0], 7, 0)
        edge = lax.broadcasted_iota(jnp.int32, (8, LANES), 0) == 7
        return jnp.stack([f[1], jnp.where(edge, swap(near), near)], 0)

    @staticmethod
    def west(f):
        near = pltpu.roll(f[1], 1, 0)
        edge = lax.broadcasted_iota(jnp.int32, (8, LANES), 0) == 0
        return jnp.stack([jnp.where(edge, swap(near), near), f[0]], 0)

    @staticmethod
    def fold(f):
        return f[0] + f[1]

    @staticmethod
    def join(f):
        return f + swap(f)

    @staticmethod
    def store(ref, i, f):
        low = lax.broadcasted_iota(jnp.int32, (1, LANES), 1) < EDGE
        for v in range(2):
            other = swap(f[v])
            ref[pl.ds(CX * i + v, 8, stride=2), :] = jnp.where(low, f[v], other)
            ref[pl.ds(CX * i + 16 + v, 8, stride=2), :] = jnp.where(low, other, f[v])


def swap(x):
    return pltpu.roll(x, EDGE, 1)


def prepare(form, sur_ref):
    east, west = form.east, form.west
    r0, r1, s2 = form.rows(sur_ref, 0), form.rows(sur_ref, 1), form.rows(sur_ref, 2)
    sy, sw = (r1 - 0.3 * r0) * (1.0 / 0.62), r0 + 0.8 * r1

    def xsum(f):
        return form.join(jnp.sum(form.fold(f), axis=0, keepdims=True))

    def parts(s):
        e, w = east(s), west(s)
        return 0.6 * s + 0.2 * (e + w), e - w

    ay, dy = parts(sy)
    a2, d2 = parts(s2)
    af, df = -0.25 * a2, -0.25 * d2
    aw, dw = parts(sw)
    ew, ef = s2 * dw, s2 * df
    haw, hdw, hew = east(aw) - west(aw), east(dw) - west(dw), east(ew) - west(ew)
    gram = (xsum(af * haw), xsum(af * hdw + df * haw), xsum(af * hew + ef * haw),
            xsum(df * hdw), xsum(df * hew + ef * hdw), xsum(ef * hew))
    means = (xsum(sw) * (1.0 / CX), xsum(ew) * (1.0 / CX))
    return s2, ay, dy, af, df, aw, dw, ef, haw, hdw, hew, gram, means


def cloud(form, consts, prep, prof_ref, lanes, tail_ref, lev_ref, part_ref, diag_ref):
    s2, ay, dy, af, df, aw, dw, ef, haw, hdw, hew, gram, means = prep
    east, west = form.east, form.west

    def level(start, z):
        return prof_ref[start + z:start + z + 1, lanes][None]

    def horizontal(z):
        turn = level(128, z) + consts["c2"][z] * s2
        y = (level(0, z) + consts["c1"][z] * ay) + turn * dy
        pull = (level(64, z) + consts["c1"][z] * af) + turn * df
        one = jnp.log(1.0 + jnp.exp2(y * (0.62 * math.log2(math.e))))
        y = y - one
        e, w = east(y), west(y)
        return (1.5 * y + w) + pull * (e - w), one

    def vertical(z, h, above, below):
        v = consts["stay"][z] * h + consts["move"][z] * (above + below)
        two = jnp.maximum(jnp.log(1.0 + jnp.exp(jnp.minimum(v, 80.0))), v)
        part_ref[8 * z:8 * z + 8, :] = form.fold(v) - 0.62 * form.fold(two)
        return v, two

    h, rain = horizontal(0)
    below = h
    total_v = total_2 = None
    for z in range(CZ):
        if z + 1 < CZ:
            above, one = horizontal(z + 1)
            rain = rain + one
        else:
            above = h
        v, two = vertical(z, h, above, below)
        total_v = v if z == 0 else total_v + v
        total_2 = two if z == 0 else total_2 + two
        h, below = above, h
    sum_y = total_v - 0.62 * total_2

    pf = prof_ref[64:128, lanes] - 0.5
    q = prof_ref[128:192, lanes]
    s1p, s2p, s1q, sq2, sq, spw, sb = [prof_ref[336 + i:337 + i, lanes] for i in range(7)]
    c1 = lev_ref[0:ZP, :]
    c2 = lev_ref[ZP:2 * ZP, :]
    kap = lev_ref[2 * ZP:3 * ZP, :]
    g11, g12, g13, g22, g23, g33 = gram
    bend = c1 * (c1 * g11 + q * g12 + c2 * g13) + q * (q * g22 + c2 * g23) + (c2 * c2) * g33
    mean_w = c1 * means[0] + c2 * means[1] + (0.4 / CX) * bend
    qk = q * kap
    sqp = jnp.sum(qk * pf, axis=0, keepdims=True)
    sqq = jnp.sum(qk * q, axis=0, keepdims=True)
    s11, s12, s22 = consts["s11"], consts["s12"], consts["s22"]
    w1 = (spw + consts["sc1"] * aw) + (sq * dw + consts["sc2"] * (s2 * dw))
    sum_w = (
        (0.6 * w1 + 0.2 * (east(w1) + west(w1)))
        + 0.4 * (
            haw * ((s1p + s11 * af) + (s1q * df + s12 * ef))
            + hdw * ((sqp + s1q * af) + (sqq * df + sq2 * ef))
            + hew * ((s2p + s12 * af) + (sq2 * df + s22 * ef))
        )
    )
    form.store(diag_ref, 0, 0.5 * (rain + total_2))
    form.store(diag_ref, 1, (sum_y + 0.3 * sum_w) * (1.0 / (1.24 * CZ)))
    form.store(diag_ref, 2, (sum_w - 0.8 * sum_y) * (1.0 / (1.24 * CZ)) - sb * (1.0 / CZ))

    mean_y = part_ref[pl.ds(0, CZ, stride=8), :]
    for s in range(1, 8):
        mean_y = mean_y + part_ref[pl.ds(s, CZ, stride=8), :]
    mean_y = form.join(mean_y) * (1.0 / CX)
    hi, lo = halves(jnp.concatenate([mean_w, mean_y, jnp.zeros((ZP - CZ, LANES), F32)], 0))
    return prof_ref[192:336, lanes] + dot(tail_ref[...], jnp.concatenate([hi, hi, lo], 0))


PARTS = ((slice(0, 112), slice(8, 64)), (slice(112, 224), slice(64, 120)), (slice(224, 288), slice(120, 152)))
SENT = ((0, 64), (64, 56), (120, 32))


def kernel(consts, n_elem, state_ref, surface_ref, mass_hbm, active_hbm, maps_hbm, tail_hbm, passive_hbm,
           drift_hbm, lev_hbm, out_ref, diag_out_ref,
           xs, hi_ref, lo_ref, su, ones_ref, send, recv, sur, prof, edge_prof, part, diag, both_hi, both_lo, own_ref,
           mass_ref, active_ref, maps_ref, tail_ref, passive_ref, drift_ref, lev_ref,
           in_sem, send_sem, recv_sem):
    e, g = lax.axis_index("elem"), lax.axis_index("grp")
    after = lax.rem(e + 1, n_elem)
    before = lax.rem(e + n_elem - 1, n_elem)
    barrier = pltpu.get_barrier_semaphore()
    for other in (before, after):
        pl.semaphore_signal(barrier, inc=1, device_id=(other, g), device_id_type=MESH)

    tiles = [slice(LANES * b, LANES * (b + 1)) for b in range(4)]
    ends = (tiles[3], tiles[0])
    loads = [
        pltpu.make_async_copy(state_ref.at[rows, lanes], xs.at[rows, lanes], in_sem.at[2 * c + i])
        for c, (rows, _) in enumerate(PARTS) for i, lanes in enumerate(ends)
    ] + [
        pltpu.make_async_copy(state_ref.at[:, pl.ds(LANES, 2 * LANES)], xs.at[:, pl.ds(LANES, 2 * LANES)], in_sem.at[6]),
        pltpu.make_async_copy(surface_ref, su, in_sem.at[7]),
    ]
    small = [
        pltpu.make_async_copy(a, b, in_sem.at[8 + i])
        for i, (a, b) in enumerate((
            (mass_hbm, mass_ref), (active_hbm, active_ref), (maps_hbm, maps_ref), (lev_hbm, lev_ref),
            (tail_hbm, tail_ref), (passive_hbm, passive_ref), (drift_hbm, drift_ref)))
    ]
    for load in small[:1] + loads[:6] + small[1:2] + loads[6:] + small[2:]:
        load.start()

    low = lax.broadcasted_iota(jnp.int32, (1, LANES), 1) < EDGE
    sides = (~low, low)

    def twice(x, i):
        return jnp.where(sides[i], x, swap(x))

    sent = [
        pltpu.make_async_remote_copy(
            src_ref=send.at[i, pl.ds(*rows)], dst_ref=recv.at[i, pl.ds(*rows)],
            send_sem=send_sem.at[2 * c + i], recv_sem=recv_sem.at[2 * c + i],
            device_id=(other, g), device_id_type=MESH)
        for c, rows in enumerate(SENT) for i, other in enumerate((after, before))
    ]

    def enter():
        pl.semaphore_wait(barrier, 2)

    pl.when(e != 0)(enter)
    small[0].wait()
    for c, (rows, to) in enumerate(PARTS):
        for i, lanes in enumerate(ends):
            if c == 0:
                send[i, 0:8, :] = jnp.broadcast_to(twice(mass_ref[:, lanes], i), (8, LANES))
            loads[2 * c + i].wait()
            x = xs[rows, lanes]
            a, b = x[:x.shape[0] // 2], x[x.shape[0] // 2:]
            send[i, to, :] = jnp.where(low, swap(a), b) if i == 0 else jnp.where(low, a, swap(b))
            pl.when(e != 0)(sent[2 * c + i].start)

    small[1].wait()
    act = [active_ref[:, lanes].astype(F32) for lanes in tiles]
    inner = [jnp.where(low, 0.0, act[0]), act[1], act[2], jnp.where(low, act[3], 0.0)]
    marks = jnp.concatenate(inner + [jnp.zeros((4, LANES), F32)], 0)
    r = lax.broadcasted_iota(jnp.int32, (LANES, LANES), 0)
    c = lax.broadcasted_iota(jnp.int32, (LANES, LANES), 1)
    tri = jnp.where(r <= c, 1.0, 0.0).astype(BF16)
    counts = dot(marks.astype(BF16), jnp.concatenate([tri, jnp.ones((LANES, LANES), BF16)], 1))
    where = lax.broadcasted_iota(jnp.int32, (2 * BLOCK, LANES), 0).astype(F32)
    offset = jnp.full((1, LANES), -1.0, F32)
    for b, lanes in enumerate(tiles):
        place = jnp.where(inner[b] > 0.5, counts[b:b + 1, :LANES] + offset, -1.0)
        ones_ref[:, lanes] = jnp.where(where == place, 1.0, 0.0).astype(BF16)
        offset = offset + counts[b:b + 1, LANES:]

    loads[6].wait()
    loads[7].wait()
    hi, lo = halves(xs[...])
    hi_ref[0:288, :] = hi
    lo_ref[0:288, :] = lo
    hi, lo = halves(su[...])
    hi_ref[288:384, :] = hi
    lo_ref[288:384, :] = lo
    for load in small[2:]:
        load.wait()

    def gather(ref, rows):
        return dot_t(ref[rows, :], ones_ref[...])

    def maps(hi, lo):
        x = dot(maps_ref[...], jnp.concatenate([hi, hi, lo], 0))
        return jnp.concatenate([x[:64], x[64:128] + 0.5, x[128:]], 0)

    main = slice(0, STATE_ROWS)
    prof[...] = maps(gather(hi_ref, main).astype(BF16), gather(lo_ref, main).astype(BF16))
    found = gather(hi_ref, slice(288, 384)) + gather(lo_ref, slice(288, 384))
    for i in range(2):
        lanes = tiles[i]
        sur[...] = found[:, lanes]
        tend = cloud(Whole, consts, prepare(Whole, sur), prof, lanes, tail_ref, lev_ref, part, diag)
        hi, lo = halves(jnp.concatenate([tend, diag[...]], 0))
        both_hi[:, lanes] = hi
        both_lo[:, lanes] = lo

    @pl.when(e == 0)
    def _():
        enter()
        for copy in sent:
            copy.start()

    def passive(lanes, hi, lo):
        slow = dot(passive_ref[...], jnp.concatenate([hi, hi, lo], 0))
        mean2 = jnp.sum(su[2 * CX:3 * CX, lanes], axis=0, keepdims=True)
        return jnp.concatenate([slow[:LEV] + drift_ref[...] * mean2, slow[LEV:]], 0)

    for b, lanes in enumerate(tiles):
        out_ref[HALF:, lanes] = xs[HALF:, lanes] + jnp.where(
            act[b] > 0.5, passive(lanes, hi_ref[HALF:288, lanes], lo_ref[HALF:288, lanes]), 0.0)
    back = dot(both_hi[...], ones_ref[...]) + dot(both_lo[...], ones_ref[...])
    out_ref[0:HALF, :] = xs[0:HALF, :] + back[0:HALF]
    diag_out_ref[...] = back[HALF:]

    for i, lanes in enumerate(ends):
        got = 1 - i
        sur[...] = twice(su[:, lanes], i)
        prep = prepare(Half, sur)
        own_ref[...] = twice(xs[:, lanes], i)
        own_mass = twice(mass_ref[:, lanes], i)
        on = jnp.where(sides[i], act[3 if i == 0 else 0], 0.0) > 0.5

        def shared(c, share, rest):
            rows, to = PARTS[c]
            x = recv[got, to, :]
            y = swap(x)
            x = jnp.concatenate([jnp.where(low, x, y), jnp.where(low, y, x)], 0)
            return own_ref[rows, :] * share + x * rest

        sent[got].wait_recv()
        sent[2 + got].wait_recv()
        other_mass = recv[got, 0:1, :]
        scale = 1.0 / (own_mass + other_mass)
        share, rest = own_mass * scale, other_mass * scale
        first = jnp.concatenate([shared(0, share, rest), shared(1, share, rest)], 0)
        hi, lo = halves(first)
        edge_prof[...] = maps(hi, lo)
        tend = cloud(Half, consts, prep, edge_prof, tiles[0], tail_ref, lev_ref, part, diag)
        sent[4 + got].wait_recv()
        last = shared(2, share, rest)
        last_hi, last_lo = halves(last)
        slow = passive(lanes, jnp.concatenate([hi[HALF:], last_hi], 0), jnp.concatenate([lo[HALF:], last_lo], 0))
        new = jnp.concatenate([first, last], 0) + jnp.where(on, jnp.concatenate([tend, slow], 0), 0.0)
        out_ref[:, lanes] = jnp.where(sides[i], new, out_ref[:, lanes])
        diag_out_ref[:, lanes] = jnp.where(sides[i], jnp.where(on, diag[...], 0.0), diag_out_ref[:, lanes])

    for copy in sent:
        copy.wait_send()


def write(state_ref, diag_ref, state_out, diag_out, sem):
    copies = [pltpu.make_async_copy(state_ref, state_out, sem.at[0]),
              pltpu.make_async_copy(diag_ref, diag_out, sem.at[1])]
    for copy in copies:
        copy.start()
    for copy in copies:
        copy.wait()


def body(n_elem, state, surface, mass, plan, active):
    cols = state.shape[2]
    maps, tail, passive, drift, levels, consts = tables()
    hbm = pl.BlockSpec(memory_space=pltpu.HBM)
    vmem = pl.BlockSpec(memory_space=pltpu.VMEM)
    state, surface, mass, active, maps, tail, passive, drift, levels = [
        pltpu.with_memory_space_constraint(x, pltpu.HBM) for x in (
            state.reshape(4 * LEV, cols), surface.reshape(3 * CX, cols), mass.reshape(1, cols),
            active.reshape(1, cols), *map(jnp.asarray, (maps, tail, passive, drift, levels)))]
    new_state, diag = pl.pallas_call(
        functools.partial(kernel, consts, n_elem),
        out_shape=(pltpu.VMEM((4 * LEV, cols), F32), pltpu.VMEM((3 * CX, cols), F32)),
        in_specs=[hbm] * 9,
        out_specs=(vmem, vmem),
        scratch_shapes=[
            pltpu.VMEM((4 * LEV, cols), F32),
            pltpu.VMEM((384, cols), BF16),
            pltpu.VMEM((384, cols), BF16),
            pltpu.VMEM((3 * CX, cols), F32),
            pltpu.VMEM((2 * BLOCK, cols), BF16),
            pltpu.VMEM((2, HALF + 8, LANES), F32),
            pltpu.VMEM((2, HALF + 8, LANES), F32),
            pltpu.VMEM((3 * CX, BLOCK), F32),
            pltpu.VMEM((352, 2 * BLOCK), F32),
            pltpu.VMEM((352, BLOCK), F32),
            pltpu.VMEM((ZP * 8, BLOCK), F32),
            pltpu.VMEM((3 * CX, BLOCK), F32),
            pltpu.VMEM((HALF + 3 * CX, 2 * BLOCK), BF16),
            pltpu.VMEM((HALF + 3 * CX, 2 * BLOCK), BF16),
            pltpu.VMEM((4 * LEV, LANES), F32),
            pltpu.VMEM((1, cols), F32),
            pltpu.VMEM((1, cols), jnp.int32),
            pltpu.VMEM(maps.shape, BF16),
            pltpu.VMEM(tail.shape, BF16),
            pltpu.VMEM(passive.shape, BF16),
            pltpu.VMEM(drift.shape, F32),
            pltpu.VMEM(levels.shape, F32),
            pltpu.SemaphoreType.DMA((15,)),
            pltpu.SemaphoreType.DMA((6,)),
            pltpu.SemaphoreType.DMA((6,)),
        ],
        compiler_params=pltpu.CompilerParams(
            collective_id=0, has_side_effects=True, vmem_limit_bytes=32 * 1024 * 1024),
    )(
        state, surface, mass, active, maps, tail, passive, drift, levels,
    )
    new_state, diag = pl.pallas_call(
        write,
        out_shape=(jax.ShapeDtypeStruct(new_state.shape, F32), jax.ShapeDtypeStruct(diag.shape, F32)),
        in_specs=[vmem, vmem],
        out_specs=(hbm, hbm),
        scratch_shapes=[pltpu.SemaphoreType.DMA((2,))],
    )(pltpu.with_memory_space_constraint(new_state, pltpu.VMEM), pltpu.with_memory_space_constraint(diag, pltpu.VMEM))
    return new_state.reshape(4, LEV, cols), diag.reshape(3, CX, cols)


def solution(mesh):
    both = ("elem", "grp")
    return jax.shard_map(
        functools.partial(body, mesh.shape["elem"]),
        mesh=mesh,
        in_specs=(P(None, None, both), P(None, None, both), P(both), P(None, both), P(both)),
        out_specs=(P(None, None, both), P(None, None, both)),
        check_vma=False,
    )
```

```python
import functools
import math

import jax
import jax.numpy as jnp
import ml_dtypes
import numpy as np
from jax import lax
from jax.experimental import pallas as pl
from jax.experimental.pallas import tpu as pltpu
from jax.sharding import PartitionSpec as P

LEV = 72
CZ = 58
CX = 32
EDGE = 64
LANES = 128
BLOCK = 128
ZP = 64
HALF = 2 * LEV
STATE_ROWS = 224
F32 = jnp.float32
BF16 = jnp.bfloat16
MESH = pl.DeviceIdType.MESH


def split_np(matrix):
    high = matrix.astype(np.float32).astype(ml_dtypes.bfloat16)
    low = (matrix - high.astype(np.float64)).astype(np.float32).astype(ml_dtypes.bfloat16)
    return high, low


def tables():
    z = np.arange(CZ, dtype=np.float64)
    lev = np.arange(LEV, dtype=np.float64)
    up = np.maximum(0.0, 1.0 - np.abs(z[:, None] * ((LEV - 1) / (CZ - 1)) - lev[None, :]))
    down = np.maximum(0.0, 1.0 - np.abs(lev[:, None] * ((CZ - 1) / (LEV - 1)) - z[None, :]))
    fall = 1.0 - 0.5 * z / (CZ - 1)
    k = 0.1 + 0.2 * z / (CZ - 1)
    mix = np.zeros((CZ, CZ))
    for i in range(CZ):
        mix[i, i] += 1.0 - 2.0 * k[i]
        mix[i, min(i + 1, CZ - 1)] += k[i]
        mix[i, max(i - 1, 0)] += k[i]
    kap = mix.sum(0)
    c1 = mix @ fall
    c2 = -0.1 * (mix @ (fall * fall))
    kb = mix @ up
    qb = -0.1 * (mix @ (fall[:, None] * up))

    py, p2, p0 = slice(0, 72), slice(72, 144), slice(144, 216)
    m = np.zeros((208, HALF))
    m[0:CZ, py] = kb / 0.62
    m[64:64 + CZ, p2] = -0.25 * kb
    m[128:128 + CZ, p2] = qb
    m[192, p2] = (kap * c1) @ (-0.25 * kb)
    m[193, p2] = (kap * c2) @ (-0.25 * kb)
    m[194, p2] = (kap * c1) @ qb
    m[195, p2] = (kap * c2) @ qb
    m[196, p2] = kap @ qb
    hi, lo = split_np(m)
    maps = np.concatenate([hi, lo, hi], 1)
    dkk = down @ mix @ kb
    m = np.zeros((160, STATE_ROWS))
    m[0:72, p0] = dkk - down @ up
    m[0:72, py] = 0.8 * dkk / 1.24
    m[72:144, p0] = 0.3 * (dkk - down @ up)
    m[72:144, py] = 0.24 * dkk / 1.24 - down @ up
    m[144, p0] = 1.24 * (kap @ kb)
    m[144, py] = 0.8 * (kap @ kb)
    m[145, p0] = up.sum(0)
    hi, lo = split_np(m)
    more = np.concatenate([hi, lo, hi], 1)

    t = np.zeros((HALF, 2 * ZP))
    t[0:72, 0:CZ] = down @ mix / 1.24
    t[72:144, 0:CZ] = 0.3 * (down @ mix) / 1.24
    t[0:72, ZP:ZP + CZ] = -0.8 * down / 1.24
    t[72:144, ZP:ZP + CZ] = down / 1.24
    hi, lo = split_np(t)
    tail = np.concatenate([hi, lo, hi], 1)

    e = np.zeros((HALF, HALF))
    e[0:72, 0:72] = down @ (mix @ kb - up)
    e[72:144, 72:144] = e[0:72, 0:72]
    hi, lo = split_np(e)
    passive = np.concatenate([hi, lo, hi], 1)
    drift = np.repeat(((down @ (mix @ (mix @ fall))) / CX)[:, None], LANES, 1).astype(np.float32)

    rows = np.zeros((3, ZP))
    rows[0, :CZ] = c1
    rows[1, :CZ] = c2
    rows[2, :CZ] = kap
    levels = np.repeat(rows.reshape(-1)[:, None], LANES, 1).astype(np.float32)
    consts = dict(
        c1=[float(a) for a in c1], c2=[float(a) for a in c2],
        stay=[float(a) for a in 0.248 * (1.0 - 2.0 * k)], move=[float(a) for a in 0.248 * k],
        s11=float((kap * c1 * c1).sum()), s12=float((kap * c1 * c2).sum()), s22=float((kap * c2 * c2).sum()),
        sc1=float((kap * c1).sum()), sc2=float((kap * c2).sum()))
    return maps, more, tail, passive, drift, levels, consts


def halves(x):
    high = x.astype(BF16)
    return high, (x - high.astype(F32)).astype(BF16)


def dot(a, b):
    return lax.dot_general(a, b, (((1,), (0,)), ((), ())), preferred_element_type=F32)


def dot_t(a, b):
    return lax.dot_general(a, b, (((1,), (1,)), ((), ())), preferred_element_type=F32)


class Whole:
    @staticmethod
    def rows(ref, j):
        return jnp.stack([ref[pl.ds(CX * j + v, 8, stride=4), :] for v in range(4)], 0)

    @staticmethod
    def east(f):
        return jnp.concatenate([f[1:], pltpu.roll(f[0], 7, 0)[None]], 0)

    @staticmethod
    def west(f):
        return jnp.concatenate([pltpu.roll(f[3], 1, 0)[None], f[:3]], 0)

    @staticmethod
    def fold(f):
        return (f[0] + f[1]) + (f[2] + f[3])

    @staticmethod
    def join(f):
        return f

    @staticmethod
    def store(ref, i, f):
        for v in range(4):
            ref[pl.ds(CX * i + v, 8, stride=4), :] = f[v]


class Half:
    @staticmethod
    def rows(ref, j):
        low = lax.broadcasted_iota(jnp.int32, (1, LANES), 1) < EDGE
        return jnp.stack([
            jnp.where(low, ref[pl.ds(CX * j + v, 8, stride=2), :], ref[pl.ds(CX * j + 16 + v, 8, stride=2), :])
            for v in range(2)], 0)

    @staticmethod
    def east(f):
        near = pltpu.roll(f[0], 7, 0)
        edge = lax.broadcasted_iota(jnp.int32, (8, LANES), 0) == 7
        return jnp.stack([f[1], jnp.where(edge, swap(near), near)], 0)

    @staticmethod
    def west(f):
        near = pltpu.roll(f[1], 1, 0)
        edge = lax.broadcasted_iota(jnp.int32, (8, LANES), 0) == 0
        return jnp.stack([jnp.where(edge, swap(near), near), f[0]], 0)

    @staticmethod
    def fold(f):
        return f[0] + f[1]

    @staticmethod
    def join(f):
        return f + swap(f)

    @staticmethod
    def store(ref, i, f):
        low = lax.broadcasted_iota(jnp.int32, (1, LANES), 1) < EDGE
        for v in range(2):
            other = swap(f[v])
            ref[pl.ds(CX * i + v, 8, stride=2), :] = jnp.where(low, f[v], other)
            ref[pl.ds(CX * i + 16 + v, 8, stride=2), :] = jnp.where(low, other, f[v])


def swap(x):
    return pltpu.roll(x, EDGE, 1)


def prepare(form, sur_ref):
    east, west = form.east, form.west
    r0, r1, s2 = form.rows(sur_ref, 0), form.rows(sur_ref, 1), form.rows(sur_ref, 2)
    sy, sw = (r1 - 0.3 * r0) * (1.0 / 0.62), r0 + 0.8 * r1

    def xsum(f):
        return form.join(jnp.sum(form.fold(f), axis=0, keepdims=True))

    def parts(s):
        e, w = east(s), west(s)
        return 0.6 * s + 0.2 * (e + w), e - w

    ay, dy = parts(sy)
    a2, d2 = parts(s2)
    af, df = -0.25 * a2, -0.25 * d2
    aw, dw = parts(sw)
    ew, ef = s2 * dw, s2 * df
    haw, hdw, hew = east(aw) - west(aw), east(dw) - west(dw), east(ew) - west(ew)
    gram = (xsum(af * haw), xsum(af * hdw + df * haw), xsum(af * hew + ef * haw),
            xsum(df * hdw), xsum(df * hew + ef * hdw), xsum(ef * hew))
    means = (xsum(sw) * (1.0 / CX), xsum(ew) * (1.0 / CX))
    return s2, ay, dy, af, df, aw, dw, ef, haw, hdw, hew, gram, means


def cloud(form, consts, prep, prof_ref, lanes, tail_ref, lev_ref, part_ref, diag_ref, at={}):
    s2, ay, dy, af, df, aw, dw, ef, haw, hdw, hew, gram, means = prep
    east, west = form.east, form.west

    def level(start, z):
        return prof_ref[start + z:start + z + 1, lanes][None]

    def horizontal(z):
        turn = level(128, z) + consts["c2"][z] * s2
        y = (level(0, z) + consts["c1"][z] * ay) + turn * dy
        pull = (level(64, z) + consts["c1"][z] * af) + turn * df
        one = jnp.log(1.0 + jnp.exp2(y * (0.62 * math.log2(math.e))))
        y = y - one
        e, w = east(y), west(y)
        return (1.5 * y + w) + pull * (e - w), one

    def vertical(z, h, above, below):
        v = consts["stay"][z] * h + consts["move"][z] * (above + below)
        two = jnp.maximum(jnp.log(1.0 + jnp.exp(jnp.minimum(v, 80.0))), v)
        part_ref[8 * z:8 * z + 8, :] = form.fold(v) - 0.62 * form.fold(two)
        return v, two

    h, rain = horizontal(0)
    below = h
    total_v = total_2 = None
    for z in range(CZ):
        if z in at:
            at[z]()
        if z + 1 < CZ:
            above, one = horizontal(z + 1)
            rain = rain + one
        else:
            above = h
        v, two = vertical(z, h, above, below)
        total_v = v if z == 0 else total_v + v
        total_2 = two if z == 0 else total_2 + two
        h, below = above, h
    sum_y = total_v - 0.62 * total_2

    pf = prof_ref[64:128, lanes] - 0.5
    q = prof_ref[128:192, lanes]
    s1p, s2p, s1q, sq2, sq = [prof_ref[192 + i:193 + i, lanes] for i in range(5)]
    spw, sb = [prof_ref[352 + i:353 + i, lanes] for i in range(2)]
    c1 = lev_ref[0:ZP, :]
    c2 = lev_ref[ZP:2 * ZP, :]
    kap = lev_ref[2 * ZP:3 * ZP, :]
    g11, g12, g13, g22, g23, g33 = gram
    bend = c1 * (c1 * g11 + q * g12 + c2 * g13) + q * (q * g22 + c2 * g23) + (c2 * c2) * g33
    mean_w = c1 * means[0] + c2 * means[1] + (0.4 / CX) * bend
    qk = q * kap
    sqp = jnp.sum(qk * pf, axis=0, keepdims=True)
    sqq = jnp.sum(qk * q, axis=0, keepdims=True)
    s11, s12, s22 = consts["s11"], consts["s12"], consts["s22"]
    w1 = (spw + consts["sc1"] * aw) + (sq * dw + consts["sc2"] * (s2 * dw))
    sum_w = (
        (0.6 * w1 + 0.2 * (east(w1) + west(w1)))
        + 0.4 * (
            haw * ((s1p + s11 * af) + (s1q * df + s12 * ef))
            + hdw * ((sqp + s1q * af) + (sqq * df + sq2 * ef))
            + hew * ((s2p + s12 * af) + (sq2 * df + s22 * ef))
        )
    )
    form.store(diag_ref, 0, 0.5 * (rain + total_2))
    form.store(diag_ref, 1, (sum_y + 0.3 * sum_w) * (1.0 / (1.24 * CZ)))
    form.store(diag_ref, 2, (sum_w - 0.8 * sum_y) * (1.0 / (1.24 * CZ)) - sb * (1.0 / CZ))

    mean_y = part_ref[pl.ds(0, CZ, stride=8), :]
    for s in range(1, 8):
        mean_y = mean_y + part_ref[pl.ds(s, CZ, stride=8), :]
    mean_y = form.join(mean_y) * (1.0 / CX)
    hi, lo = halves(jnp.concatenate([mean_w, mean_y, jnp.zeros((ZP - CZ, LANES), F32)], 0))
    return prof_ref[208:352, lanes] + dot(tail_ref[...], jnp.concatenate([hi, hi, lo], 0))


SENT = ((0, 80), (80, 72))


def kernel(consts, n_elem, state_ref, surface_ref, mass_hbm, active_hbm, maps_hbm, more_hbm, tail_hbm, passive_hbm,
           drift_hbm, lev_hbm, out_ref, diag_out_ref,
           xs, hi_ref, lo_ref, su, ones_ref, send, recv, sur, prof, edge_prof, part, diag, both_hi, both_lo, own_ref,
           mass_ref, active_ref, maps_ref, more_ref, tail_ref, passive_ref, drift_ref, lev_ref,
           in_sem, send_sem, recv_sem):
    e, g = lax.axis_index("elem"), lax.axis_index("grp")
    after = lax.rem(e + 1, n_elem)
    before = lax.rem(e + n_elem - 1, n_elem)
    barrier = pltpu.get_barrier_semaphore()
    for other in (before, after):
        pl.semaphore_signal(barrier, inc=1, device_id=(other, g), device_id_type=MESH)

    tiles = [slice(LANES * b, LANES * (b + 1)) for b in range(4)]
    ends = (tiles[3], tiles[0])
    loads = [
        pltpu.make_async_copy(state_ref.at[rows, lanes], xs.at[rows, lanes], in_sem.at[k])
        for k, (rows, lanes) in enumerate(
            (rows, lanes) for rows in (slice(0, 3 * LEV), slice(3 * LEV, 4 * LEV)) for lanes in ends)
    ] + [
        pltpu.make_async_copy(state_ref.at[:, pl.ds(LANES, 2 * LANES)], xs.at[:, pl.ds(LANES, 2 * LANES)], in_sem.at[4]),
        pltpu.make_async_copy(surface_ref, su, in_sem.at[5]),
    ]
    small = [
        pltpu.make_async_copy(a, b, in_sem.at[6 + i])
        for i, (a, b) in enumerate((
            (mass_hbm, mass_ref), (active_hbm, active_ref), (maps_hbm, maps_ref), (lev_hbm, lev_ref),
            (more_hbm, more_ref), (tail_hbm, tail_ref), (passive_hbm, passive_ref), (drift_hbm, drift_ref)))
    ]
    for load in small[:1] + loads[:4] + small[1:2] + loads[4:] + small[2:]:
        load.start()

    low = lax.broadcasted_iota(jnp.int32, (1, LANES), 1) < EDGE

    def end_copy(c, i):
        rows = pl.ds(*SENT[c])
        return pltpu.make_async_remote_copy(
            src_ref=send.at[i, rows], dst_ref=recv.at[i, rows],
            send_sem=send_sem.at[2 * c + i], recv_sem=recv_sem.at[2 * c + i],
            device_id=((after, before)[i] if isinstance(i, int) else after, g), device_id_type=MESH)

    sent = [end_copy(c, i) for i in range(2) for c in range(2)]

    def enter():
        pl.semaphore_wait(barrier, 2)

    def exchange():
        enter()
        for copy in sent:
            copy.start()

    first_e, last_e = e == 0, e == n_elem - 1
    pl.when(last_e)(enter)
    small[0].wait()
    for i, lanes in enumerate(ends):
        mass = mass_ref[:, lanes]
        mass = jnp.where(low, swap(mass), mass) if i == 0 else jnp.where(low, mass, swap(mass))
        send[i, 0:8, :] = jnp.broadcast_to(mass, (8, LANES))
        loads[i].wait()
        p0 = xs[0:LEV, lanes]
        py, p2 = xs[LEV:2 * LEV, lanes] - 0.3 * p0, xs[2 * LEV:3 * LEV, lanes]
        send[i, 8:80, :] = jnp.where(low, swap(py), p2) if i == 0 else jnp.where(low, py, swap(p2))
        pl.when(last_e)(sent[2 * i].start)
        loads[2 + i].wait()
        p0, p3 = xs[0:LEV, lanes], xs[3 * LEV:, lanes]
        send[i, 80:152, :] = jnp.where(low, swap(p0), p3) if i == 0 else jnp.where(low, p0, swap(p3))
        pl.when(last_e)(sent[2 * i + 1].start)

    small[1].wait()
    act = [active_ref[:, lanes].astype(F32) for lanes in tiles]
    inner = [jnp.where(low, 0.0, act[0]), act[1], act[2], jnp.where(low, act[3], 0.0)]
    marks = jnp.concatenate(inner + [jnp.zeros((4, LANES), F32)], 0)
    r = lax.broadcasted_iota(jnp.int32, (LANES, LANES), 0)
    c = lax.broadcasted_iota(jnp.int32, (LANES, LANES), 1)
    tri = jnp.where(r <= c, 1.0, 0.0).astype(BF16)
    counts = dot(marks.astype(BF16), jnp.concatenate([tri, jnp.ones((LANES, LANES), BF16)], 1))
    where = lax.broadcasted_iota(jnp.int32, (2 * BLOCK, LANES), 0).astype(F32)
    offset = jnp.full((1, LANES), -1.0, F32)
    for b, lanes in enumerate(tiles):
        place = jnp.where(inner[b] > 0.5, counts[b:b + 1, :LANES] + offset, -1.0)
        ones_ref[:, lanes] = jnp.where(where == place, 1.0, 0.0).astype(BF16)
        offset = offset + counts[b:b + 1, LANES:]

    loads[4].wait()
    loads[5].wait()

    def ordered(x):
        return jnp.concatenate(
            [x[LEV:2 * LEV] - 0.3 * x[0:LEV], x[2 * LEV:3 * LEV], x[0:LEV], x[3 * LEV:4 * LEV]], 0)

    hi, lo = halves(ordered(xs[...]))
    hi_ref[0:288, :] = hi
    lo_ref[0:288, :] = lo
    hi, lo = halves(su[...])
    hi_ref[288:384, :] = hi
    lo_ref[288:384, :] = lo
    for load in small[2:]:
        load.wait()
    pl.when(jnp.logical_and(e > 1, e < n_elem - 1))(exchange)

    def gather(ref, rows):
        return dot_t(ref[rows, :], ones_ref[...])

    def first_maps(ref, hi, lo):
        x = dot(maps_ref[...], jnp.concatenate([hi, hi, lo], 0))
        ref[0:64, :] = x[:64]
        ref[64:128, :] = x[64:128] + 0.5
        ref[128:208, :] = x[128:]

    def more_maps(ref, hi, lo):
        ref[208:368, :] = dot(more_ref[...], jnp.concatenate([hi, hi, lo], 0))

    def to_next():
        for c in range(2):
            end_copy(c, 1).wait_recv()
        sent[0].start()
        sent[1].start()

    def to_previous():
        enter()
        sent[2].start()
        sent[3].start()

    meanwhile = ({24: lambda: pl.when(e == 1)(exchange)}, {8: lambda: pl.when(first_e)(to_next)})
    main = slice(0, STATE_ROWS)
    hi, lo = gather(hi_ref, main).astype(BF16), gather(lo_ref, main).astype(BF16)
    first_maps(prof, hi[:HALF], lo[:HALF])
    more_maps(prof, hi, lo)
    found = gather(hi_ref, slice(288, 384)) + gather(lo_ref, slice(288, 384))
    for i in range(2):
        lanes = tiles[i]
        sur[...] = found[:, lanes]
        tend = cloud(Whole, consts, prepare(Whole, sur), prof, lanes, tail_ref, lev_ref, part, diag, meanwhile[i])
        hi, lo = halves(jnp.concatenate([tend, diag[...]], 0))
        both_hi[:, lanes] = hi
        both_lo[:, lanes] = lo

    pl.when(first_e)(to_previous)

    def passive(x, s2):
        hi, lo = halves(x)
        slow = dot(passive_ref[...], jnp.concatenate([hi, hi, lo], 0))
        mean2 = jnp.sum(s2, axis=0, keepdims=True)
        return jnp.concatenate([slow[:LEV] + drift_ref[...] * mean2, slow[LEV:]], 0)

    for b, lanes in enumerate(tiles):
        x = xs[HALF:, lanes]
        out_ref[HALF:, lanes] = x + jnp.where(act[b] > 0.5, passive(x, su[2 * CX:, lanes]), 0.0)
    back = dot(both_hi[...], ones_ref[...]) + dot(both_lo[...], ones_ref[...])
    out_ref[0:HALF, :] = xs[0:HALF, :] + back[0:HALF]
    diag_out_ref[...] = back[HALF:]

    def edge(form, own_mass, on, wait, other_mass, arrived):
        prep = prepare(form, sur)
        wait(0)
        masses = other_mass()
        scale = 1.0 / (own_mass + masses)
        share, rest = own_mass * scale, masses * scale
        start = own_ref[0:HALF, :] * share + arrived(8) * rest
        hi, lo = halves(start)
        first_maps(edge_prof, hi, lo)
        keep = []

        def late():
            wait(1)
            final = own_ref[HALF:, :] * share + arrived(80) * rest
            keep.append(final)
            more_hi, more_lo = halves(final[:80])
            more_maps(edge_prof, jnp.concatenate([hi, more_hi], 0), jnp.concatenate([lo, more_lo], 0))

        tend = cloud(form, consts, prep, edge_prof, tiles[0], tail_ref, lev_ref, part, diag, {24: late})
        py, p2, p0, p3 = start[:LEV], start[LEV:], keep[0][:LEV], keep[0][LEV:]
        slow = passive(jnp.concatenate([p2, p3], 0), sur[2 * CX:, :])
        shared = jnp.concatenate([p0, py + 0.3 * p0, p2, p3], 0)
        return shared + jnp.where(on, jnp.concatenate([tend, slow], 0), 0.0), jnp.where(on, diag[...], 0.0)

    def one_end(k, _):
        i, got = k, 1 - k
        lanes = pl.ds(pl.multiple_of((1 - i) * (3 * LANES), LANES), LANES)
        side = low == (i == 1)

        def double(x):
            return jnp.where(side, x, swap(x))

        def arrived(row):
            x = recv[got, row:row + LEV, :]
            y = swap(x)
            return jnp.concatenate([jnp.where(low, x, y), jnp.where(low, y, x)], 0)

        sur[...] = double(su[:, lanes])
        own_ref[...] = ordered(double(xs[:, lanes]))
        new, seen = edge(
            Half, double(mass_ref[:, lanes]), jnp.where(side, active_ref[:, lanes], 0) == 1,
            lambda c: pl.when(jnp.logical_not(jnp.logical_and(first_e, got == 1)))(end_copy(c, got).wait_recv),
            lambda: recv[got, 0:1, :], arrived)
        out_ref[:, lanes] = jnp.where(side, new, out_ref[:, lanes])
        diag_out_ref[:, lanes] = jnp.where(side, seen, diag_out_ref[:, lanes])
        return 0

    def both_ends():
        t0, t3 = tiles[0], tiles[3]

        def merge(ref):
            return jnp.where(low, ref[:, t0], ref[:, t3])

        def wait(c):
            for got in range(2):
                end_copy(c, got).wait_recv()

        def arrived(row):
            x, y = recv[0, row:row + LEV, :], recv[1, row:row + LEV, :]
            return jnp.concatenate([jnp.where(low, x, swap(y)), jnp.where(low, swap(x), y)], 0)

        sur[...] = merge(su)
        own_ref[...] = ordered(merge(xs))
        new, seen = edge(
            Whole, merge(mass_ref), merge(active_ref) == 1, wait,
            lambda: jnp.where(low, recv[0, 0:1, :], recv[1, 0:1, :]), arrived)
        out_ref[:, t0] = jnp.where(low, new, out_ref[:, t0])
        out_ref[:, t3] = jnp.where(low, out_ref[:, t3], new)
        diag_out_ref[:, t0] = jnp.where(low, seen, diag_out_ref[:, t0])
        diag_out_ref[:, t3] = jnp.where(low, diag_out_ref[:, t3], seen)

    alone = e <= 1

    @pl.when(alone)
    def _():
        lax.fori_loop(0, 2, one_end, 0)

    pl.when(jnp.logical_not(alone))(both_ends)

    for copy in sent:
        copy.wait_send()


def write(state_ref, diag_ref, state_out, diag_out, sem):
    copies = [pltpu.make_async_copy(state_ref, state_out, sem.at[0]),
              pltpu.make_async_copy(diag_ref, diag_out, sem.at[1])]
    for copy in copies:
        copy.start()
    for copy in copies:
        copy.wait()


def body(n_elem, state, surface, mass, plan, active):
    cols = state.shape[2]
    maps, more, tail, passive, drift, levels, consts = tables()
    hbm = pl.BlockSpec(memory_space=pltpu.HBM)
    vmem = pl.BlockSpec(memory_space=pltpu.VMEM)
    state, surface, mass, active, maps, more, tail, passive, drift, levels = [
        pltpu.with_memory_space_constraint(x, pltpu.HBM) for x in (
            state.reshape(4 * LEV, cols), surface.reshape(3 * CX, cols), mass.reshape(1, cols),
            active.reshape(1, cols), *map(jnp.asarray, (maps, more, tail, passive, drift, levels)))]
    new_state, diag = pl.pallas_call(
        functools.partial(kernel, consts, n_elem),
        out_shape=(pltpu.VMEM((4 * LEV, cols), F32), pltpu.VMEM((3 * CX, cols), F32)),
        in_specs=[hbm] * 10,
        out_specs=(vmem, vmem),
        scratch_shapes=[
            pltpu.VMEM((4 * LEV, cols), F32),
            pltpu.VMEM((384, cols), BF16),
            pltpu.VMEM((384, cols), BF16),
            pltpu.VMEM((3 * CX, cols), F32),
            pltpu.VMEM((2 * BLOCK, cols), BF16),
            pltpu.VMEM((2, HALF + 8, LANES), F32),
            pltpu.VMEM((2, HALF + 8, LANES), F32),
            pltpu.VMEM((3 * CX, BLOCK), F32),
            pltpu.VMEM((368, 2 * BLOCK), F32),
            pltpu.VMEM((368, BLOCK), F32),
            pltpu.VMEM((ZP * 8, BLOCK), F32),
            pltpu.VMEM((3 * CX, BLOCK), F32),
            pltpu.VMEM((HALF + 3 * CX, 2 * BLOCK), BF16),
            pltpu.VMEM((HALF + 3 * CX, 2 * BLOCK), BF16),
            pltpu.VMEM((4 * LEV, LANES), F32),
            pltpu.VMEM((1, cols), F32),
            pltpu.VMEM((1, cols), jnp.int32),
            pltpu.VMEM(maps.shape, BF16),
            pltpu.VMEM(more.shape, BF16),
            pltpu.VMEM(tail.shape, BF16),
            pltpu.VMEM(passive.shape, BF16),
            pltpu.VMEM(drift.shape, F32),
            pltpu.VMEM(levels.shape, F32),
            pltpu.SemaphoreType.DMA((14,)),
            pltpu.SemaphoreType.DMA((4,)),
            pltpu.SemaphoreType.DMA((4,)),
        ],
        compiler_params=pltpu.CompilerParams(
            collective_id=0, has_side_effects=True, vmem_limit_bytes=32 * 1024 * 1024),
    )(
        state, surface, mass, active, maps, more, tail, passive, drift, levels,
    )
    new_state, diag = pl.pallas_call(
        write,
        out_shape=(jax.ShapeDtypeStruct(new_state.shape, F32), jax.ShapeDtypeStruct(diag.shape, F32)),
        in_specs=[vmem, vmem],
        out_specs=(hbm, hbm),
        scratch_shapes=[pltpu.SemaphoreType.DMA((2,))],
    )(pltpu.with_memory_space_constraint(new_state, pltpu.VMEM), pltpu.with_memory_space_constraint(diag, pltpu.VMEM))
    return new_state.reshape(4, LEV, cols), diag.reshape(3, CX, cols)


def solution(mesh):
    both = ("elem", "grp")
    return jax.shard_map(
        functools.partial(body, mesh.shape["elem"]),
        mesh=mesh,
        in_specs=(P(None, None, both), P(None, None, both), P(both), P(None, both), P(both)),
        out_specs=(P(None, None, both), P(None, None, both)),
        check_vma=False,
    )
```

```python
import functools
import math

import jax
import jax.numpy as jnp
import ml_dtypes
import numpy as np
from jax import lax
from jax.experimental import pallas as pl
from jax.experimental.pallas import tpu as pltpu
from jax.sharding import PartitionSpec as P

LEV = 72
CZ = 58
CX = 32
EDGE = 64
LANES = 128
BLOCK = 128
ZP = 64
HALF = 2 * LEV
STATE_ROWS = 240
F32 = jnp.float32
BF16 = jnp.bfloat16
MESH = pl.DeviceIdType.MESH


def split_np(matrix):
    high = matrix.astype(np.float32).astype(ml_dtypes.bfloat16)
    low = (matrix - high.astype(np.float64)).astype(np.float32).astype(ml_dtypes.bfloat16)
    return high, low


def tables():
    z = np.arange(CZ, dtype=np.float64)
    lev = np.arange(LEV, dtype=np.float64)
    up = np.maximum(0.0, 1.0 - np.abs(z[:, None] * ((LEV - 1) / (CZ - 1)) - lev[None, :]))
    down = np.maximum(0.0, 1.0 - np.abs(lev[:, None] * ((CZ - 1) / (LEV - 1)) - z[None, :]))
    fall = 1.0 - 0.5 * z / (CZ - 1)
    k = 0.1 + 0.2 * z / (CZ - 1)
    mix = np.zeros((CZ, CZ))
    for i in range(CZ):
        mix[i, i] += 1.0 - 2.0 * k[i]
        mix[i, min(i + 1, CZ - 1)] += k[i]
        mix[i, max(i - 1, 0)] += k[i]
    kap = mix.sum(0)
    c1 = mix @ fall
    c2 = -0.1 * (mix @ (fall * fall))
    kb = mix @ up
    qb = -0.1 * (mix @ (fall[:, None] * up))

    m = np.zeros((208, 80))
    m[0:CZ, :LEV] = kb / 0.62
    m[64:64 + CZ, :LEV] = -0.25 * kb
    m[128:128 + CZ, :LEV] = qb
    m[192, :LEV] = (kap * c1) @ (-0.25 * kb)
    m[193, :LEV] = (kap * c2) @ (-0.25 * kb)
    m[194, :LEV] = (kap * c1) @ qb
    m[195, :LEV] = (kap * c2) @ qb
    m[196, :LEV] = kap @ qb
    hi, lo = split_np(m)
    maps = np.concatenate([hi, lo, hi], 1)
    dkk = down @ mix @ kb
    py, p0 = slice(0, 72), slice(80, 152)
    m = np.zeros((160, 160))
    m[0:72, p0] = dkk - down @ up
    m[0:72, py] = 0.8 * dkk / 1.24
    m[72:144, p0] = 0.3 * (dkk - down @ up)
    m[72:144, py] = 0.24 * dkk / 1.24 - down @ up
    m[144, p0] = 1.24 * (kap @ kb)
    m[144, py] = 0.8 * (kap @ kb)
    m[145, p0] = up.sum(0)
    hi, lo = split_np(m)
    more = np.concatenate([hi, lo, hi], 1)

    t = np.zeros((2 * HALF, ZP))
    t[0:72, 0:CZ] = down @ mix / 1.24
    t[72:144, 0:CZ] = 0.3 * (down @ mix) / 1.24
    t[144:216, 0:CZ] = -0.8 * down / 1.24
    t[216:288, 0:CZ] = down / 1.24
    hi, lo = split_np(t)
    tail = np.concatenate([hi, lo, hi], 1)

    e = np.zeros((HALF, HALF))
    e[0:72, 0:72] = down @ (mix @ kb - up)
    e[72:144, 72:144] = e[0:72, 0:72]
    hi, lo = split_np(e)
    passive = np.concatenate([hi, lo, hi], 1)
    drift = np.repeat(((down @ (mix @ (mix @ fall))) / CX)[:, None], LANES, 1).astype(np.float32)

    rows = np.zeros((3, ZP))
    rows[0, :CZ] = c1
    rows[1, :CZ] = c2
    rows[2, :CZ] = kap
    levels = np.repeat(rows.reshape(-1)[:, None], LANES, 1).astype(np.float32)
    consts = dict(
        c1=[float(a) for a in c1], c2=[float(a) for a in c2],
        stay=[float(a) for a in 0.248 * (1.0 - 2.0 * k)], move=[float(a) for a in 0.248 * k],
        s11=float((kap * c1 * c1).sum()), s12=float((kap * c1 * c2).sum()), s22=float((kap * c2 * c2).sum()),
        sc1=float((kap * c1).sum()), sc2=float((kap * c2).sum()))
    return maps, more, tail, passive, drift, levels, consts


def halves(x):
    high = x.astype(BF16)
    return high, (x - high.astype(F32)).astype(BF16)


def dot(a, b):
    return lax.dot_general(a, b, (((1,), (0,)), ((), ())), preferred_element_type=F32)


def dot_t(a, b):
    return lax.dot_general(a, b, (((1,), (1,)), ((), ())), preferred_element_type=F32)


class Whole:
    @staticmethod
    def rows(ref, j):
        return jnp.stack([ref[pl.ds(CX * j + v, 8, stride=4), :] for v in range(4)], 0)

    @staticmethod
    def east(f):
        return jnp.concatenate([f[1:], pltpu.roll(f[0], 7, 0)[None]], 0)

    @staticmethod
    def west(f):
        return jnp.concatenate([pltpu.roll(f[3], 1, 0)[None], f[:3]], 0)

    @staticmethod
    def fold(f):
        return (f[0] + f[1]) + (f[2] + f[3])

    @staticmethod
    def join(f):
        return f

    @staticmethod
    def store(ref, i, f):
        for v in range(4):
            ref[pl.ds(CX * i + v, 8, stride=4), :] = f[v]


class Half:
    @staticmethod
    def rows(ref, j):
        low = lax.broadcasted_iota(jnp.int32, (1, LANES), 1) < EDGE
        return jnp.stack([
            jnp.where(low, ref[pl.ds(CX * j + v, 8, stride=2), :], ref[pl.ds(CX * j + 16 + v, 8, stride=2), :])
            for v in range(2)], 0)

    @staticmethod
    def east(f):
        near = pltpu.roll(f[0], 7, 0)
        edge = lax.broadcasted_iota(jnp.int32, (8, LANES), 0) == 7
        return jnp.stack([f[1], jnp.where(edge, swap(near), near)], 0)

    @staticmethod
    def west(f):
        near = pltpu.roll(f[1], 1, 0)
        edge = lax.broadcasted_iota(jnp.int32, (8, LANES), 0) == 0
        return jnp.stack([jnp.where(edge, swap(near), near), f[0]], 0)

    @staticmethod
    def fold(f):
        return f[0] + f[1]

    @staticmethod
    def join(f):
        return f + swap(f)

    @staticmethod
    def store(ref, i, f):
        low = lax.broadcasted_iota(jnp.int32, (1, LANES), 1) < EDGE
        for v in range(2):
            other = swap(f[v])
            ref[pl.ds(CX * i + v, 8, stride=2), :] = jnp.where(low, f[v], other)
            ref[pl.ds(CX * i + 16 + v, 8, stride=2), :] = jnp.where(low, other, f[v])


def swap(x):
    return pltpu.roll(x, EDGE, 1)


def prepare(form, sur_ref):
    east, west = form.east, form.west
    r0, r1, s2 = form.rows(sur_ref, 0), form.rows(sur_ref, 1), form.rows(sur_ref, 2)
    sy, sw = (r1 - 0.3 * r0) * (1.0 / 0.62), r0 + 0.8 * r1

    def xsum(f):
        return form.join(jnp.sum(form.fold(f), axis=0, keepdims=True))

    def parts(s):
        e, w = east(s), west(s)
        return 0.6 * s + 0.2 * (e + w), e - w

    ay, dy = parts(sy)
    a2, d2 = parts(s2)
    af, df = -0.25 * a2, -0.25 * d2
    aw, dw = parts(sw)
    ew, ef = s2 * dw, s2 * df
    haw, hdw, hew = east(aw) - west(aw), east(dw) - west(dw), east(ew) - west(ew)
    gram = (xsum(af * haw), xsum(af * hdw + df * haw), xsum(af * hew + ef * haw),
            xsum(df * hdw), xsum(df * hew + ef * hdw), xsum(ef * hew))
    means = (xsum(sw) * (1.0 / CX), xsum(ew) * (1.0 / CX))
    return s2, ay, dy, af, df, aw, dw, ef, haw, hdw, hew, gram, means


def cloud(form, consts, prep, prof_ref, lanes, tail_ref, lev_ref, part_ref, diag_ref, at={}):
    s2, ay, dy, af, df, aw, dw, ef, haw, hdw, hew, gram, means = prep
    east, west = form.east, form.west

    def level(start, z):
        return prof_ref[start + z:start + z + 1, lanes][None]

    def horizontal(z):
        turn = level(128, z) + consts["c2"][z] * s2
        y = (level(0, z) + consts["c1"][z] * ay) + turn * dy
        pull = (level(64, z) + consts["c1"][z] * af) + turn * df
        one = jnp.log(1.0 + jnp.exp2(y * (0.62 * math.log2(math.e))))
        y = y - one
        e, w = east(y), west(y)
        return (1.5 * y + w) + pull * (e - w), one

    def vertical(z, h, above, below):
        v = consts["stay"][z] * h + consts["move"][z] * (above + below)
        two = jnp.maximum(jnp.log(1.0 + jnp.exp(jnp.minimum(v, 80.0))), v)
        part_ref[8 * z:8 * z + 8, :] = form.fold(v) - 0.62 * form.fold(two)
        return v, two

    h, rain = horizontal(0)
    below = h
    total_v = total_2 = None
    def passive_sums():
        pf = prof_ref[64:128, lanes] - 0.5
        q = prof_ref[128:192, lanes]
        s1p, s2p, s1q, sq2, sq = [prof_ref[192 + i:193 + i, lanes] for i in range(5)]
        c1 = lev_ref[0:ZP, :]
        c2 = lev_ref[ZP:2 * ZP, :]
        kap = lev_ref[2 * ZP:3 * ZP, :]
        g11, g12, g13, g22, g23, g33 = gram
        bend = c1 * (c1 * g11 + q * g12 + c2 * g13) + q * (q * g22 + c2 * g23) + (c2 * c2) * g33
        mean_w = c1 * means[0] + c2 * means[1] + (0.4 / CX) * bend
        hi, lo = halves(mean_w)
        prof_ref[208:352, lanes] += dot(tail_ref[0:HALF, :], jnp.concatenate([hi, hi, lo], 0))
        qk = q * kap
        sqp = jnp.sum(qk * pf, axis=0, keepdims=True)
        sqq = jnp.sum(qk * q, axis=0, keepdims=True)
        s11, s12, s22 = consts["s11"], consts["s12"], consts["s22"]
        w1 = (prof_ref[352:353, lanes] + consts["sc1"] * aw) + (sq * dw + consts["sc2"] * (s2 * dw))
        return (
            (0.6 * w1 + 0.2 * (east(w1) + west(w1)))
            + 0.4 * (
                haw * ((s1p + s11 * af) + (s1q * df + s12 * ef))
                + hdw * ((sqp + s1q * af) + (sqq * df + sq2 * ef))
                + hew * ((s2p + s12 * af) + (sq2 * df + s22 * ef))
            )
        )

    for z in range(CZ):
        if z in at:
            at[z]()
        if z == 26:
            sum_w = passive_sums()
            form.store(diag_ref, 1, 0.3 * sum_w)
            form.store(diag_ref, 2, sum_w - 1.24 * prof_ref[353:354, lanes])
        if z + 1 < CZ:
            above, one = horizontal(z + 1)
            rain = rain + one
        else:
            above = h
        v, two = vertical(z, h, above, below)
        total_v = v if z == 0 else total_v + v
        total_2 = two if z == 0 else total_2 + two
        h, below = above, h
    mean_y = part_ref[pl.ds(0, CZ, stride=8), :]
    for s in range(1, 8):
        mean_y = mean_y + part_ref[pl.ds(s, CZ, stride=8), :]
    mean_y = form.join(mean_y) * (1.0 / CX)
    hi, lo = halves(jnp.concatenate([mean_y, jnp.zeros((ZP - CZ, LANES), F32)], 0))
    tend = prof_ref[208:352, lanes] + dot(tail_ref[HALF:, :], jnp.concatenate([hi, hi, lo], 0))
    sum_y = total_v - 0.62 * total_2
    form.store(diag_ref, 0, 0.5 * (rain + total_2))
    form.store(part_ref, 0, sum_y)
    scale = 1.0 / (1.24 * CZ)
    sums = part_ref[0:CX, :]
    diag_ref[CX:2 * CX, :] = (diag_ref[CX:2 * CX, :] + sums) * scale
    diag_ref[2 * CX:, :] = (diag_ref[2 * CX:, :] - 0.8 * sums) * scale
    return tend


def first_maps(maps_ref, ref, hi, lo):
    ref[0:64, :] = dot(maps_ref[0:64, :], jnp.concatenate([hi[:80], hi[:80], lo[:80]], 0))
    x = dot(maps_ref[64:208, :], jnp.concatenate([hi[80:160], hi[80:160], lo[80:160]], 0))
    ref[64:128, :] = x[:64] + 0.5
    ref[128:208, :] = x[64:]


def more_maps(more_ref, ref, hi, lo):
    ref[208:368, :] = dot(more_ref[...], jnp.concatenate([hi, hi, lo], 0))


SENT = ((0, 80), (80, 72))


def kernel(consts, n_elem, state_ref, surface_ref, mass_hbm, active_hbm, maps_hbm, more_hbm, tail_hbm, passive_hbm,
           drift_hbm, lev_hbm, out_ref, diag_out_ref,
           xs, hi_ref, lo_ref, su, ones_ref, send, recv, sur, prof, edge_prof, part, diag, both_hi, both_lo, own_ref,
           mass_ref, active_ref, maps_ref, more_ref, tail_ref, passive_ref, drift_ref, lev_ref,
           in_sem, send_sem, recv_sem):
    e, g = lax.axis_index("elem"), lax.axis_index("grp")
    after = lax.rem(e + 1, n_elem)
    before = lax.rem(e + n_elem - 1, n_elem)
    barrier = pltpu.get_barrier_semaphore()
    for other in (before, after):
        pl.semaphore_signal(barrier, inc=1, device_id=(other, g), device_id_type=MESH)

    tiles = [slice(LANES * b, LANES * (b + 1)) for b in range(4)]
    ends = (tiles[3], tiles[0])
    loads = [
        pltpu.make_async_copy(state_ref.at[rows, lanes], xs.at[rows, lanes], in_sem.at[k])
        for k, (rows, lanes) in enumerate(
            (rows, lanes) for rows in (slice(0, 3 * LEV), slice(3 * LEV, 4 * LEV)) for lanes in ends)
    ] + [
        pltpu.make_async_copy(state_ref.at[:, pl.ds(LANES, 2 * LANES)], xs.at[:, pl.ds(LANES, 2 * LANES)], in_sem.at[4]),
        pltpu.make_async_copy(surface_ref, su, in_sem.at[5]),
    ]
    small = [
        pltpu.make_async_copy(a, b, in_sem.at[6 + i])
        for i, (a, b) in enumerate((
            (mass_hbm, mass_ref), (active_hbm, active_ref), (maps_hbm, maps_ref), (lev_hbm, lev_ref),
            (more_hbm, more_ref), (tail_hbm, tail_ref), (passive_hbm, passive_ref), (drift_hbm, drift_ref)))
    ]
    for load in small[:1] + loads[:4] + small[1:2] + loads[4:] + small[2:]:
        load.start()

    low = lax.broadcasted_iota(jnp.int32, (1, LANES), 1) < EDGE

    def end_copy(c, i):
        rows = pl.ds(*SENT[c])
        return pltpu.make_async_remote_copy(
            src_ref=send.at[i, rows], dst_ref=recv.at[i, rows],
            send_sem=send_sem.at[2 * c + i], recv_sem=recv_sem.at[2 * c + i],
            device_id=((after, before)[i] if isinstance(i, int) else after, g), device_id_type=MESH)

    sent = [end_copy(c, i) for i in range(2) for c in range(2)]

    def enter():
        pl.semaphore_wait(barrier, 2)

    def exchange():
        enter()
        for copy in sent:
            copy.start()

    first_e, last_e = e == 0, e == n_elem - 1
    pl.when(last_e)(enter)
    small[0].wait()
    for i, lanes in enumerate(ends):
        mass = mass_ref[:, lanes]
        mass = jnp.where(low, swap(mass), mass) if i == 0 else jnp.where(low, mass, swap(mass))
        send[i, 0:8, :] = jnp.broadcast_to(mass, (8, LANES))
        loads[i].wait()
        p0 = xs[0:LEV, lanes]
        py, p2 = xs[LEV:2 * LEV, lanes] - 0.3 * p0, xs[2 * LEV:3 * LEV, lanes]
        send[i, 8:80, :] = jnp.where(low, swap(py), p2) if i == 0 else jnp.where(low, py, swap(p2))
        pl.when(last_e)(sent[2 * i].start)
        loads[2 + i].wait()
        p0, p3 = xs[0:LEV, lanes], xs[3 * LEV:, lanes]
        send[i, 80:152, :] = jnp.where(low, swap(p0), p3) if i == 0 else jnp.where(low, p0, swap(p3))
        pl.when(last_e)(sent[2 * i + 1].start)

    small[1].wait()
    act = [active_ref[:, lanes].astype(F32) for lanes in tiles]
    inner = [jnp.where(low, 0.0, act[0]), act[1], act[2], jnp.where(low, act[3], 0.0)]
    marks = jnp.concatenate(inner + [jnp.zeros((4, LANES), F32)], 0)
    r = lax.broadcasted_iota(jnp.int32, (LANES, LANES), 0)
    c = lax.broadcasted_iota(jnp.int32, (LANES, LANES), 1)
    tri = jnp.where(r <= c, 1.0, 0.0).astype(BF16)
    counts = dot(marks.astype(BF16), jnp.concatenate([tri, jnp.ones((LANES, LANES), BF16)], 1))
    where = lax.broadcasted_iota(jnp.int32, (2 * BLOCK, LANES), 0).astype(F32)
    offset = jnp.full((1, LANES), -1.0, F32)
    for b, lanes in enumerate(tiles):
        place = jnp.where(inner[b] > 0.5, counts[b:b + 1, :LANES] + offset, -1.0)
        ones_ref[:, lanes] = jnp.where(where == place, 1.0, 0.0).astype(BF16)
        offset = offset + counts[b:b + 1, LANES:]

    loads[4].wait()
    loads[5].wait()

    def ordered(x):
        pad = jnp.zeros((8, x.shape[1]), F32)
        return jnp.concatenate(
            [x[LEV:2 * LEV] - 0.3 * x[0:LEV], pad, x[2 * LEV:3 * LEV], pad, x[0:LEV], x[3 * LEV:4 * LEV]], 0)

    hi, lo = halves(ordered(xs[...]))
    hi_ref[0:304, :] = hi
    lo_ref[0:304, :] = lo
    hi, lo = halves(su[...])
    hi_ref[304:400, :] = hi
    lo_ref[304:400, :] = lo
    for load in small[2:]:
        load.wait()
    pl.when(jnp.logical_and(e > 1, e < n_elem - 1))(exchange)

    def gather(ref, rows):
        return dot_t(ref[rows, :], ones_ref[...])

    def to_next():
        for c in range(2):
            end_copy(c, 1).wait_recv()
        sent[0].start()
        sent[1].start()

    def to_previous():
        enter()
        sent[2].start()
        sent[3].start()

    meanwhile = ({24: lambda: pl.when(e == 1)(exchange)}, {8: lambda: pl.when(first_e)(to_next)})
    main = slice(0, STATE_ROWS)
    hi, lo = gather(hi_ref, main).astype(BF16), gather(lo_ref, main).astype(BF16)
    first_maps(maps_ref, prof, hi, lo)
    more_maps(more_ref, prof, jnp.concatenate([hi[:80], hi[160:]], 0), jnp.concatenate([lo[:80], lo[160:]], 0))
    found = gather(hi_ref, slice(304, 400)) + gather(lo_ref, slice(304, 400))
    for i in range(2):
        lanes = tiles[i]
        sur[...] = found[:, lanes]
        tend = cloud(Whole, consts, prepare(Whole, sur), prof, lanes, tail_ref, lev_ref, part, diag, meanwhile[i])
        hi, lo = halves(jnp.concatenate([tend, diag[...]], 0))
        both_hi[:, lanes] = hi
        both_lo[:, lanes] = lo

    pl.when(first_e)(to_previous)

    def passive(x, s2):
        hi, lo = halves(x)
        slow = dot(passive_ref[...], jnp.concatenate([hi, hi, lo], 0))
        mean2 = jnp.sum(s2, axis=0, keepdims=True)
        return jnp.concatenate([slow[:LEV] + drift_ref[...] * mean2, slow[LEV:]], 0)

    for b, lanes in enumerate(tiles):
        x = xs[HALF:, lanes]
        out_ref[HALF:, lanes] = x + jnp.where(act[b] > 0.5, passive(x, su[2 * CX:, lanes]), 0.0)
    back = dot(both_hi[...], ones_ref[...]) + dot(both_lo[...], ones_ref[...])
    out_ref[0:HALF, :] = xs[0:HALF, :] + back[0:HALF]
    diag_out_ref[...] = back[HALF:]

    def edge(form, own_mass, on, wait, other_mass, arrived, emit):
        prep = prepare(form, sur)
        wait(0)
        masses = other_mass()
        scale = 1.0 / (own_mass + masses)
        share, rest = own_mass * scale, masses * scale
        pad = jnp.zeros((8, LANES), F32)
        py, p2 = arrived(8)
        start = own_ref[0:160, :] * share + jnp.concatenate([py, pad, p2, pad], 0) * rest
        hi, lo = halves(start)
        first_maps(maps_ref, edge_prof, hi, lo)
        both_p = []

        def late():
            wait(1)
            final = own_ref[160:, :] * share + jnp.concatenate(arrived(80), 0) * rest
            more_hi, more_lo = halves(final[:80])
            more_maps(more_ref, edge_prof, jnp.concatenate([hi[:80], more_hi], 0),
                      jnp.concatenate([lo[:80], more_lo], 0))
            p0, p2, p3 = final[:LEV], start[80:152], final[LEV:]
            both_p.append(jnp.concatenate([p0, start[:LEV] + 0.3 * p0], 0))
            x = jnp.concatenate([p2, p3], 0)
            emit(slice(HALF, 2 * HALF), x + jnp.where(on, passive(x, sur[2 * CX:, :]), 0.0))

        tend = cloud(form, consts, prep, edge_prof, tiles[0], tail_ref, lev_ref, part, diag, {24: late})
        emit(slice(0, HALF), both_p[0] + jnp.where(on, tend, 0.0))
        return jnp.where(on, diag[...], 0.0)

    def one_end(k, _):
        i, got = k, 1 - k
        lanes = pl.ds(pl.multiple_of((1 - i) * (3 * LANES), LANES), LANES)
        side = low == (i == 1)

        def double(x):
            return jnp.where(side, x, swap(x))

        def arrived(row):
            x = recv[got, row:row + LEV, :]
            y = swap(x)
            return jnp.where(low, x, y), jnp.where(low, y, x)

        def emit(rows, new):
            out_ref[rows, lanes] = jnp.where(side, new, out_ref[rows, lanes])

        sur[...] = double(su[:, lanes])
        own_ref[...] = ordered(double(xs[:, lanes]))
        seen = edge(
            Half, double(mass_ref[:, lanes]), jnp.where(side, active_ref[:, lanes], 0) == 1,
            lambda c: pl.when(jnp.logical_not(jnp.logical_and(first_e, got == 1)))(end_copy(c, got).wait_recv),
            lambda: recv[got, 0:1, :], arrived, emit)
        diag_out_ref[:, lanes] = jnp.where(side, seen, diag_out_ref[:, lanes])
        return 0

    def both_ends():
        t0, t3 = tiles[0], tiles[3]

        def merge(ref):
            return jnp.where(low, ref[:, t0], ref[:, t3])

        def wait(c):
            for got in range(2):
                end_copy(c, got).wait_recv()

        def arrived(row):
            x, y = recv[0, row:row + LEV, :], recv[1, row:row + LEV, :]
            return jnp.where(low, x, swap(y)), jnp.where(low, swap(x), y)

        def emit(rows, new):
            out_ref[rows, t0] = jnp.where(low, new, out_ref[rows, t0])
            out_ref[rows, t3] = jnp.where(low, out_ref[rows, t3], new)

        sur[...] = merge(su)
        own_ref[...] = ordered(merge(xs))
        seen = edge(
            Whole, merge(mass_ref), merge(active_ref) == 1, wait,
            lambda: jnp.where(low, recv[0, 0:1, :], recv[1, 0:1, :]), arrived, emit)
        diag_out_ref[:, t0] = jnp.where(low, seen, diag_out_ref[:, t0])
        diag_out_ref[:, t3] = jnp.where(low, diag_out_ref[:, t3], seen)

    alone = e <= 1

    @pl.when(alone)
    def _():
        lax.fori_loop(0, 2, one_end, 0)

    pl.when(jnp.logical_not(alone))(both_ends)

    for copy in sent:
        copy.wait_send()


def write(state_ref, diag_ref, state_out, diag_out, sem):
    copies = [pltpu.make_async_copy(state_ref, state_out, sem.at[0]),
              pltpu.make_async_copy(diag_ref, diag_out, sem.at[1])]
    for copy in copies:
        copy.start()
    for copy in copies:
        copy.wait()


def body(n_elem, state, surface, mass, plan, active):
    cols = state.shape[2]
    maps, more, tail, passive, drift, levels, consts = tables()
    hbm = pl.BlockSpec(memory_space=pltpu.HBM)
    vmem = pl.BlockSpec(memory_space=pltpu.VMEM)
    state, surface, mass, active, maps, more, tail, passive, drift, levels = [
        pltpu.with_memory_space_constraint(x, pltpu.HBM) for x in (
            state.reshape(4 * LEV, cols), surface.reshape(3 * CX, cols), mass.reshape(1, cols),
            active.reshape(1, cols), *map(jnp.asarray, (maps, more, tail, passive, drift, levels)))]
    new_state, diag = pl.pallas_call(
        functools.partial(kernel, consts, n_elem),
        out_shape=(pltpu.VMEM((4 * LEV, cols), F32), pltpu.VMEM((3 * CX, cols), F32)),
        in_specs=[hbm] * 10,
        out_specs=(vmem, vmem),
        scratch_shapes=[
            pltpu.VMEM((4 * LEV, cols), F32),
            pltpu.VMEM((400, cols), BF16),
            pltpu.VMEM((400, cols), BF16),
            pltpu.VMEM((3 * CX, cols), F32),
            pltpu.VMEM((2 * BLOCK, cols), BF16),
            pltpu.VMEM((2, HALF + 8, LANES), F32),
            pltpu.VMEM((2, HALF + 8, LANES), F32),
            pltpu.VMEM((3 * CX, BLOCK), F32),
            pltpu.VMEM((368, 2 * BLOCK), F32),
            pltpu.VMEM((368, BLOCK), F32),
            pltpu.VMEM((ZP * 8, BLOCK), F32),
            pltpu.VMEM((3 * CX, BLOCK), F32),
            pltpu.VMEM((HALF + 3 * CX, 2 * BLOCK), BF16),
            pltpu.VMEM((HALF + 3 * CX, 2 * BLOCK), BF16),
            pltpu.VMEM((4 * LEV + 16, LANES), F32),
            pltpu.VMEM((1, cols), F32),
            pltpu.VMEM((1, cols), jnp.int32),
            pltpu.VMEM(maps.shape, BF16),
            pltpu.VMEM(more.shape, BF16),
            pltpu.VMEM(tail.shape, BF16),
            pltpu.VMEM(passive.shape, BF16),
            pltpu.VMEM(drift.shape, F32),
            pltpu.VMEM(levels.shape, F32),
            pltpu.SemaphoreType.DMA((14,)),
            pltpu.SemaphoreType.DMA((4,)),
            pltpu.SemaphoreType.DMA((4,)),
        ],
        compiler_params=pltpu.CompilerParams(
            collective_id=0, has_side_effects=True, vmem_limit_bytes=32 * 1024 * 1024),
    )(
        state, surface, mass, active, maps, more, tail, passive, drift, levels,
    )
    new_state, diag = pl.pallas_call(
        write,
        out_shape=(jax.ShapeDtypeStruct(new_state.shape, F32), jax.ShapeDtypeStruct(diag.shape, F32)),
        in_specs=[vmem, vmem],
        out_specs=(hbm, hbm),
        scratch_shapes=[pltpu.SemaphoreType.DMA((2,))],
    )(pltpu.with_memory_space_constraint(new_state, pltpu.VMEM), pltpu.with_memory_space_constraint(diag, pltpu.VMEM))
    return new_state.reshape(4, LEV, cols), diag.reshape(3, CX, cols)


def solution(mesh):
    both = ("elem", "grp")
    return jax.shard_map(
        functools.partial(body, mesh.shape["elem"]),
        mesh=mesh,
        in_specs=(P(None, None, both), P(None, None, both), P(both), P(None, both), P(both)),
        out_specs=(P(None, None, both), P(None, None, both)),
        check_vma=False,
    )
```

```python
import functools
import math

import jax
import jax.numpy as jnp
import ml_dtypes
import numpy as np
from jax import lax
from jax.experimental import pallas as pl
from jax.experimental.pallas import tpu as pltpu
from jax.sharding import PartitionSpec as P

LEV = 72
CZ = 58
CX = 32
EDGE = 64
LANES = 128
BLOCK = 128
ZP = 64
HALF = 2 * LEV
STATE_ROWS = 240
F32 = jnp.float32
BF16 = jnp.bfloat16
MESH = pl.DeviceIdType.MESH


def split_np(matrix):
    high = matrix.astype(np.float32).astype(ml_dtypes.bfloat16)
    low = (matrix - high.astype(np.float64)).astype(np.float32).astype(ml_dtypes.bfloat16)
    return high, low


def tables():
    z = np.arange(CZ, dtype=np.float64)
    lev = np.arange(LEV, dtype=np.float64)
    up = np.maximum(0.0, 1.0 - np.abs(z[:, None] * ((LEV - 1) / (CZ - 1)) - lev[None, :]))
    down = np.maximum(0.0, 1.0 - np.abs(lev[:, None] * ((CZ - 1) / (LEV - 1)) - z[None, :]))
    fall = 1.0 - 0.5 * z / (CZ - 1)
    k = 0.1 + 0.2 * z / (CZ - 1)
    mix = np.zeros((CZ, CZ))
    for i in range(CZ):
        mix[i, i] += 1.0 - 2.0 * k[i]
        mix[i, min(i + 1, CZ - 1)] += k[i]
        mix[i, max(i - 1, 0)] += k[i]
    kap = mix.sum(0)
    c1 = mix @ fall
    c2 = -0.1 * (mix @ (fall * fall))
    kb = mix @ up
    qb = -0.1 * (mix @ (fall[:, None] * up))

    m = np.zeros((208, 80))
    m[0:CZ, :LEV] = kb / 0.62
    m[64:64 + CZ, :LEV] = -0.25 * kb
    m[128:128 + CZ, :LEV] = qb
    m[192, :LEV] = (kap * c1) @ (-0.25 * kb)
    m[193, :LEV] = (kap * c2) @ (-0.25 * kb)
    m[194, :LEV] = (kap * c1) @ qb
    m[195, :LEV] = (kap * c2) @ qb
    m[196, :LEV] = kap @ qb
    hi, lo = split_np(m)
    maps = np.concatenate([hi, lo, hi], 1)
    dkk = down @ mix @ kb
    py, p0 = slice(0, 72), slice(80, 152)
    m = np.zeros((160, 160))
    m[0:72, p0] = dkk - down @ up
    m[0:72, py] = 0.8 * dkk / 1.24
    m[72:144, p0] = 0.3 * (dkk - down @ up)
    m[72:144, py] = 0.24 * dkk / 1.24 - down @ up
    m[144, p0] = 1.24 * (kap @ kb)
    m[144, py] = 0.8 * (kap @ kb)
    m[145, p0] = up.sum(0)
    hi, lo = split_np(m)
    more = np.concatenate([hi, lo, hi], 1)

    t = np.zeros((2 * HALF, ZP))
    t[0:72, 0:CZ] = down @ mix / 1.24
    t[72:144, 0:CZ] = 0.3 * (down @ mix) / 1.24
    t[144:216, 0:CZ] = -0.8 * down / 1.24
    t[216:288, 0:CZ] = down / 1.24
    hi, lo = split_np(t)
    tail = np.concatenate([hi, lo, hi], 1)

    e = np.zeros((HALF, HALF))
    e[0:72, 0:72] = down @ (mix @ kb - up)
    e[72:144, 72:144] = e[0:72, 0:72]
    hi, lo = split_np(e)
    passive = np.concatenate([hi, lo, hi], 1)
    drift = np.repeat(((down @ (mix @ (mix @ fall))) / CX)[:, None], LANES, 1).astype(np.float32)

    rows = np.zeros((3, ZP))
    rows[0, :CZ] = c1
    rows[1, :CZ] = c2
    rows[2, :CZ] = kap
    levels = np.repeat(rows.reshape(-1)[:, None], LANES, 1).astype(np.float32)
    consts = dict(
        c1=[float(a) for a in c1], c2=[float(a) for a in c2],
        stay=[float(a) for a in 0.248 * (1.0 - 2.0 * k)], move=[float(a) for a in 0.248 * k],
        s11=float((kap * c1 * c1).sum()), s12=float((kap * c1 * c2).sum()), s22=float((kap * c2 * c2).sum()),
        sc1=float((kap * c1).sum()), sc2=float((kap * c2).sum()))
    return maps, more, tail, passive, drift, levels, consts


def halves(x):
    high = x.astype(BF16)
    return high, (x - high.astype(F32)).astype(BF16)


def dot(a, b):
    return lax.dot_general(a, b, (((1,), (0,)), ((), ())), preferred_element_type=F32)


def dot_t(a, b):
    return lax.dot_general(a, b, (((1,), (1,)), ((), ())), preferred_element_type=F32)


class Whole:
    @staticmethod
    def rows(ref, j):
        return jnp.stack([ref[pl.ds(CX * j + v, 8, stride=4), :] for v in range(4)], 0)

    @staticmethod
    def east(f):
        return jnp.concatenate([f[1:], pltpu.roll(f[0], 7, 0)[None]], 0)

    @staticmethod
    def west(f):
        return jnp.concatenate([pltpu.roll(f[3], 1, 0)[None], f[:3]], 0)

    @staticmethod
    def fold(f):
        return (f[0] + f[1]) + (f[2] + f[3])

    @staticmethod
    def join(f):
        return f

    @staticmethod
    def store(ref, i, f):
        for v in range(4):
            ref[pl.ds(CX * i + v, 8, stride=4), :] = f[v]


class Half:
    @staticmethod
    def rows(ref, j):
        low = lax.broadcasted_iota(jnp.int32, (1, LANES), 1) < EDGE
        return jnp.stack([
            jnp.where(low, ref[pl.ds(CX * j + v, 8, stride=2), :], ref[pl.ds(CX * j + 16 + v, 8, stride=2), :])
            for v in range(2)], 0)

    @staticmethod
    def east(f):
        near = pltpu.roll(f[0], 7, 0)
        edge = lax.broadcasted_iota(jnp.int32, (8, LANES), 0) == 7
        return jnp.stack([f[1], jnp.where(edge, swap(near), near)], 0)

    @staticmethod
    def west(f):
        near = pltpu.roll(f[1], 1, 0)
        edge = lax.broadcasted_iota(jnp.int32, (8, LANES), 0) == 0
        return jnp.stack([jnp.where(edge, swap(near), near), f[0]], 0)

    @staticmethod
    def fold(f):
        return f[0] + f[1]

    @staticmethod
    def join(f):
        return f + swap(f)

    @staticmethod
    def store(ref, i, f):
        low = lax.broadcasted_iota(jnp.int32, (1, LANES), 1) < EDGE
        for v in range(2):
            other = swap(f[v])
            ref[pl.ds(CX * i + v, 8, stride=2), :] = jnp.where(low, f[v], other)
            ref[pl.ds(CX * i + 16 + v, 8, stride=2), :] = jnp.where(low, other, f[v])


def swap(x):
    return pltpu.roll(x, EDGE, 1)


def prepare(form, sur_ref):
    east, west = form.east, form.west
    r0, r1, s2 = form.rows(sur_ref, 0), form.rows(sur_ref, 1), form.rows(sur_ref, 2)
    sy, sw = (r1 - 0.3 * r0) * (1.0 / 0.62), r0 + 0.8 * r1

    def xsum(f):
        return form.join(jnp.sum(form.fold(f), axis=0, keepdims=True))

    def parts(s):
        e, w = east(s), west(s)
        return 0.6 * s + 0.2 * (e + w), e - w

    ay, dy = parts(sy)
    a2, d2 = parts(s2)
    af, df = -0.25 * a2, -0.25 * d2
    aw, dw = parts(sw)
    ew, ef = s2 * dw, s2 * df
    haw, hdw, hew = east(aw) - west(aw), east(dw) - west(dw), east(ew) - west(ew)
    gram = (xsum(af * haw), xsum(af * hdw + df * haw), xsum(af * hew + ef * haw),
            xsum(df * hdw), xsum(df * hew + ef * hdw), xsum(ef * hew))
    means = (xsum(sw) * (1.0 / CX), xsum(ew) * (1.0 / CX))
    return s2, ay, dy, af, df, aw, dw, ef, haw, hdw, hew, gram, means


def cloud(form, consts, prep, prof_ref, lanes, tail_ref, lev_ref, part_ref, diag_ref, at={}, steady=None):
    s2, ay, dy, af, df, aw, dw, ef, haw, hdw, hew, gram, means = prep
    east, west = form.east, form.west

    def level(start, z):
        return prof_ref[start + z:start + z + 1, lanes][None]

    def horizontal(z):
        if steady is None:
            turn = level(128, z) + consts["c2"][z] * s2
            y = (level(0, z) + consts["c1"][z] * ay) + turn * dy
            pull = (level(64, z) + consts["c1"][z] * af) + turn * df
        else:
            turn = level(128, z)
            y = (level(0, z) + steady[z, 0]) + turn * dy
            pull = (level(64, z) + steady[z, 1]) + turn * df
        one = jnp.log(1.0 + jnp.exp2(y * (0.62 * math.log2(math.e))))
        y = y - one
        e, w = east(y), west(y)
        return (1.5 * y + w) + pull * (e - w), one

    def vertical(z, h, above, below):
        v = consts["stay"][z] * h + consts["move"][z] * (above + below)
        two = jnp.maximum(jnp.log(1.0 + jnp.exp(jnp.minimum(v, 80.0))), v)
        part_ref[8 * z:8 * z + 8, :] = form.fold(v) - 0.62 * form.fold(two)
        return v, two

    h, rain = horizontal(0)
    below = h
    total_v = total_2 = None
    def passive_sums():
        pf = prof_ref[64:128, lanes] - 0.5
        q = prof_ref[128:192, lanes]
        s1p, s2p, s1q, sq2, sq = [prof_ref[192 + i:193 + i, lanes] for i in range(5)]
        c1 = lev_ref[0:ZP, :]
        c2 = lev_ref[ZP:2 * ZP, :]
        kap = lev_ref[2 * ZP:3 * ZP, :]
        g11, g12, g13, g22, g23, g33 = gram
        bend = c1 * (c1 * g11 + q * g12 + c2 * g13) + q * (q * g22 + c2 * g23) + (c2 * c2) * g33
        mean_w = c1 * means[0] + c2 * means[1] + (0.4 / CX) * bend
        hi, lo = halves(mean_w)
        prof_ref[208:352, lanes] += dot(tail_ref[0:HALF, :], jnp.concatenate([hi, hi, lo], 0))
        qk = q * kap
        sqp = jnp.sum(qk * pf, axis=0, keepdims=True)
        sqq = jnp.sum(qk * q, axis=0, keepdims=True)
        s11, s12, s22 = consts["s11"], consts["s12"], consts["s22"]
        w1 = (prof_ref[352:353, lanes] + consts["sc1"] * aw) + (sq * dw + consts["sc2"] * (s2 * dw))
        return (
            (0.6 * w1 + 0.2 * (east(w1) + west(w1)))
            + 0.4 * (
                haw * ((s1p + s11 * af) + (s1q * df + s12 * ef))
                + hdw * ((sqp + s1q * af) + (sqq * df + sq2 * ef))
                + hew * ((s2p + s12 * af) + (sq2 * df + s22 * ef))
            )
        )

    for z in range(CZ):
        if z in at:
            at[z]()
        if z == 26:
            sum_w = passive_sums()
            form.store(diag_ref, 1, 0.3 * sum_w)
            form.store(diag_ref, 2, sum_w - 1.24 * prof_ref[353:354, lanes])
        if z + 1 < CZ:
            above, one = horizontal(z + 1)
            rain = rain + one
        else:
            above = h
        v, two = vertical(z, h, above, below)
        total_v = v if z == 0 else total_v + v
        total_2 = two if z == 0 else total_2 + two
        h, below = above, h
    mean_y = part_ref[pl.ds(0, CZ, stride=8), :]
    for s in range(1, 8):
        mean_y = mean_y + part_ref[pl.ds(s, CZ, stride=8), :]
    mean_y = form.join(mean_y) * (1.0 / CX)
    hi, lo = halves(jnp.concatenate([mean_y, jnp.zeros((ZP - CZ, LANES), F32)], 0))
    tend = prof_ref[208:352, lanes] + dot(tail_ref[HALF:, :], jnp.concatenate([hi, hi, lo], 0))
    sum_y = total_v - 0.62 * total_2
    form.store(diag_ref, 0, 0.5 * (rain + total_2))
    form.store(part_ref, 0, sum_y)
    scale = 1.0 / (1.24 * CZ)
    sums = part_ref[0:CX, :]
    diag_ref[CX:2 * CX, :] = (diag_ref[CX:2 * CX, :] + sums) * scale
    diag_ref[2 * CX:, :] = (diag_ref[2 * CX:, :] - 0.8 * sums) * scale
    return tend


def first_maps(maps_ref, ref, hi, lo):
    ref[0:64, :] = dot(maps_ref[0:64, :], jnp.concatenate([hi[:80], hi[:80], lo[:80]], 0))
    x = dot(maps_ref[64:208, :], jnp.concatenate([hi[80:160], hi[80:160], lo[80:160]], 0))
    ref[64:128, :] = x[:64] + 0.5
    ref[128:208, :] = x[64:]


def more_maps(more_ref, ref, hi, lo):
    ref[208:368, :] = dot(more_ref[...], jnp.concatenate([hi, hi, lo], 0))


SENT = ((0, 80), (80, 72))


def kernel(consts, n_elem, state_ref, surface_ref, mass_hbm, active_hbm, maps_hbm, more_hbm, tail_hbm, passive_hbm,
           drift_hbm, lev_hbm, out_ref, diag_out_ref,
           xs, hi_ref, lo_ref, su, ones_ref, send, recv, sur, prof, edge_prof, part, diag, both_hi, both_lo, own_ref, steady_ref,
           mass_ref, active_ref, maps_ref, more_ref, tail_ref, passive_ref, drift_ref, lev_ref,
           in_sem, send_sem, recv_sem):
    e, g = lax.axis_index("elem"), lax.axis_index("grp")
    after = lax.rem(e + 1, n_elem)
    before = lax.rem(e + n_elem - 1, n_elem)
    barrier = pltpu.get_barrier_semaphore()
    for other in (before, after):
        pl.semaphore_signal(barrier, inc=1, device_id=(other, g), device_id_type=MESH)

    tiles = [slice(LANES * b, LANES * (b + 1)) for b in range(4)]
    ends = (tiles[3], tiles[0])
    loads = [
        pltpu.make_async_copy(state_ref.at[rows, lanes], xs.at[rows, lanes], in_sem.at[k])
        for k, (rows, lanes) in enumerate(
            (rows, lanes) for rows in (slice(0, 3 * LEV), slice(3 * LEV, 4 * LEV)) for lanes in ends)
    ] + [
        pltpu.make_async_copy(state_ref.at[:, pl.ds(LANES, 2 * LANES)], xs.at[:, pl.ds(LANES, 2 * LANES)], in_sem.at[4]),
        pltpu.make_async_copy(surface_ref, su, in_sem.at[5]),
    ]
    small = [
        pltpu.make_async_copy(a, b, in_sem.at[6 + i])
        for i, (a, b) in enumerate((
            (mass_hbm, mass_ref), (active_hbm, active_ref), (maps_hbm, maps_ref), (lev_hbm, lev_ref),
            (more_hbm, more_ref), (tail_hbm, tail_ref), (passive_hbm, passive_ref), (drift_hbm, drift_ref)))
    ]
    for load in small[:1] + loads[:4] + small[1:2] + loads[4:] + small[2:]:
        load.start()

    low = lax.broadcasted_iota(jnp.int32, (1, LANES), 1) < EDGE

    def end_copy(c, i):
        rows = pl.ds(*SENT[c])
        return pltpu.make_async_remote_copy(
            src_ref=send.at[i, rows], dst_ref=recv.at[i, rows],
            send_sem=send_sem.at[2 * c + i], recv_sem=recv_sem.at[2 * c + i],
            device_id=((after, before)[i] if isinstance(i, int) else after, g), device_id_type=MESH)

    sent = [end_copy(c, i) for i in range(2) for c in range(2)]

    def enter():
        pl.semaphore_wait(barrier, 2)

    def exchange():
        enter()
        for copy in sent:
            copy.start()

    first_e, last_e = e == 0, e == n_elem - 1
    pl.when(last_e)(enter)
    small[0].wait()
    for i, lanes in enumerate(ends):
        mass = mass_ref[:, lanes]
        mass = jnp.where(low, swap(mass), mass) if i == 0 else jnp.where(low, mass, swap(mass))
        send[i, 0:8, :] = jnp.broadcast_to(mass, (8, LANES))
        loads[i].wait()
        p0 = xs[0:LEV, lanes]
        py, p2 = xs[LEV:2 * LEV, lanes] - 0.3 * p0, xs[2 * LEV:3 * LEV, lanes]
        send[i, 8:80, :] = jnp.where(low, swap(py), p2) if i == 0 else jnp.where(low, py, swap(p2))
        pl.when(last_e)(sent[2 * i].start)
        loads[2 + i].wait()
        p0, p3 = xs[0:LEV, lanes], xs[3 * LEV:, lanes]
        send[i, 80:152, :] = jnp.where(low, swap(p0), p3) if i == 0 else jnp.where(low, p0, swap(p3))
        pl.when(last_e)(sent[2 * i + 1].start)

    small[1].wait()
    act = [active_ref[:, lanes].astype(F32) for lanes in tiles]
    inner = [jnp.where(low, 0.0, act[0]), act[1], act[2], jnp.where(low, act[3], 0.0)]
    marks = jnp.concatenate(inner + [jnp.zeros((4, LANES), F32)], 0)
    r = lax.broadcasted_iota(jnp.int32, (LANES, LANES), 0)
    c = lax.broadcasted_iota(jnp.int32, (LANES, LANES), 1)
    tri = jnp.where(r <= c, 1.0, 0.0).astype(BF16)
    counts = dot(marks.astype(BF16), jnp.concatenate([tri, jnp.ones((LANES, LANES), BF16)], 1))
    where = lax.broadcasted_iota(jnp.int32, (2 * BLOCK, LANES), 0).astype(F32)
    offset = jnp.full((1, LANES), -1.0, F32)
    for b, lanes in enumerate(tiles):
        place = jnp.where(inner[b] > 0.5, counts[b:b + 1, :LANES] + offset, -1.0)
        ones_ref[:, lanes] = jnp.where(where == place, 1.0, 0.0).astype(BF16)
        offset = offset + counts[b:b + 1, LANES:]

    loads[4].wait()
    loads[5].wait()

    def ordered(x):
        pad = jnp.zeros((8, x.shape[1]), F32)
        return jnp.concatenate(
            [x[LEV:2 * LEV] - 0.3 * x[0:LEV], pad, x[2 * LEV:3 * LEV], pad, x[0:LEV], x[3 * LEV:4 * LEV]], 0)

    hi, lo = halves(ordered(xs[...]))
    hi_ref[0:304, :] = hi
    lo_ref[0:304, :] = lo
    hi, lo = halves(su[...])
    hi_ref[304:400, :] = hi
    lo_ref[304:400, :] = lo
    for load in small[2:]:
        load.wait()
    pl.when(jnp.logical_and(e > 1, e < n_elem - 1))(exchange)

    def gather(ref, rows):
        return dot_t(ref[rows, :], ones_ref[...])

    def to_next():
        for c in range(2):
            end_copy(c, 1).wait_recv()
        sent[0].start()
        sent[1].start()

    def to_previous():
        enter()
        sent[2].start()
        sent[3].start()

    meanwhile = ({24: lambda: pl.when(e == 1)(exchange)}, {8: lambda: pl.when(first_e)(to_next)})
    main = slice(0, STATE_ROWS)
    hi, lo = gather(hi_ref, main).astype(BF16), gather(lo_ref, main).astype(BF16)
    first_maps(maps_ref, prof, hi, lo)
    more_maps(more_ref, prof, jnp.concatenate([hi[:80], hi[160:]], 0), jnp.concatenate([lo[:80], lo[160:]], 0))
    found = gather(hi_ref, slice(304, 400)) + gather(lo_ref, slice(304, 400))
    for i in range(2):
        lanes = tiles[i]
        sur[...] = found[:, lanes]
        tend = cloud(Whole, consts, prepare(Whole, sur), prof, lanes, tail_ref, lev_ref, part, diag, meanwhile[i])
        hi, lo = halves(jnp.concatenate([tend, diag[...]], 0))
        both_hi[:, lanes] = hi
        both_lo[:, lanes] = lo

    pl.when(first_e)(to_previous)

    def passive(x, s2):
        hi, lo = halves(x)
        slow = dot(passive_ref[...], jnp.concatenate([hi, hi, lo], 0))
        mean2 = jnp.sum(s2, axis=0, keepdims=True)
        return jnp.concatenate([slow[:LEV] + drift_ref[...] * mean2, slow[LEV:]], 0)

    for b, lanes in enumerate(tiles):
        x = xs[HALF:, lanes]
        out_ref[HALF:, lanes] = x + jnp.where(act[b] > 0.5, passive(x, su[2 * CX:, lanes]), 0.0)
    back = dot(both_hi[...], ones_ref[...]) + dot(both_lo[...], ones_ref[...])
    out_ref[0:HALF, :] = xs[0:HALF, :] + back[0:HALF]
    diag_out_ref[...] = back[HALF:]

    def edge(form, own_mass, on, wait, other_mass, arrived, emit):
        prep = prepare(form, sur)
        steady = None
        if form is Half:
            steady = steady_ref
            s2, ay, dy, af, df = prep[:5]
            sdy, sdf = s2 * dy, s2 * df
            for z in range(CZ):
                steady[z, 0] = consts["c1"][z] * ay + consts["c2"][z] * sdy
                steady[z, 1] = consts["c1"][z] * af + consts["c2"][z] * sdf
        wait(0)
        masses = other_mass()
        scale = 1.0 / (own_mass + masses)
        share, rest = own_mass * scale, masses * scale
        pad = jnp.zeros((8, LANES), F32)
        py, p2 = arrived(8)
        start = own_ref[0:160, :] * share + jnp.concatenate([py, pad, p2, pad], 0) * rest
        hi, lo = halves(start)
        first_maps(maps_ref, edge_prof, hi, lo)
        both_p = []

        def late():
            wait(1)
            final = own_ref[160:, :] * share + jnp.concatenate(arrived(80), 0) * rest
            more_hi, more_lo = halves(final[:80])
            more_maps(more_ref, edge_prof, jnp.concatenate([hi[:80], more_hi], 0),
                      jnp.concatenate([lo[:80], more_lo], 0))
            p0, p2, p3 = final[:LEV], start[80:152], final[LEV:]
            both_p.append(jnp.concatenate([p0, start[:LEV] + 0.3 * p0], 0))
            x = jnp.concatenate([p2, p3], 0)
            emit(slice(HALF, 2 * HALF), x + jnp.where(on, passive(x, sur[2 * CX:, :]), 0.0))

        tend = cloud(form, consts, prep, edge_prof, tiles[0], tail_ref, lev_ref, part, diag, {24: late}, steady)
        emit(slice(0, HALF), both_p[0] + jnp.where(on, tend, 0.0))
        return jnp.where(on, diag[...], 0.0)

    def one_end(k, _):
        i, got = k, 1 - k
        lanes = pl.ds(pl.multiple_of((1 - i) * (3 * LANES), LANES), LANES)
        side = low == (i == 1)

        def double(x):
            return jnp.where(side, x, swap(x))

        def arrived(row):
            x = recv[got, row:row + LEV, :]
            y = swap(x)
            return jnp.where(low, x, y), jnp.where(low, y, x)

        def emit(rows, new):
            out_ref[rows, lanes] = jnp.where(side, new, out_ref[rows, lanes])

        sur[...] = double(su[:, lanes])
        own_ref[...] = ordered(double(xs[:, lanes]))
        seen = edge(
            Half, double(mass_ref[:, lanes]), jnp.where(side, active_ref[:, lanes], 0) == 1,
            lambda c: pl.when(jnp.logical_not(jnp.logical_and(first_e, got == 1)))(end_copy(c, got).wait_recv),
            lambda: recv[got, 0:1, :], arrived, emit)
        diag_out_ref[:, lanes] = jnp.where(side, seen, diag_out_ref[:, lanes])
        return 0

    def both_ends():
        t0, t3 = tiles[0], tiles[3]

        def merge(ref):
            return jnp.where(low, ref[:, t0], ref[:, t3])

        def wait(c):
            for got in range(2):
                end_copy(c, got).wait_recv()

        def arrived(row):
            x, y = recv[0, row:row + LEV, :], recv[1, row:row + LEV, :]
            return jnp.where(low, x, swap(y)), jnp.where(low, swap(x), y)

        def emit(rows, new):
            out_ref[rows, t0] = jnp.where(low, new, out_ref[rows, t0])
            out_ref[rows, t3] = jnp.where(low, out_ref[rows, t3], new)

        sur[...] = merge(su)
        own_ref[...] = ordered(merge(xs))
        seen = edge(
            Whole, merge(mass_ref), merge(active_ref) == 1, wait,
            lambda: jnp.where(low, recv[0, 0:1, :], recv[1, 0:1, :]), arrived, emit)
        diag_out_ref[:, t0] = jnp.where(low, seen, diag_out_ref[:, t0])
        diag_out_ref[:, t3] = jnp.where(low, diag_out_ref[:, t3], seen)

    alone = e <= 1

    @pl.when(alone)
    def _():
        lax.fori_loop(0, 2, one_end, 0)

    pl.when(jnp.logical_not(alone))(both_ends)

    for copy in sent:
        copy.wait_send()


def write(state_ref, diag_ref, state_out, diag_out, sem):
    copies = [pltpu.make_async_copy(state_ref, state_out, sem.at[0]),
              pltpu.make_async_copy(diag_ref, diag_out, sem.at[1])]
    for copy in copies:
        copy.start()
    for copy in copies:
        copy.wait()


def body(n_elem, state, surface, mass, plan, active):
    cols = state.shape[2]
    maps, more, tail, passive, drift, levels, consts = tables()
    hbm = pl.BlockSpec(memory_space=pltpu.HBM)
    vmem = pl.BlockSpec(memory_space=pltpu.VMEM)
    state, surface, mass, active, maps, more, tail, passive, drift, levels = [
        pltpu.with_memory_space_constraint(x, pltpu.HBM) for x in (
            state.reshape(4 * LEV, cols), surface.reshape(3 * CX, cols), mass.reshape(1, cols),
            active.reshape(1, cols), *map(jnp.asarray, (maps, more, tail, passive, drift, levels)))]
    new_state, diag = pl.pallas_call(
        functools.partial(kernel, consts, n_elem),
        out_shape=(pltpu.VMEM((4 * LEV, cols), F32), pltpu.VMEM((3 * CX, cols), F32)),
        in_specs=[hbm] * 10,
        out_specs=(vmem, vmem),
        scratch_shapes=[
            pltpu.VMEM((4 * LEV, cols), F32),
            pltpu.VMEM((400, cols), BF16),
            pltpu.VMEM((400, cols), BF16),
            pltpu.VMEM((3 * CX, cols), F32),
            pltpu.VMEM((2 * BLOCK, cols), BF16),
            pltpu.VMEM((2, HALF + 8, LANES), F32),
            pltpu.VMEM((2, HALF + 8, LANES), F32),
            pltpu.VMEM((3 * CX, BLOCK), F32),
            pltpu.VMEM((368, 2 * BLOCK), F32),
            pltpu.VMEM((368, BLOCK), F32),
            pltpu.VMEM((ZP * 8, BLOCK), F32),
            pltpu.VMEM((3 * CX, BLOCK), F32),
            pltpu.VMEM((HALF + 3 * CX, 2 * BLOCK), BF16),
            pltpu.VMEM((HALF + 3 * CX, 2 * BLOCK), BF16),
            pltpu.VMEM((4 * LEV + 16, LANES), F32),
            pltpu.VMEM((CZ, 2, 2, 8, LANES), F32),
            pltpu.VMEM((1, cols), F32),
            pltpu.VMEM((1, cols), jnp.int32),
            pltpu.VMEM(maps.shape, BF16),
            pltpu.VMEM(more.shape, BF16),
            pltpu.VMEM(tail.shape, BF16),
            pltpu.VMEM(passive.shape, BF16),
            pltpu.VMEM(drift.shape, F32),
            pltpu.VMEM(levels.shape, F32),
            pltpu.SemaphoreType.DMA((14,)),
            pltpu.SemaphoreType.DMA((4,)),
            pltpu.SemaphoreType.DMA((4,)),
        ],
        compiler_params=pltpu.CompilerParams(
            collective_id=0, has_side_effects=True, vmem_limit_bytes=32 * 1024 * 1024),
    )(
        state, surface, mass, active, maps, more, tail, passive, drift, levels,
    )
    new_state, diag = pl.pallas_call(
        write,
        out_shape=(jax.ShapeDtypeStruct(new_state.shape, F32), jax.ShapeDtypeStruct(diag.shape, F32)),
        in_specs=[vmem, vmem],
        out_specs=(hbm, hbm),
        scratch_shapes=[pltpu.SemaphoreType.DMA((2,))],
    )(pltpu.with_memory_space_constraint(new_state, pltpu.VMEM), pltpu.with_memory_space_constraint(diag, pltpu.VMEM))
    return new_state.reshape(4, LEV, cols), diag.reshape(3, CX, cols)


def solution(mesh):
    both = ("elem", "grp")
    return jax.shard_map(
        functools.partial(body, mesh.shape["elem"]),
        mesh=mesh,
        in_specs=(P(None, None, both), P(None, None, both), P(both), P(None, both), P(both)),
        out_specs=(P(None, None, both), P(None, None, both)),
        check_vma=False,
    )
```

```python
import functools
import math

import jax
import jax.numpy as jnp
import ml_dtypes
import numpy as np
from jax import lax
from jax.experimental import pallas as pl
from jax.experimental.pallas import tpu as pltpu
from jax.sharding import PartitionSpec as P

LEV = 72
CZ = 58
CX = 32
EDGE = 64
LANES = 128
BLOCK = 128
ZP = 64
HALF = 2 * LEV
STATE_ROWS = 240
F32 = jnp.float32
BF16 = jnp.bfloat16
MESH = pl.DeviceIdType.MESH


def split_np(matrix):
    high = matrix.astype(np.float32).astype(ml_dtypes.bfloat16)
    low = (matrix - high.astype(np.float64)).astype(np.float32).astype(ml_dtypes.bfloat16)
    return high, low


def tables():
    z = np.arange(CZ, dtype=np.float64)
    lev = np.arange(LEV, dtype=np.float64)
    up = np.maximum(0.0, 1.0 - np.abs(z[:, None] * ((LEV - 1) / (CZ - 1)) - lev[None, :]))
    down = np.maximum(0.0, 1.0 - np.abs(lev[:, None] * ((CZ - 1) / (LEV - 1)) - z[None, :]))
    fall = 1.0 - 0.5 * z / (CZ - 1)
    k = 0.1 + 0.2 * z / (CZ - 1)
    mix = np.zeros((CZ, CZ))
    for i in range(CZ):
        mix[i, i] += 1.0 - 2.0 * k[i]
        mix[i, min(i + 1, CZ - 1)] += k[i]
        mix[i, max(i - 1, 0)] += k[i]
    kap = mix.sum(0)
    c1 = mix @ fall
    c2 = -0.1 * (mix @ (fall * fall))
    kb = mix @ up
    qb = -0.1 * (mix @ (fall[:, None] * up))

    m = np.zeros((208, 80))
    m[0:CZ, :LEV] = kb / 0.62
    m[64:64 + CZ, :LEV] = -0.25 * kb
    m[128:128 + CZ, :LEV] = qb
    m[192, :LEV] = (kap * c1) @ (-0.25 * kb)
    m[193, :LEV] = (kap * c2) @ (-0.25 * kb)
    m[194, :LEV] = (kap * c1) @ qb
    m[195, :LEV] = (kap * c2) @ qb
    m[196, :LEV] = kap @ qb
    hi, lo = split_np(m)
    maps = np.concatenate([hi, lo, hi], 1)
    dkk = down @ mix @ kb
    py, p0 = slice(0, 72), slice(80, 152)
    m = np.zeros((160, 160))
    m[0:72, p0] = dkk - down @ up
    m[0:72, py] = 0.8 * dkk / 1.24
    m[72:144, p0] = 0.3 * (dkk - down @ up)
    m[72:144, py] = 0.24 * dkk / 1.24 - down @ up
    m[144, p0] = 1.24 * (kap @ kb)
    m[144, py] = 0.8 * (kap @ kb)
    m[145, p0] = up.sum(0)
    hi, lo = split_np(m)
    more = np.concatenate([hi, lo, hi], 1)

    t = np.zeros((2 * HALF, ZP))
    t[0:72, 0:CZ] = down @ mix / 1.24
    t[72:144, 0:CZ] = 0.3 * (down @ mix) / 1.24
    t[144:216, 0:CZ] = -0.8 * down / 1.24
    t[216:288, 0:CZ] = down / 1.24
    hi, lo = split_np(t)
    tail = np.concatenate([hi, lo, hi], 1)

    e = np.zeros((HALF, HALF))
    e[0:72, 0:72] = down @ (mix @ kb - up)
    e[72:144, 72:144] = e[0:72, 0:72]
    hi, lo = split_np(e)
    passive = np.concatenate([hi, lo, hi], 1)
    drift = np.repeat(((down @ (mix @ (mix @ fall))) / CX)[:, None], LANES, 1).astype(np.float32)

    rows = np.zeros((3, ZP))
    rows[0, :CZ] = c1
    rows[1, :CZ] = c2
    rows[2, :CZ] = kap
    levels = np.repeat(rows.reshape(-1)[:, None], LANES, 1).astype(np.float32)
    consts = dict(
        c1=[float(a) for a in c1], c2=[float(a) for a in c2],
        stay=[float(a) for a in 0.248 * (1.0 - 2.0 * k)], move=[float(a) for a in 0.248 * k],
        s11=float((kap * c1 * c1).sum()), s12=float((kap * c1 * c2).sum()), s22=float((kap * c2 * c2).sum()),
        sc1=float((kap * c1).sum()), sc2=float((kap * c2).sum()))
    return maps, more, tail, passive, drift, levels, consts


def halves(x):
    high = x.astype(BF16)
    return high, (x - high.astype(F32)).astype(BF16)


def dot(a, b):
    return lax.dot_general(a, b, (((1,), (0,)), ((), ())), preferred_element_type=F32)


def dot_t(a, b):
    return lax.dot_general(a, b, (((1,), (1,)), ((), ())), preferred_element_type=F32)


class Whole:
    @staticmethod
    def rows(ref, j):
        return jnp.stack([ref[pl.ds(CX * j + v, 8, stride=4), :] for v in range(4)], 0)

    @staticmethod
    def east(f):
        return jnp.concatenate([f[1:], pltpu.roll(f[0], 7, 0)[None]], 0)

    @staticmethod
    def west(f):
        return jnp.concatenate([pltpu.roll(f[3], 1, 0)[None], f[:3]], 0)

    @staticmethod
    def fold(f):
        return (f[0] + f[1]) + (f[2] + f[3])

    @staticmethod
    def join(f):
        return f

    @staticmethod
    def store(ref, i, f):
        for v in range(4):
            ref[pl.ds(CX * i + v, 8, stride=4), :] = f[v]


class Half:
    @staticmethod
    def rows(ref, j):
        low = lax.broadcasted_iota(jnp.int32, (1, LANES), 1) < EDGE
        return jnp.stack([
            jnp.where(low, ref[pl.ds(CX * j + v, 8, stride=2), :], ref[pl.ds(CX * j + 16 + v, 8, stride=2), :])
            for v in range(2)], 0)

    @staticmethod
    def east(f):
        near = pltpu.roll(f[0], 7, 0)
        edge = lax.broadcasted_iota(jnp.int32, (8, LANES), 0) == 7
        return jnp.stack([f[1], jnp.where(edge, swap(near), near)], 0)

    @staticmethod
    def west(f):
        near = pltpu.roll(f[1], 1, 0)
        edge = lax.broadcasted_iota(jnp.int32, (8, LANES), 0) == 0
        return jnp.stack([jnp.where(edge, swap(near), near), f[0]], 0)

    @staticmethod
    def fold(f):
        return f[0] + f[1]

    @staticmethod
    def join(f):
        return f + swap(f)

    @staticmethod
    def store(ref, i, f):
        low = lax.broadcasted_iota(jnp.int32, (1, LANES), 1) < EDGE
        for v in range(2):
            other = swap(f[v])
            ref[pl.ds(CX * i + v, 8, stride=2), :] = jnp.where(low, f[v], other)
            ref[pl.ds(CX * i + 16 + v, 8, stride=2), :] = jnp.where(low, other, f[v])


def swap(x):
    return pltpu.roll(x, EDGE, 1)


def prepare(form, sur_ref):
    east, west = form.east, form.west
    r0, r1, s2 = form.rows(sur_ref, 0), form.rows(sur_ref, 1), form.rows(sur_ref, 2)
    sy, sw = (r1 - 0.3 * r0) * (1.0 / 0.62), r0 + 0.8 * r1

    def xsum(f):
        return form.join(jnp.sum(form.fold(f), axis=0, keepdims=True))

    def parts(s):
        e, w = east(s), west(s)
        return 0.6 * s + 0.2 * (e + w), e - w

    ay, dy = parts(sy)
    a2, d2 = parts(s2)
    af, df = -0.25 * a2, -0.25 * d2
    aw, dw = parts(sw)
    ew, ef = s2 * dw, s2 * df
    haw, hdw, hew = east(aw) - west(aw), east(dw) - west(dw), east(ew) - west(ew)
    gram = (xsum(af * haw), xsum(af * hdw + df * haw), xsum(af * hew + ef * haw),
            xsum(df * hdw), xsum(df * hew + ef * hdw), xsum(ef * hew))
    means = (xsum(sw) * (1.0 / CX), xsum(ew) * (1.0 / CX))
    return s2, ay, dy, af, df, aw, dw, ef, haw, hdw, hew, gram, means


def cloud(form, consts, prep, prof_ref, lanes, tail_ref, lev_ref, part_ref, diag_ref, at={}, steady=None):
    s2, ay, dy, af, df, aw, dw, ef, haw, hdw, hew, gram, means = prep
    east, west = form.east, form.west

    def level(start, z):
        return prof_ref[start + z:start + z + 1, lanes][None]

    def horizontal(z):
        if steady is None:
            turn = level(128, z) + consts["c2"][z] * s2
            y = (level(0, z) + consts["c1"][z] * ay) + turn * dy
            pull = (level(64, z) + consts["c1"][z] * af) + turn * df
        else:
            turn = level(128, z)
            y = (level(0, z) + steady[z, 0]) + turn * dy
            pull = (level(64, z) + steady[z, 1]) + turn * df
        one = jnp.log(1.0 + jnp.exp2(y * (0.62 * math.log2(math.e))))
        y = y - one
        e, w = east(y), west(y)
        return (1.5 * y + w) + pull * (e - w), one

    def vertical(z, h, above, below):
        v = consts["stay"][z] * h + consts["move"][z] * (above + below)
        two = jnp.maximum(jnp.log(1.0 + jnp.exp(jnp.minimum(v, 80.0))), v)
        part_ref[8 * z:8 * z + 8, :] = form.fold(v) - 0.62 * form.fold(two)
        return v, two

    h, rain = horizontal(0)
    below = h
    total_v = total_2 = None
    def passive_sums():
        pf = prof_ref[64:128, lanes] - 0.5
        q = prof_ref[128:192, lanes]
        s1p, s2p, s1q, sq2, sq = [prof_ref[192 + i:193 + i, lanes] for i in range(5)]
        c1 = lev_ref[0:ZP, :]
        c2 = lev_ref[ZP:2 * ZP, :]
        kap = lev_ref[2 * ZP:3 * ZP, :]
        g11, g12, g13, g22, g23, g33 = gram
        bend = c1 * (c1 * g11 + q * g12 + c2 * g13) + q * (q * g22 + c2 * g23) + (c2 * c2) * g33
        mean_w = c1 * means[0] + c2 * means[1] + (0.4 / CX) * bend
        hi, lo = halves(mean_w)
        prof_ref[208:352, lanes] += dot(tail_ref[0:HALF, :], jnp.concatenate([hi, hi, lo], 0))
        qk = q * kap
        sqp = jnp.sum(qk * pf, axis=0, keepdims=True)
        sqq = jnp.sum(qk * q, axis=0, keepdims=True)
        s11, s12, s22 = consts["s11"], consts["s12"], consts["s22"]
        w1 = (prof_ref[352:353, lanes] + consts["sc1"] * aw) + (sq * dw + consts["sc2"] * (s2 * dw))
        return (
            (0.6 * w1 + 0.2 * (east(w1) + west(w1)))
            + 0.4 * (
                haw * ((s1p + s11 * af) + (s1q * df + s12 * ef))
                + hdw * ((sqp + s1q * af) + (sqq * df + sq2 * ef))
                + hew * ((s2p + s12 * af) + (sq2 * df + s22 * ef))
            )
        )

    for z in range(CZ):
        if z in at:
            at[z]()
        if z == 36:
            sum_w = passive_sums()
            form.store(diag_ref, 1, 0.3 * sum_w)
            form.store(diag_ref, 2, sum_w - 1.24 * prof_ref[353:354, lanes])
        if z + 1 < CZ:
            above, one = horizontal(z + 1)
            rain = rain + one
        else:
            above = h
        v, two = vertical(z, h, above, below)
        total_v = v if z == 0 else total_v + v
        total_2 = two if z == 0 else total_2 + two
        h, below = above, h
    mean_y = part_ref[pl.ds(0, CZ, stride=8), :]
    for s in range(1, 8):
        mean_y = mean_y + part_ref[pl.ds(s, CZ, stride=8), :]
    mean_y = form.join(mean_y) * (1.0 / CX)
    hi, lo = halves(jnp.concatenate([mean_y, jnp.zeros((ZP - CZ, LANES), F32)], 0))
    tend = prof_ref[208:352, lanes] + dot(tail_ref[HALF:, :], jnp.concatenate([hi, hi, lo], 0))
    sum_y = total_v - 0.62 * total_2
    form.store(diag_ref, 0, 0.5 * (rain + total_2))
    form.store(part_ref, 0, sum_y)
    scale = 1.0 / (1.24 * CZ)
    sums = part_ref[0:CX, :]
    diag_ref[CX:2 * CX, :] = (diag_ref[CX:2 * CX, :] + sums) * scale
    diag_ref[2 * CX:, :] = (diag_ref[2 * CX:, :] - 0.8 * sums) * scale
    return tend


def first_maps(maps_ref, ref, hi, lo):
    ref[0:64, :] = dot(maps_ref[0:64, :], jnp.concatenate([hi[:80], hi[:80], lo[:80]], 0))
    x = dot(maps_ref[64:208, :], jnp.concatenate([hi[80:160], hi[80:160], lo[80:160]], 0))
    ref[64:128, :] = x[:64] + 0.5
    ref[128:208, :] = x[64:]


def more_maps(more_ref, ref, hi, lo):
    ref[208:368, :] = dot(more_ref[...], jnp.concatenate([hi, hi, lo], 0))


SENT = ((0, 48), (48, 40), (88, 72))


def kernel(consts, n_elem, state_ref, surface_ref, mass_hbm, active_hbm, maps_hbm, more_hbm, tail_hbm, passive_hbm,
           drift_hbm, lev_hbm, out_ref, diag_out_ref,
           xs, hi_ref, lo_ref, su, ones_ref, send, recv, sur, prof, edge_prof, part, diag, both_hi, both_lo, own_ref, steady_ref,
           mass_ref, active_ref, maps_ref, more_ref, tail_ref, passive_ref, drift_ref, lev_ref,
           in_sem, send_sem, recv_sem):
    e, g = lax.axis_index("elem"), lax.axis_index("grp")
    after = lax.rem(e + 1, n_elem)
    before = lax.rem(e + n_elem - 1, n_elem)
    barrier = pltpu.get_barrier_semaphore()
    for other in (before, after):
        pl.semaphore_signal(barrier, inc=1, device_id=(other, g), device_id_type=MESH)

    tiles = [slice(LANES * b, LANES * (b + 1)) for b in range(4)]
    ends = (tiles[3], tiles[0])
    loads = [
        pltpu.make_async_copy(state_ref.at[rows, lanes], xs.at[rows, lanes], in_sem.at[k])
        for k, (rows, lanes) in enumerate(
            (rows, lanes) for rows in (slice(2 * LEV, 3 * LEV), slice(0, 2 * LEV), slice(3 * LEV, 4 * LEV)) for lanes in ends)
    ] + [
        pltpu.make_async_copy(state_ref.at[:, pl.ds(LANES, 2 * LANES)], xs.at[:, pl.ds(LANES, 2 * LANES)], in_sem.at[14]),
        pltpu.make_async_copy(surface_ref, su, in_sem.at[15]),
    ]
    small = [
        pltpu.make_async_copy(a, b, in_sem.at[6 + i])
        for i, (a, b) in enumerate((
            (mass_hbm, mass_ref), (active_hbm, active_ref), (maps_hbm, maps_ref), (lev_hbm, lev_ref),
            (more_hbm, more_ref), (tail_hbm, tail_ref), (passive_hbm, passive_ref), (drift_hbm, drift_ref)))
    ]
    for load in loads[:1] + small[:1] + loads[2:3] + loads[1:2] + loads[3:6] + small[1:2] + loads[6:] + small[2:]:
        load.start()

    low = lax.broadcasted_iota(jnp.int32, (1, LANES), 1) < EDGE

    def end_copy(c, i):
        rows = pl.ds(*SENT[c])
        return pltpu.make_async_remote_copy(
            src_ref=send.at[i, rows], dst_ref=recv.at[i, rows],
            send_sem=send_sem.at[2 * c + i], recv_sem=recv_sem.at[2 * c + i],
            device_id=((after, before)[i] if isinstance(i, int) else after, g), device_id_type=MESH)

    sent = [end_copy(c, i) for i in range(2) for c in range(3)]

    def enter():
        pl.semaphore_wait(barrier, 2)

    def exchange():
        enter()
        for copy in sent:
            copy.start()

    first_e, last_e = e == 0, e == n_elem - 1
    pl.when(last_e)(enter)
    small[0].wait()
    for i, lanes in enumerate(ends):
        mass = mass_ref[:, lanes]
        mass = jnp.where(low, swap(mass), mass) if i == 0 else jnp.where(low, mass, swap(mass))
        send[i, 0:8, :] = jnp.broadcast_to(mass, (8, LANES))

        def folded(x):
            top, bottom = x[:40], jnp.concatenate([x[40:], jnp.zeros((8, LANES), F32)], 0)
            return jnp.where(low, swap(top), bottom) if i == 0 else jnp.where(low, top, swap(bottom))

        loads[i].wait()
        send[i, 8:48, :] = folded(xs[2 * LEV:3 * LEV, lanes])
        pl.when(last_e)(sent[3 * i].start)
        loads[2 + i].wait()
        p0 = xs[0:LEV, lanes]
        send[i, 48:88, :] = folded(xs[LEV:2 * LEV, lanes] - 0.3 * p0)
        pl.when(last_e)(sent[3 * i + 1].start)
        loads[4 + i].wait()
        p3 = xs[3 * LEV:, lanes]
        send[i, 88:160, :] = jnp.where(low, swap(p0), p3) if i == 0 else jnp.where(low, p0, swap(p3))
        pl.when(last_e)(sent[3 * i + 2].start)

    small[1].wait()
    act = [active_ref[:, lanes].astype(F32) for lanes in tiles]
    inner = [jnp.where(low, 0.0, act[0]), act[1], act[2], jnp.where(low, act[3], 0.0)]
    marks = jnp.concatenate(inner + [jnp.zeros((4, LANES), F32)], 0)
    r = lax.broadcasted_iota(jnp.int32, (LANES, LANES), 0)
    c = lax.broadcasted_iota(jnp.int32, (LANES, LANES), 1)
    tri = jnp.where(r <= c, 1.0, 0.0).astype(BF16)
    counts = dot(marks.astype(BF16), jnp.concatenate([tri, jnp.ones((LANES, LANES), BF16)], 1))
    where = lax.broadcasted_iota(jnp.int32, (2 * BLOCK, LANES), 0).astype(F32)
    offset = jnp.full((1, LANES), -1.0, F32)
    for b, lanes in enumerate(tiles):
        place = jnp.where(inner[b] > 0.5, counts[b:b + 1, :LANES] + offset, -1.0)
        ones_ref[:, lanes] = jnp.where(where == place, 1.0, 0.0).astype(BF16)
        offset = offset + counts[b:b + 1, LANES:]

    loads[6].wait()
    loads[7].wait()

    def ordered(x):
        pad = jnp.zeros((8, x.shape[1]), F32)
        return jnp.concatenate(
            [x[LEV:2 * LEV] - 0.3 * x[0:LEV], pad, x[2 * LEV:3 * LEV], pad, x[0:LEV], x[3 * LEV:4 * LEV]], 0)

    hi, lo = halves(ordered(xs[...]))
    hi_ref[0:304, :] = hi
    lo_ref[0:304, :] = lo
    hi, lo = halves(su[...])
    hi_ref[304:400, :] = hi
    lo_ref[304:400, :] = lo
    for load in small[2:]:
        load.wait()
    pl.when(jnp.logical_and(e > 1, e < n_elem - 1))(exchange)

    def gather(ref, rows):
        return dot_t(ref[rows, :], ones_ref[...])

    def to_next():
        for c in range(3):
            end_copy(c, 1).wait_recv()
        for copy in sent[:3]:
            copy.start()

    def to_previous():
        enter()
        for copy in sent[3:]:
            copy.start()

    meanwhile = ({24: lambda: pl.when(e == 1)(exchange)}, {8: lambda: pl.when(first_e)(to_next)})
    main = slice(0, STATE_ROWS)
    hi, lo = gather(hi_ref, main).astype(BF16), gather(lo_ref, main).astype(BF16)
    first_maps(maps_ref, prof, hi, lo)
    more_maps(more_ref, prof, jnp.concatenate([hi[:80], hi[160:]], 0), jnp.concatenate([lo[:80], lo[160:]], 0))
    found = gather(hi_ref, slice(304, 400)) + gather(lo_ref, slice(304, 400))
    for i in range(2):
        lanes = tiles[i]
        sur[...] = found[:, lanes]
        tend = cloud(Whole, consts, prepare(Whole, sur), prof, lanes, tail_ref, lev_ref, part, diag, meanwhile[i])
        hi, lo = halves(jnp.concatenate([tend, diag[...]], 0))
        both_hi[:, lanes] = hi
        both_lo[:, lanes] = lo

    pl.when(first_e)(to_previous)

    def passive(x, s2):
        hi, lo = halves(x)
        slow = dot(passive_ref[...], jnp.concatenate([hi, hi, lo], 0))
        mean2 = jnp.sum(s2, axis=0, keepdims=True)
        return jnp.concatenate([slow[:LEV] + drift_ref[...] * mean2, slow[LEV:]], 0)

    for b, lanes in enumerate(tiles):
        x = xs[HALF:, lanes]
        out_ref[HALF:, lanes] = x + jnp.where(act[b] > 0.5, passive(x, su[2 * CX:, lanes]), 0.0)
    back = dot(both_hi[...], ones_ref[...]) + dot(both_lo[...], ones_ref[...])
    out_ref[0:HALF, :] = xs[0:HALF, :] + back[0:HALF]
    diag_out_ref[...] = back[HALF:]

    def edge(form, own_mass, on, wait, other_mass, arrived, emit):
        prep = prepare(form, sur)
        steady = None
        if form is Half:
            steady = steady_ref
            s2, ay, dy, af, df = prep[:5]
            sdy, sdf = s2 * dy, s2 * df
            for z in range(CZ):
                steady[z, 0] = consts["c1"][z] * ay + consts["c2"][z] * sdy
                steady[z, 1] = consts["c1"][z] * af + consts["c2"][z] * sdf
        wait(0)
        wait(1)
        masses = other_mass()
        scale = 1.0 / (own_mass + masses)
        share, rest = own_mass * scale, masses * scale
        pad = jnp.zeros((8, LANES), F32)
        p2, py = [jnp.concatenate([a, b[:32]], 0) for a, b in (arrived(8, 40), arrived(48, 40))]
        start = own_ref[0:160, :] * share + jnp.concatenate([py, pad, p2, pad], 0) * rest
        hi, lo = halves(start)
        first_maps(maps_ref, edge_prof, hi, lo)
        both_p = []

        def late():
            wait(2)
            final = own_ref[160:, :] * share + jnp.concatenate(arrived(88, LEV), 0) * rest
            more_hi, more_lo = halves(final[:80])
            more_maps(more_ref, edge_prof, jnp.concatenate([hi[:80], more_hi], 0),
                      jnp.concatenate([lo[:80], more_lo], 0))
            p0, p2, p3 = final[:LEV], start[80:152], final[LEV:]
            both_p.append(jnp.concatenate([p0, start[:LEV] + 0.3 * p0], 0))
            x = jnp.concatenate([p2, p3], 0)
            emit(slice(HALF, 2 * HALF), x + jnp.where(on, passive(x, sur[2 * CX:, :]), 0.0))

        tend = cloud(form, consts, prep, edge_prof, tiles[0], tail_ref, lev_ref, part, diag, {34: late}, steady)
        emit(slice(0, HALF), both_p[0] + jnp.where(on, tend, 0.0))
        return jnp.where(on, diag[...], 0.0)

    def one_end(k, _):
        i, got = k, 1 - k
        lanes = pl.ds(pl.multiple_of((1 - i) * (3 * LANES), LANES), LANES)
        side = low == (i == 1)

        def double(x):
            return jnp.where(side, x, swap(x))

        def arrived(row, count):
            x = recv[got, row:row + count, :]
            y = swap(x)
            return jnp.where(low, x, y), jnp.where(low, y, x)

        def emit(rows, new):
            out_ref[rows, lanes] = jnp.where(side, new, out_ref[rows, lanes])

        sur[...] = double(su[:, lanes])
        own_ref[...] = ordered(double(xs[:, lanes]))
        seen = edge(
            Half, double(mass_ref[:, lanes]), jnp.where(side, active_ref[:, lanes], 0) == 1,
            lambda c: pl.when(jnp.logical_not(jnp.logical_and(first_e, got == 1)))(end_copy(c, got).wait_recv),
            lambda: recv[got, 0:1, :], arrived, emit)
        diag_out_ref[:, lanes] = jnp.where(side, seen, diag_out_ref[:, lanes])
        return 0

    def both_ends():
        t0, t3 = tiles[0], tiles[3]

        def merge(ref):
            return jnp.where(low, ref[:, t0], ref[:, t3])

        def wait(c):
            for got in range(2):
                end_copy(c, got).wait_recv()

        def arrived(row, count):
            x, y = recv[0, row:row + count, :], recv[1, row:row + count, :]
            return jnp.where(low, x, swap(y)), jnp.where(low, swap(x), y)

        def emit(rows, new):
            out_ref[rows, t0] = jnp.where(low, new, out_ref[rows, t0])
            out_ref[rows, t3] = jnp.where(low, out_ref[rows, t3], new)

        sur[...] = merge(su)
        own_ref[...] = ordered(merge(xs))
        seen = edge(
            Whole, merge(mass_ref), merge(active_ref) == 1, wait,
            lambda: jnp.where(low, recv[0, 0:1, :], recv[1, 0:1, :]), arrived, emit)
        diag_out_ref[:, t0] = jnp.where(low, seen, diag_out_ref[:, t0])
        diag_out_ref[:, t3] = jnp.where(low, diag_out_ref[:, t3], seen)

    alone = e <= 1

    @pl.when(alone)
    def _():
        lax.fori_loop(0, 2, one_end, 0)

    pl.when(jnp.logical_not(alone))(both_ends)

    for copy in sent:
        copy.wait_send()


def write(state_ref, diag_ref, state_out, diag_out, sem):
    copies = [pltpu.make_async_copy(state_ref, state_out, sem.at[0]),
              pltpu.make_async_copy(diag_ref, diag_out, sem.at[1])]
    for copy in copies:
        copy.start()
    for copy in copies:
        copy.wait()


def body(n_elem, state, surface, mass, plan, active):
    cols = state.shape[2]
    maps, more, tail, passive, drift, levels, consts = tables()
    hbm = pl.BlockSpec(memory_space=pltpu.HBM)
    vmem = pl.BlockSpec(memory_space=pltpu.VMEM)
    state, surface, mass, active, maps, more, tail, passive, drift, levels = [
        pltpu.with_memory_space_constraint(x, pltpu.HBM) for x in (
            state.reshape(4 * LEV, cols), surface.reshape(3 * CX, cols), mass.reshape(1, cols),
            active.reshape(1, cols), *map(jnp.asarray, (maps, more, tail, passive, drift, levels)))]
    new_state, diag = pl.pallas_call(
        functools.partial(kernel, consts, n_elem),
        out_shape=(pltpu.VMEM((4 * LEV, cols), F32), pltpu.VMEM((3 * CX, cols), F32)),
        in_specs=[hbm] * 10,
        out_specs=(vmem, vmem),
        scratch_shapes=[
            pltpu.VMEM((4 * LEV, cols), F32),
            pltpu.VMEM((400, cols), BF16),
            pltpu.VMEM((400, cols), BF16),
            pltpu.VMEM((3 * CX, cols), F32),
            pltpu.VMEM((2 * BLOCK, cols), BF16),
            pltpu.VMEM((2, 160, LANES), F32),
            pltpu.VMEM((2, 160, LANES), F32),
            pltpu.VMEM((3 * CX, BLOCK), F32),
            pltpu.VMEM((368, 2 * BLOCK), F32),
            pltpu.VMEM((368, BLOCK), F32),
            pltpu.VMEM((ZP * 8, BLOCK), F32),
            pltpu.VMEM((3 * CX, BLOCK), F32),
            pltpu.VMEM((HALF + 3 * CX, 2 * BLOCK), BF16),
            pltpu.VMEM((HALF + 3 * CX, 2 * BLOCK), BF16),
            pltpu.VMEM((4 * LEV + 16, LANES), F32),
            pltpu.VMEM((CZ, 2, 2, 8, LANES), F32),
            pltpu.VMEM((1, cols), F32),
            pltpu.VMEM((1, cols), jnp.int32),
            pltpu.VMEM(maps.shape, BF16),
            pltpu.VMEM(more.shape, BF16),
            pltpu.VMEM(tail.shape, BF16),
            pltpu.VMEM(passive.shape, BF16),
            pltpu.VMEM(drift.shape, F32),
            pltpu.VMEM(levels.shape, F32),
            pltpu.SemaphoreType.DMA((16,)),
            pltpu.SemaphoreType.DMA((6,)),
            pltpu.SemaphoreType.DMA((6,)),
        ],
        compiler_params=pltpu.CompilerParams(
            collective_id=0, has_side_effects=True, vmem_limit_bytes=32 * 1024 * 1024),
    )(
        state, surface, mass, active, maps, more, tail, passive, drift, levels,
    )
    new_state, diag = pl.pallas_call(
        write,
        out_shape=(jax.ShapeDtypeStruct(new_state.shape, F32), jax.ShapeDtypeStruct(diag.shape, F32)),
        in_specs=[vmem, vmem],
        out_specs=(hbm, hbm),
        scratch_shapes=[pltpu.SemaphoreType.DMA((2,))],
    )(pltpu.with_memory_space_constraint(new_state, pltpu.VMEM), pltpu.with_memory_space_constraint(diag, pltpu.VMEM))
    return new_state.reshape(4, LEV, cols), diag.reshape(3, CX, cols)


def solution(mesh):
    both = ("elem", "grp")
    return jax.shard_map(
        functools.partial(body, mesh.shape["elem"]),
        mesh=mesh,
        in_specs=(P(None, None, both), P(None, None, both), P(both), P(None, both), P(both)),
        out_specs=(P(None, None, both), P(None, None, both)),
        check_vma=False,
    )
```

```python
import functools
import math

import jax
import jax.numpy as jnp
import ml_dtypes
import numpy as np
from jax import lax
from jax.experimental import pallas as pl
from jax.experimental.pallas import tpu as pltpu
from jax.sharding import PartitionSpec as P

LEV = 72
CZ = 58
CX = 32
EDGE = 64
LANES = 128
BLOCK = 128
ZP = 64
HALF = 2 * LEV
STATE_ROWS = 240
F32 = jnp.float32
BF16 = jnp.bfloat16
MESH = pl.DeviceIdType.MESH


def split_np(matrix):
    high = matrix.astype(np.float32).astype(ml_dtypes.bfloat16)
    low = (matrix - high.astype(np.float64)).astype(np.float32).astype(ml_dtypes.bfloat16)
    return high, low


def tables():
    z = np.arange(CZ, dtype=np.float64)
    lev = np.arange(LEV, dtype=np.float64)
    up = np.maximum(0.0, 1.0 - np.abs(z[:, None] * ((LEV - 1) / (CZ - 1)) - lev[None, :]))
    down = np.maximum(0.0, 1.0 - np.abs(lev[:, None] * ((CZ - 1) / (LEV - 1)) - z[None, :]))
    fall = 1.0 - 0.5 * z / (CZ - 1)
    k = 0.1 + 0.2 * z / (CZ - 1)
    mix = np.zeros((CZ, CZ))
    for i in range(CZ):
        mix[i, i] += 1.0 - 2.0 * k[i]
        mix[i, min(i + 1, CZ - 1)] += k[i]
        mix[i, max(i - 1, 0)] += k[i]
    kap = mix.sum(0)
    c1 = mix @ fall
    c2 = -0.1 * (mix @ (fall * fall))
    kb = mix @ up
    qb = -0.1 * (mix @ (fall[:, None] * up))

    m = np.zeros((208, 80))
    m[0:CZ, :LEV] = kb / 0.62
    m[64:64 + CZ, :LEV] = -0.25 * kb
    m[128:128 + CZ, :LEV] = qb
    m[192, :LEV] = (kap * c1) @ (-0.25 * kb)
    m[193, :LEV] = (kap * c2) @ (-0.25 * kb)
    m[194, :LEV] = (kap * c1) @ qb
    m[195, :LEV] = (kap * c2) @ qb
    m[196, :LEV] = kap @ qb
    hi, lo = split_np(m)
    maps = np.concatenate([hi, lo, hi], 1)
    dkk = down @ mix @ kb
    py, p0 = slice(0, 72), slice(80, 152)
    m = np.zeros((160, 160))
    m[0:72, p0] = dkk - down @ up
    m[0:72, py] = 0.8 * dkk / 1.24
    m[72:144, p0] = 0.3 * (dkk - down @ up)
    m[72:144, py] = 0.24 * dkk / 1.24 - down @ up
    m[144, p0] = 1.24 * (kap @ kb)
    m[144, py] = 0.8 * (kap @ kb)
    m[145, p0] = up.sum(0)
    hi, lo = split_np(m)
    more = np.concatenate([hi, lo, hi], 1)

    t = np.zeros((2 * HALF, ZP))
    t[0:72, 0:CZ] = down @ mix / 1.24
    t[72:144, 0:CZ] = 0.3 * (down @ mix) / 1.24
    t[144:216, 0:CZ] = -0.8 * down / 1.24
    t[216:288, 0:CZ] = down / 1.24
    hi, lo = split_np(t)
    tail = np.concatenate([hi, lo, hi], 1)

    e = np.zeros((HALF, HALF))
    e[0:72, 0:72] = down @ (mix @ kb - up)
    e[72:144, 72:144] = e[0:72, 0:72]
    hi, lo = split_np(e)
    passive = np.concatenate([hi, lo, hi], 1)
    drift = np.repeat(((down @ (mix @ (mix @ fall))) / CX)[:, None], LANES, 1).astype(np.float32)

    rows = np.zeros((3, ZP))
    rows[0, :CZ] = c1
    rows[1, :CZ] = c2
    rows[2, :CZ] = kap
    levels = np.repeat(rows.reshape(-1)[:, None], LANES, 1).astype(np.float32)
    consts = dict(
        c1=[float(a) for a in c1], c2=[float(a) for a in c2],
        stay=[float(a) for a in 0.248 * (1.0 - 2.0 * k)], move=[float(a) for a in 0.248 * k],
        s11=float((kap * c1 * c1).sum()), s12=float((kap * c1 * c2).sum()), s22=float((kap * c2 * c2).sum()),
        sc1=float((kap * c1).sum()), sc2=float((kap * c2).sum()))
    return maps, more, tail, passive, drift, levels, consts


def halves(x):
    high = x.astype(BF16)
    return high, (x - high.astype(F32)).astype(BF16)


def dot(a, b):
    return lax.dot_general(a, b, (((1,), (0,)), ((), ())), preferred_element_type=F32)


def dot_t(a, b):
    return lax.dot_general(a, b, (((1,), (1,)), ((), ())), preferred_element_type=F32)


class Whole:
    @staticmethod
    def rows(ref, j):
        return jnp.stack([ref[pl.ds(CX * j + v, 8, stride=4), :] for v in range(4)], 0)

    @staticmethod
    def east(f):
        return jnp.concatenate([f[1:], pltpu.roll(f[0], 7, 0)[None]], 0)

    @staticmethod
    def west(f):
        return jnp.concatenate([pltpu.roll(f[3], 1, 0)[None], f[:3]], 0)

    @staticmethod
    def fold(f):
        return (f[0] + f[1]) + (f[2] + f[3])

    @staticmethod
    def join(f):
        return f

    @staticmethod
    def store(ref, i, f):
        for v in range(4):
            ref[pl.ds(CX * i + v, 8, stride=4), :] = f[v]


class Half:
    @staticmethod
    def rows(ref, j):
        low = lax.broadcasted_iota(jnp.int32, (1, LANES), 1) < EDGE
        return jnp.stack([
            jnp.where(low, ref[pl.ds(CX * j + v, 8, stride=2), :], ref[pl.ds(CX * j + 16 + v, 8, stride=2), :])
            for v in range(2)], 0)

    @staticmethod
    def east(f):
        near = pltpu.roll(f[0], 7, 0)
        edge = lax.broadcasted_iota(jnp.int32, (8, LANES), 0) == 7
        return jnp.stack([f[1], jnp.where(edge, swap(near), near)], 0)

    @staticmethod
    def west(f):
        near = pltpu.roll(f[1], 1, 0)
        edge = lax.broadcasted_iota(jnp.int32, (8, LANES), 0) == 0
        return jnp.stack([jnp.where(edge, swap(near), near), f[0]], 0)

    @staticmethod
    def fold(f):
        return f[0] + f[1]

    @staticmethod
    def join(f):
        return f + swap(f)

    @staticmethod
    def store(ref, i, f):
        low = lax.broadcasted_iota(jnp.int32, (1, LANES), 1) < EDGE
        for v in range(2):
            other = swap(f[v])
            ref[pl.ds(CX * i + v, 8, stride=2), :] = jnp.where(low, f[v], other)
            ref[pl.ds(CX * i + 16 + v, 8, stride=2), :] = jnp.where(low, other, f[v])


def swap(x):
    return pltpu.roll(x, EDGE, 1)


def prepare(form, sur_ref):
    east, west = form.east, form.west
    r0, r1, s2 = form.rows(sur_ref, 0), form.rows(sur_ref, 1), form.rows(sur_ref, 2)
    sy, sw = (r1 - 0.3 * r0) * (1.0 / 0.62), r0 + 0.8 * r1

    def xsum(f):
        return form.join(jnp.sum(form.fold(f), axis=0, keepdims=True))

    def parts(s):
        e, w = east(s), west(s)
        return 0.6 * s + 0.2 * (e + w), e - w

    ay, dy = parts(sy)
    a2, d2 = parts(s2)
    af, df = -0.25 * a2, -0.25 * d2
    aw, dw = parts(sw)
    ew, ef = s2 * dw, s2 * df
    haw, hdw, hew = east(aw) - west(aw), east(dw) - west(dw), east(ew) - west(ew)
    gram = (xsum(af * haw), xsum(af * hdw + df * haw), xsum(af * hew + ef * haw),
            xsum(df * hdw), xsum(df * hew + ef * hdw), xsum(ef * hew))
    means = (xsum(sw) * (1.0 / CX), xsum(ew) * (1.0 / CX))
    return s2, ay, dy, af, df, aw, dw, ef, haw, hdw, hew, gram, means


def cloud(form, consts, prep, prof_ref, lanes, tail_ref, lev_ref, part_ref, diag_ref, at={}, steady=None):
    s2, ay, dy, af, df, aw, dw, ef, haw, hdw, hew, gram, means = prep
    east, west = form.east, form.west

    def level(start, z):
        return prof_ref[start + z:start + z + 1, lanes][None]

    def horizontal(z):
        if steady is None:
            turn = level(128, z) + consts["c2"][z] * s2
            y = (level(0, z) + consts["c1"][z] * ay) + turn * dy
            pull = (level(64, z) + consts["c1"][z] * af) + turn * df
        else:
            turn = level(128, z)
            y = (level(0, z) + steady[z, 0]) + turn * dy
            pull = (level(64, z) + steady[z, 1]) + turn * df
        one = jnp.log(1.0 + jnp.exp2(y * (0.62 * math.log2(math.e))))
        y = y - one
        e, w = east(y), west(y)
        return (1.5 * y + w) + pull * (e - w), one

    def vertical(z, h, above, below):
        v = consts["stay"][z] * h + consts["move"][z] * (above + below)
        two = jnp.maximum(jnp.log(1.0 + jnp.exp(jnp.minimum(v, 80.0))), v)
        part_ref[8 * z:8 * z + 8, :] = form.fold(v) - 0.62 * form.fold(two)
        return v, two

    h, rain = horizontal(0)
    below = h
    total_v = total_2 = None
    def passive_sums():
        pf = prof_ref[64:128, lanes] - 0.5
        q = prof_ref[128:192, lanes]
        s1p, s2p, s1q, sq2, sq = [prof_ref[192 + i:193 + i, lanes] for i in range(5)]
        c1 = lev_ref[0:ZP, :]
        c2 = lev_ref[ZP:2 * ZP, :]
        kap = lev_ref[2 * ZP:3 * ZP, :]
        g11, g12, g13, g22, g23, g33 = gram
        bend = c1 * (c1 * g11 + q * g12 + c2 * g13) + q * (q * g22 + c2 * g23) + (c2 * c2) * g33
        mean_w = c1 * means[0] + c2 * means[1] + (0.4 / CX) * bend
        hi, lo = halves(mean_w)
        prof_ref[208:352, lanes] += dot(tail_ref[0:HALF, :], jnp.concatenate([hi, hi, lo], 0))
        qk = q * kap
        sqp = jnp.sum(qk * pf, axis=0, keepdims=True)
        sqq = jnp.sum(qk * q, axis=0, keepdims=True)
        s11, s12, s22 = consts["s11"], consts["s12"], consts["s22"]
        w1 = (prof_ref[352:353, lanes] + consts["sc1"] * aw) + (sq * dw + consts["sc2"] * (s2 * dw))
        return (
            (0.6 * w1 + 0.2 * (east(w1) + west(w1)))
            + 0.4 * (
                haw * ((s1p + s11 * af) + (s1q * df + s12 * ef))
                + hdw * ((sqp + s1q * af) + (sqq * df + sq2 * ef))
                + hew * ((s2p + s12 * af) + (sq2 * df + s22 * ef))
            )
        )

    for z in range(CZ):
        if z in at:
            at[z]()
        if z == 36:
            sum_w = passive_sums()
            form.store(diag_ref, 1, 0.3 * sum_w)
            form.store(diag_ref, 2, sum_w - 1.24 * prof_ref[353:354, lanes])
        if z + 1 < CZ:
            above, one = horizontal(z + 1)
            rain = rain + one
        else:
            above = h
        v, two = vertical(z, h, above, below)
        total_v = v if z == 0 else total_v + v
        total_2 = two if z == 0 else total_2 + two
        h, below = above, h
    mean_y = part_ref[pl.ds(0, CZ, stride=8), :]
    for s in range(1, 8):
        mean_y = mean_y + part_ref[pl.ds(s, CZ, stride=8), :]
    mean_y = form.join(mean_y) * (1.0 / CX)
    hi, lo = halves(jnp.concatenate([mean_y, jnp.zeros((ZP - CZ, LANES), F32)], 0))
    tend = prof_ref[208:352, lanes] + dot(tail_ref[HALF:, :], jnp.concatenate([hi, hi, lo], 0))
    sum_y = total_v - 0.62 * total_2
    form.store(diag_ref, 0, 0.5 * (rain + total_2))
    form.store(part_ref, 0, sum_y)
    scale = 1.0 / (1.24 * CZ)
    sums = part_ref[0:CX, :]
    diag_ref[CX:2 * CX, :] = (diag_ref[CX:2 * CX, :] + sums) * scale
    diag_ref[2 * CX:, :] = (diag_ref[2 * CX:, :] - 0.8 * sums) * scale
    return tend


def maps_1(maps_ref, ref, hi, lo):
    ref[0:64, :] = dot(maps_ref[0:64, :], jnp.concatenate([hi, hi, lo], 0))


def maps_2(maps_ref, ref, hi, lo):
    x = dot(maps_ref[64:208, :], jnp.concatenate([hi, hi, lo], 0))
    ref[64:128, :] = x[:64] + 0.5
    ref[128:208, :] = x[64:]


def more_maps(more_ref, ref, hi, lo):
    ref[208:368, :] = dot(more_ref[...], jnp.concatenate([hi, hi, lo], 0))


SENT = ((0, 48), (48, 40), (88, 72))


def kernel(consts, n_elem, state_ref, surface_ref, mass_hbm, active_hbm, maps_hbm, more_hbm, tail_hbm, passive_hbm,
           drift_hbm, lev_hbm, out_ref, diag_out_ref,
           xs, hi_ref, lo_ref, su, ones_ref, send, recv, sur, prof, edge_prof, part, diag, both_hi, both_lo, own_ref, steady_ref,
           mass_ref, active_ref, maps_ref, more_ref, tail_ref, passive_ref, drift_ref, lev_ref,
           in_sem, send_sem, recv_sem):
    e, g = lax.axis_index("elem"), lax.axis_index("grp")
    after = lax.rem(e + 1, n_elem)
    before = lax.rem(e + n_elem - 1, n_elem)
    barrier = pltpu.get_barrier_semaphore()
    for other in (before, after):
        pl.semaphore_signal(barrier, inc=1, device_id=(other, g), device_id_type=MESH)

    tiles = [slice(LANES * b, LANES * (b + 1)) for b in range(4)]
    ends = (tiles[3], tiles[0])
    loads = [
        pltpu.make_async_copy(state_ref.at[rows, lanes], xs.at[rows, lanes], in_sem.at[k])
        for k, (rows, lanes) in enumerate(
            (rows, lanes) for rows in (slice(2 * LEV, 3 * LEV), slice(0, 2 * LEV), slice(3 * LEV, 4 * LEV)) for lanes in ends)
    ] + [
        pltpu.make_async_copy(state_ref.at[:, pl.ds(LANES, 2 * LANES)], xs.at[:, pl.ds(LANES, 2 * LANES)], in_sem.at[14]),
        pltpu.make_async_copy(surface_ref, su, in_sem.at[15]),
    ]
    small = [
        pltpu.make_async_copy(a, b, in_sem.at[6 + i])
        for i, (a, b) in enumerate((
            (mass_hbm, mass_ref), (active_hbm, active_ref), (maps_hbm, maps_ref), (lev_hbm, lev_ref),
            (more_hbm, more_ref), (tail_hbm, tail_ref), (passive_hbm, passive_ref), (drift_hbm, drift_ref)))
    ]
    for load in loads[:1] + small[:1] + loads[2:3] + loads[1:2] + loads[3:6] + small[1:2] + loads[6:] + small[2:]:
        load.start()

    low = lax.broadcasted_iota(jnp.int32, (1, LANES), 1) < EDGE

    def end_copy(c, i):
        rows = pl.ds(*SENT[c])
        return pltpu.make_async_remote_copy(
            src_ref=send.at[i, rows], dst_ref=recv.at[i, rows],
            send_sem=send_sem.at[2 * c + i], recv_sem=recv_sem.at[2 * c + i],
            device_id=((after, before)[i] if isinstance(i, int) else after, g), device_id_type=MESH)

    sent = [end_copy(c, i) for i in range(2) for c in range(3)]

    def enter():
        pl.semaphore_wait(barrier, 2)

    def exchange():
        enter()
        for copy in sent:
            copy.start()

    first_e, last_e = e == 0, e == n_elem - 1
    pl.when(last_e)(enter)
    small[0].wait()
    for i, lanes in enumerate(ends):
        mass = mass_ref[:, lanes]
        mass = jnp.where(low, swap(mass), mass) if i == 0 else jnp.where(low, mass, swap(mass))
        send[i, 0:8, :] = jnp.broadcast_to(mass, (8, LANES))

        def folded(x):
            top, bottom = x[:40], jnp.concatenate([x[40:], jnp.zeros((8, LANES), F32)], 0)
            return jnp.where(low, swap(top), bottom) if i == 0 else jnp.where(low, top, swap(bottom))

        loads[i].wait()
        send[i, 8:48, :] = folded(xs[2 * LEV:3 * LEV, lanes])
        pl.when(last_e)(sent[3 * i].start)
        loads[2 + i].wait()
        p0 = xs[0:LEV, lanes]
        send[i, 48:88, :] = folded(xs[LEV:2 * LEV, lanes] - 0.3 * p0)
        pl.when(last_e)(sent[3 * i + 1].start)
        loads[4 + i].wait()
        p3 = xs[3 * LEV:, lanes]
        send[i, 88:160, :] = jnp.where(low, swap(p0), p3) if i == 0 else jnp.where(low, p0, swap(p3))
        pl.when(last_e)(sent[3 * i + 2].start)

    small[1].wait()
    act = [active_ref[:, lanes].astype(F32) for lanes in tiles]
    inner = [jnp.where(low, 0.0, act[0]), act[1], act[2], jnp.where(low, act[3], 0.0)]
    marks = jnp.concatenate(inner + [jnp.zeros((4, LANES), F32)], 0)
    r = lax.broadcasted_iota(jnp.int32, (LANES, LANES), 0)
    c = lax.broadcasted_iota(jnp.int32, (LANES, LANES), 1)
    tri = jnp.where(r <= c, 1.0, 0.0).astype(BF16)
    counts = dot(marks.astype(BF16), jnp.concatenate([tri, jnp.ones((LANES, LANES), BF16)], 1))
    where = lax.broadcasted_iota(jnp.int32, (2 * BLOCK, LANES), 0).astype(F32)
    offset = jnp.full((1, LANES), -1.0, F32)
    for b, lanes in enumerate(tiles):
        place = jnp.where(inner[b] > 0.5, counts[b:b + 1, :LANES] + offset, -1.0)
        ones_ref[:, lanes] = jnp.where(where == place, 1.0, 0.0).astype(BF16)
        offset = offset + counts[b:b + 1, LANES:]

    loads[6].wait()
    loads[7].wait()

    def ordered(x):
        pad = jnp.zeros((8, x.shape[1]), F32)
        return jnp.concatenate(
            [x[LEV:2 * LEV] - 0.3 * x[0:LEV], pad, x[2 * LEV:3 * LEV], pad, x[0:LEV], x[3 * LEV:4 * LEV]], 0)

    hi, lo = halves(ordered(xs[...]))
    hi_ref[0:304, :] = hi
    lo_ref[0:304, :] = lo
    hi, lo = halves(su[...])
    hi_ref[304:400, :] = hi
    lo_ref[304:400, :] = lo
    for load in small[2:]:
        load.wait()
    pl.when(jnp.logical_and(e > 1, e < n_elem - 1))(exchange)

    def gather(ref, rows):
        return dot_t(ref[rows, :], ones_ref[...])

    def to_next():
        for c in range(3):
            end_copy(c, 1).wait_recv()
        for copy in sent[:3]:
            copy.start()

    def to_previous():
        enter()
        for copy in sent[3:]:
            copy.start()

    meanwhile = ({24: lambda: pl.when(e == 1)(exchange)}, {8: lambda: pl.when(first_e)(to_next)})
    main = slice(0, STATE_ROWS)
    hi, lo = gather(hi_ref, main).astype(BF16), gather(lo_ref, main).astype(BF16)
    maps_1(maps_ref, prof, hi[:80], lo[:80])
    maps_2(maps_ref, prof, hi[80:160], lo[80:160])
    more_maps(more_ref, prof, jnp.concatenate([hi[:80], hi[160:]], 0), jnp.concatenate([lo[:80], lo[160:]], 0))
    found = gather(hi_ref, slice(304, 400)) + gather(lo_ref, slice(304, 400))
    for i in range(2):
        lanes = tiles[i]
        sur[...] = found[:, lanes]
        tend = cloud(Whole, consts, prepare(Whole, sur), prof, lanes, tail_ref, lev_ref, part, diag, meanwhile[i])
        hi, lo = halves(jnp.concatenate([tend, diag[...]], 0))
        both_hi[:, lanes] = hi
        both_lo[:, lanes] = lo

    pl.when(first_e)(to_previous)

    def passive(x, s2):
        hi, lo = halves(x)
        slow = dot(passive_ref[...], jnp.concatenate([hi, hi, lo], 0))
        mean2 = jnp.sum(s2, axis=0, keepdims=True)
        return jnp.concatenate([slow[:LEV] + drift_ref[...] * mean2, slow[LEV:]], 0)

    for b, lanes in enumerate(tiles):
        x = xs[HALF:, lanes]
        out_ref[HALF:, lanes] = x + jnp.where(act[b] > 0.5, passive(x, su[2 * CX:, lanes]), 0.0)
    back = dot(both_hi[...], ones_ref[...]) + dot(both_lo[...], ones_ref[...])
    out_ref[0:HALF, :] = xs[0:HALF, :] + back[0:HALF]
    diag_out_ref[...] = back[HALF:]

    def edge(form, own_mass, on, wait, other_mass, arrived, emit):
        prep = prepare(form, sur)
        steady = None
        if form is Half:
            steady = steady_ref
            s2, ay, dy, af, df = prep[:5]
            sdy, sdf = s2 * dy, s2 * df
            for z in range(CZ):
                steady[z, 0] = consts["c1"][z] * ay + consts["c2"][z] * sdy
                steady[z, 1] = consts["c1"][z] * af + consts["c2"][z] * sdf
        wait(0)
        masses = other_mass()
        scale = 1.0 / (own_mass + masses)
        share, rest = own_mass * scale, masses * scale
        pad = jnp.zeros((8, LANES), F32)

        def shared(row, at):
            top, bottom = arrived(row, 40)
            x = jnp.concatenate([top, bottom[:32], pad], 0)
            return own_ref[at:at + 80, :] * share + x * rest

        second = shared(8, 80)
        maps_2(maps_ref, edge_prof, *halves(second))
        wait(1)
        first = shared(48, 0)
        hi, lo = halves(first)
        maps_1(maps_ref, edge_prof, hi, lo)
        both_p = []

        def late():
            wait(2)
            final = own_ref[160:, :] * share + jnp.concatenate(arrived(88, LEV), 0) * rest
            more_hi, more_lo = halves(final[:80])
            more_maps(more_ref, edge_prof, jnp.concatenate([hi, more_hi], 0),
                      jnp.concatenate([lo, more_lo], 0))
            p0, p2, p3 = final[:LEV], second[:LEV], final[LEV:]
            both_p.append(jnp.concatenate([p0, first[:LEV] + 0.3 * p0], 0))
            x = jnp.concatenate([p2, p3], 0)
            emit(slice(HALF, 2 * HALF), x + jnp.where(on, passive(x, sur[2 * CX:, :]), 0.0))

        tend = cloud(form, consts, prep, edge_prof, tiles[0], tail_ref, lev_ref, part, diag, {34: late}, steady)
        emit(slice(0, HALF), both_p[0] + jnp.where(on, tend, 0.0))
        return jnp.where(on, diag[...], 0.0)

    def one_end(k, _):
        i, got = k, 1 - k
        lanes = pl.ds(pl.multiple_of((1 - i) * (3 * LANES), LANES), LANES)
        side = low == (i == 1)

        def double(x):
            return jnp.where(side, x, swap(x))

        def arrived(row, count):
            x = recv[got, row:row + count, :]
            y = swap(x)
            return jnp.where(low, x, y), jnp.where(low, y, x)

        def emit(rows, new):
            out_ref[rows, lanes] = jnp.where(side, new, out_ref[rows, lanes])

        sur[...] = double(su[:, lanes])
        own_ref[...] = ordered(double(xs[:, lanes]))
        seen = edge(
            Half, double(mass_ref[:, lanes]), jnp.where(side, active_ref[:, lanes], 0) == 1,
            lambda c: pl.when(jnp.logical_not(jnp.logical_and(first_e, got == 1)))(end_copy(c, got).wait_recv),
            lambda: recv[got, 0:1, :], arrived, emit)
        diag_out_ref[:, lanes] = jnp.where(side, seen, diag_out_ref[:, lanes])
        return 0

    def both_ends():
        t0, t3 = tiles[0], tiles[3]

        def merge(ref):
            return jnp.where(low, ref[:, t0], ref[:, t3])

        def wait(c):
            for got in range(2):
                end_copy(c, got).wait_recv()

        def arrived(row, count):
            x, y = recv[0, row:row + count, :], recv[1, row:row + count, :]
            return jnp.where(low, x, swap(y)), jnp.where(low, swap(x), y)

        def emit(rows, new):
            out_ref[rows, t0] = jnp.where(low, new, out_ref[rows, t0])
            out_ref[rows, t3] = jnp.where(low, out_ref[rows, t3], new)

        sur[...] = merge(su)
        own_ref[...] = ordered(merge(xs))
        seen = edge(
            Whole, merge(mass_ref), merge(active_ref) == 1, wait,
            lambda: jnp.where(low, recv[0, 0:1, :], recv[1, 0:1, :]), arrived, emit)
        diag_out_ref[:, t0] = jnp.where(low, seen, diag_out_ref[:, t0])
        diag_out_ref[:, t3] = jnp.where(low, diag_out_ref[:, t3], seen)

    alone = e <= 1

    @pl.when(alone)
    def _():
        lax.fori_loop(0, 2, one_end, 0)

    pl.when(jnp.logical_not(alone))(both_ends)

    for copy in sent:
        copy.wait_send()


def write(state_ref, diag_ref, state_out, diag_out, sem):
    copies = [pltpu.make_async_copy(state_ref, state_out, sem.at[0]),
              pltpu.make_async_copy(diag_ref, diag_out, sem.at[1])]
    for copy in copies:
        copy.start()
    for copy in copies:
        copy.wait()


def body(n_elem, state, surface, mass, plan, active):
    cols = state.shape[2]
    maps, more, tail, passive, drift, levels, consts = tables()
    hbm = pl.BlockSpec(memory_space=pltpu.HBM)
    vmem = pl.BlockSpec(memory_space=pltpu.VMEM)
    state, surface, mass, active, maps, more, tail, passive, drift, levels = [
        pltpu.with_memory_space_constraint(x, pltpu.HBM) for x in (
            state.reshape(4 * LEV, cols), surface.reshape(3 * CX, cols), mass.reshape(1, cols),
            active.reshape(1, cols), *map(jnp.asarray, (maps, more, tail, passive, drift, levels)))]
    new_state, diag = pl.pallas_call(
        functools.partial(kernel, consts, n_elem),
        out_shape=(pltpu.VMEM((4 * LEV, cols), F32), pltpu.VMEM((3 * CX, cols), F32)),
        in_specs=[hbm] * 10,
        out_specs=(vmem, vmem),
        scratch_shapes=[
            pltpu.VMEM((4 * LEV, cols), F32),
            pltpu.VMEM((400, cols), BF16),
            pltpu.VMEM((400, cols), BF16),
            pltpu.VMEM((3 * CX, cols), F32),
            pltpu.VMEM((2 * BLOCK, cols), BF16),
            pltpu.VMEM((2, 160, LANES), F32),
            pltpu.VMEM((2, 160, LANES), F32),
            pltpu.VMEM((3 * CX, BLOCK), F32),
            pltpu.VMEM((368, 2 * BLOCK), F32),
            pltpu.VMEM((368, BLOCK), F32),
            pltpu.VMEM((ZP * 8, BLOCK), F32),
            pltpu.VMEM((3 * CX, BLOCK), F32),
            pltpu.VMEM((HALF + 3 * CX, 2 * BLOCK), BF16),
            pltpu.VMEM((HALF + 3 * CX, 2 * BLOCK), BF16),
            pltpu.VMEM((4 * LEV + 16, LANES), F32),
            pltpu.VMEM((CZ, 2, 2, 8, LANES), F32),
            pltpu.VMEM((1, cols), F32),
            pltpu.VMEM((1, cols), jnp.int32),
            pltpu.VMEM(maps.shape, BF16),
            pltpu.VMEM(more.shape, BF16),
            pltpu.VMEM(tail.shape, BF16),
            pltpu.VMEM(passive.shape, BF16),
            pltpu.VMEM(drift.shape, F32),
            pltpu.VMEM(levels.shape, F32),
            pltpu.SemaphoreType.DMA((16,)),
            pltpu.SemaphoreType.DMA((6,)),
            pltpu.SemaphoreType.DMA((6,)),
        ],
        compiler_params=pltpu.CompilerParams(
            collective_id=0, has_side_effects=True, vmem_limit_bytes=32 * 1024 * 1024),
    )(
        state, surface, mass, active, maps, more, tail, passive, drift, levels,
    )
    new_state, diag = pl.pallas_call(
        write,
        out_shape=(jax.ShapeDtypeStruct(new_state.shape, F32), jax.ShapeDtypeStruct(diag.shape, F32)),
        in_specs=[vmem, vmem],
        out_specs=(hbm, hbm),
        scratch_shapes=[pltpu.SemaphoreType.DMA((2,))],
    )(pltpu.with_memory_space_constraint(new_state, pltpu.VMEM), pltpu.with_memory_space_constraint(diag, pltpu.VMEM))
    return new_state.reshape(4, LEV, cols), diag.reshape(3, CX, cols)


def solution(mesh):
    both = ("elem", "grp")
    return jax.shard_map(
        functools.partial(body, mesh.shape["elem"]),
        mesh=mesh,
        in_specs=(P(None, None, both), P(None, None, both), P(both), P(None, both), P(both)),
        out_specs=(P(None, None, both), P(None, None, both)),
        check_vma=False,
    )
```
